128 devices in a mesh: dp: 2 (over z_hi), seq: 16 (over z_lo, x, core), tp: 4 (over y).
Axes of the slice: x: 4, y: 4, z: 4 (z_hi: 2, z_lo: 2; z = z_hi * 2 + z_lo), core: 2. Of those that a mesh axis runs over, the one named last changes fastest.
Arguments:
- hidden_in: bfloat16 [6, 2048, 2048], P('dp', 'seq'), may hold values from -6 to 6
- segments: int32 [6, 2048], P('dp', 'seq'), may hold values from 0 to 3, as said below
- keep_mask: int32 [6, 2048], P('dp', 'seq'), may hold values 0 or 1
- ln_gain: float32 [2048], replicated, may hold values from 0.5 to 1.5
- ln_shift: float32 [2048], replicated, may hold values from -3 to 3
- w_qkv: float32 [2048, 3, 2048], P(('dp', 'seq'), None, 'tp'), may hold values from -0.125 to 0.125
- b_qkv: float32 [3, 2048], P(None, 'tp'), may hold values from -3 to 3
- w_dense: float32 [2048, 2048], P('tp', ('dp', 'seq')), may hold values from -0.5 to 0.5
- b_dense: float32 [2048], replicated, may hold values from -3 to 3
- w_up: float32 [2048, 8192], P(('dp', 'seq'), 'tp'), may hold values from -0.125 to 0.125
- b_up: float32 [8192], P('tp'), may hold values from -3 to 3
- w_down: float32 [8192, 2048], P('tp', ('dp', 'seq')), may hold values from -0.0625 to 0.0625
- b_down: float32 [2048], replicated, may hold values from -3 to 3
- cotangent: bfloat16 [6, 2048, 2048], P('dp', 'seq'), may hold values from -6 to 6
Outputs:
- block_out: float32 [6, 2048, 2048], P('dp', 'seq')
- input_grad: float32 [6, 2048, 2048], P('dp', 'seq')
- grad_gain: float32 [2048], replicated
- grad_shift: float32 [2048], replicated
- grad_qkv: float32 [2048, 3, 2048], P(('dp', 'seq'), None, 'tp')
- grad_bqkv: float32 [3, 2048], P(None, 'tp')
- grad_dense: float32 [2048, 2048], P('tp', ('dp', 'seq'))
- grad_bdense: float32 [2048], replicated
- grad_up: float32 [2048, 8192], P(('dp', 'seq'), 'tp')
- grad_bup: float32 [8192], P('tp')
- grad_down: float32 [8192, 2048], P('tp', ('dp', 'seq'))
- grad_bdown: float32 [2048], replicated
The draws below stay inside these ranges and needn't reach their ends.
Inputs may be any that keep to these rules, and one draw needn't show every extreme that they name: `segments`: within each sequence the numbers start at 0 and never fall; in each group of 6 / 2 consecutive sequences one sequence, drawn from the seed, is a single document, and every other sequence holds four documents.
All inputs are finite; a program needn't handle non-finite values. No bound on the sum of `keep_mask` on one device may be relied on, other than what follows from the above.
Results may differ from the reference program's by a relative error of at most 0.02.
Values may be sent and summed in bfloat16 or wider, within the bound.
A program may use at most 320 MiB of HBM per device.

```python
import math
import jax
import jax.numpy as jnp
from jax import lax

D = 2048
H = 32
HD = 64
ROT = 32
FF = 8192
WINDOW = 1024
LENGTH = 2048
SEQS = 6
N_DP = 2


def draw_segments(key, part):
    key = jax.random.fold_in(key, 11)
    first_key, second_key = jax.random.split(key)
    row_keys = jax.random.split(first_key, SEQS)
    orders = jax.vmap(lambda row_key: jax.random.permutation(row_key, LENGTH - 1))(row_keys)
    bounds = orders[:, :3] + 1
    places = jnp.arange(LENGTH, dtype=jnp.int32)
    starts = jnp.any(places[None, :, None] == bounds[:, None, :], axis=-1)
    group = SEQS // N_DP
    chosen = jax.random.randint(second_key, (N_DP,), 0, group)
    rows = jnp.arange(SEQS)
    single = rows % group == chosen[rows // group]
    starts = starts & jnp.logical_not(single)[:, None]
    return jnp.cumsum(starts.astype(jnp.int32), axis=1).astype(jnp.int32)


def place_ends(drawn, rng, smallest, top_value):
    place = [jax.random.randint(jax.random.fold_in(rng, axis), (), 0, length) for axis, length in enumerate(drawn.shape)]
    longest = drawn.shape.index(max(drawn.shape))
    beside = place[:longest] + [(place[longest] + 1) % drawn.shape[longest]] + place[longest + 1:]
    return drawn.at[tuple(place)].set(smallest).at[tuple(beside)].set(top_value)


def block_scale(stream_key, dims, shards, least, top_value):
    level = 1.0
    for position, blocks in shards:
        heights = jax.random.uniform(jax.random.fold_in(jax.random.fold_in(stream_key, 6), position), (blocks,), jnp.float32, least / len(shards), top_value / len(shards))
        level = level * jnp.repeat(jnp.exp(heights), dims[position] // blocks).reshape((-1,) + (1,) * (len(dims) - 1 - position))
    return level


def normal_values(own_key, shape, spread, limit, cuts=(), kind=jnp.bfloat16):
    gain = block_scale(own_key, shape, cuts, -0.22, 0.18) if cuts else 1.0
    values = jax.random.normal(own_key, shape, jnp.float32) * spread * gain
    return jnp.minimum(jnp.maximum(values, -limit), limit).astype(kind)


def setup_inputs(seed: int = 0) -> dict:
    key_of = jax.random.split(jax.random.key(seed), 15)
    return {
        "hidden_in": normal_values(key_of[0], (SEQS, LENGTH, D), 1.0, 6.0, ((0, 2), (1, 16))),
        "segments": draw_segments(jax.random.fold_in(key_of[14], 71), 0),
        "keep_mask": place_ends((jax.random.randint(key_of[2], (SEQS, LENGTH), 0, 8) < 7).astype(jnp.int32), jax.random.fold_in(key_of[2], 1), 0, 1),
        "ln_gain": jnp.clip(1.0 + 0.1 * jax.random.normal(key_of[3], (D,), jnp.float32), 0.5, 1.5),
        "ln_shift": normal_values(key_of[4], (D,), 0.5, 3.0, (), jnp.float32),
        "w_qkv": normal_values(key_of[5], (D, 3, D), D ** -0.5, 0.125, ((0, 32), (2, 4)), jnp.float32),
        "b_qkv": normal_values(key_of[6], (3, D), 0.5, 3.0, ((1, 4),), jnp.float32),
        "w_dense": normal_values(key_of[7], (D, D), (D // 16) ** -0.5, 0.5, ((0, 4), (1, 32)), jnp.float32),
        "b_dense": normal_values(key_of[8], (D,), 0.5, 3.0, (), jnp.float32),
        "w_up": normal_values(key_of[9], (D, FF), D ** -0.5, 0.125, ((0, 32), (1, 4)), jnp.float32),
        "b_up": normal_values(key_of[10], (FF,), 0.5, 3.0, ((0, 4),), jnp.float32),
        "w_down": normal_values(key_of[11], (FF, D), FF ** -0.5, 0.0625, ((0, 4), (1, 32)), jnp.float32),
        "b_down": normal_values(key_of[12], (D,), 0.5, 3.0, (), jnp.float32),
        "cotangent": normal_values(key_of[13], (SEQS, LENGTH, D), 1.0, 6.0, ((0, 2), (1, 16))),
    }


@jax.custom_vjp
def low(v):
    return lax.optimization_barrier(v.astype(jnp.bfloat16)).astype(jnp.float32)

@jax.custom_vjp
def low_back(v):
    return v

def low_keep(v):
    return (low(v), None)

def low_pass(kept, grad):
    return (grad,)

def back_keep(v):
    return (v, None)

def back_low(kept, grad):
    return (low(grad),)
low.defvjp(low_keep, low_pass)
low_back.defvjp(back_keep, back_low)

def rotate(tensor, cosine, sine):
    half_rot = cosine.shape[-1]
    first = tensor[..., :half_rot]
    second = tensor[..., half_rot:2 * half_rot]
    return jnp.concatenate([first * cosine - second * sine, second * cosine + first * sine, tensor[..., 2 * half_rot:]], axis=-1)

def sequence_forward(hidden, segment, key_info, params):
    ln_gain, ln_shift, w_qkv, b_qkv, w_dense, b_dense, w_up, b_up, w_down, b_down = params
    highest = lax.Precision.HIGHEST
    length = hidden.shape[0]
    mean = lax.optimization_barrier(jnp.mean(hidden, axis=-1, keepdims=True))
    centered = hidden - mean
    variance = lax.optimization_barrier(jnp.mean(centered * centered, axis=-1, keepdims=True))
    normed = centered * lax.rsqrt(variance + 1e-05) * ln_gain + ln_shift
    inputs = low(normed)
    joined = jnp.einsum('ld,dte->lte', inputs, low(w_qkv), precision=highest) + b_qkv
    joined = low_back(joined)
    split = joined.reshape(length, 3, H, HD).transpose(1, 2, 0, 3)
    half_rot = ROT // 2
    frequency = 10000.0 ** (-(jnp.arange(half_rot, dtype=jnp.float32) * 2.0) / ROT)
    angles = jnp.arange(length, dtype=jnp.float32)[:, None] * frequency[None, :]
    cosine = jnp.cos(angles)
    sine = jnp.sin(angles)
    queries = low(rotate(split[0], cosine, sine))
    keys = low(rotate(split[1], cosine, sine))
    values = low(split[2])
    scale = HD ** (-0.5)
    block = math.gcd(length, 512)
    key_positions = jnp.arange(length, dtype=jnp.int32)

    def attend(start):
        rows = lax.dynamic_slice_in_dim(queries, start, block, 1)
        scores = jnp.einsum('hqe,hke->hqk', rows, keys, precision=highest) * scale
        scores = low_back(scores)
        query_positions = start + jnp.arange(block, dtype=jnp.int32)
        query_segment = lax.dynamic_slice_in_dim(segment, start, block, 0)
        allowed = (query_segment[:, None] == key_info[None, :]) | (query_positions[:, None] == key_positions[None, :])
        allowed = allowed & (key_positions[None, :] <= query_positions[:, None]) & (query_positions[:, None] - key_positions[None, :] < WINDOW)
        scores = jnp.where(allowed[None], scores, -1e+30)
        row_top = lax.optimization_barrier(jnp.max(scores, axis=-1, keepdims=True))
        expo = jnp.exp(scores - row_top)
        probs = expo / lax.optimization_barrier(jnp.sum(expo, axis=-1, keepdims=True))
        return jnp.einsum('hqk,hke->hqe', low(probs), values, precision=highest)
    starts = jnp.arange(0, length, block, dtype=jnp.int32)
    blocks = lax.map(jax.checkpoint(attend), starts)
    attended = blocks.transpose(0, 2, 1, 3).reshape(length, H * HD)
    attended = low(low_back(attended))
    mixed = jnp.dot(attended, low(w_dense), precision=highest, preferred_element_type=jnp.float32) + b_dense
    up_pre = jnp.dot(inputs, low(w_up), precision=highest, preferred_element_type=jnp.float32) + b_up
    up_pre = low_back(up_pre)
    active = low(jax.nn.gelu(up_pre, approximate=True))
    branch = jnp.dot(active, low(w_down), precision=highest, preferred_element_type=jnp.float32) + b_down
    return hidden + mixed + branch

def reference(hidden_in, segments, keep_mask, ln_gain, ln_shift, w_qkv, b_qkv, w_dense, b_dense, w_up, b_up, w_down, b_down, cotangent):
    params = (ln_gain.astype(jnp.float32), ln_shift.astype(jnp.float32), w_qkv.astype(jnp.float32), b_qkv.astype(jnp.float32), w_dense.astype(jnp.float32), b_dense.astype(jnp.float32), w_up.astype(jnp.float32), b_up.astype(jnp.float32), w_down.astype(jnp.float32), b_down.astype(jnp.float32))

    def one_sequence(totals, item):
        hidden, segment, keep, upstream = item
        key_info = jnp.where(keep > 0, segment, -1).astype(jnp.int32)
        hidden = hidden.astype(jnp.float32)

        def forward(inner, weights):
            return sequence_forward(inner, segment, key_info, weights)
        result, pull = jax.vjp(forward, hidden, params)
        grad_hidden, grad_params = pull(upstream.astype(jnp.float32))
        totals = jax.tree.map(lambda first, second: first + second, totals, grad_params)
        return (totals, (result, grad_hidden))
    zeros = jax.tree.map(jnp.zeros_like, params)
    totals, (results, grads) = lax.scan(one_sequence, zeros, (hidden_in, segments, keep_mask, cotangent))
    return (results, grads, totals[0], totals[1], totals[2], totals[3], totals[4], totals[5], totals[6], totals[7], totals[8], totals[9])
```

```python
import functools

import jax
import jax.numpy as jnp
from jax import lax
from jax.experimental import pallas as pl
from jax.experimental.pallas import tpu as pltpu
from jax.sharding import PartitionSpec as P

MESH = pl.DeviceIdType.MESH
HD = 64
ROT = 32
WINDOW = 1024
BF = jnp.bfloat16
F32 = jnp.float32
ANY = pl.BlockSpec(memory_space=pl.ANY)
VMEM = pl.BlockSpec(memory_space=pltpu.VMEM)


def wrap(v):
    return lax.rem(v + 4, 4)


def place():
    dp, sq, tp = lax.axis_index("dp"), lax.axis_index("seq"), lax.axis_index("tp")
    return dp * 2 + sq // 8, lax.rem(sq // 2, 4), lax.rem(sq, 2), tp


def device(z, x, c, y):
    z, x, y = wrap(z), wrap(x), wrap(y)
    return {"dp": z // 2, "seq": lax.rem(z, 2) * 8 + x * 2 + c, "tp": y}


class Net:
    def __init__(self, send, recv):
        self.send, self.recv, self.n, self.out, self.keys = send, recv, 0, [], {}
        self.z, self.x, self.c, self.y = place()
        self.flip = 1 - 2 * lax.rem(self.z, 2)
        self.chip = lax.rem(self.z, 2) * 4 + self.x

    def to(self, axis, way):
        z, x, c, y = self.z, self.x, self.c, self.y
        if axis == "s":
            return device(z, x, 1 - c, y)
        if axis == "x":
            return device(z, x + way, c, y)
        if axis == "z":
            return device(z + way, x, c, y)
        if axis == "y":
            return device(z, x, c, y + way)
        return device(z + axis * self.flip, x + way, c, y)

    def greet(self, targets):
        bar = pltpu.get_barrier_semaphore()
        for axis, way in targets:
            pl.semaphore_signal(bar, inc=1, device_id=self.to(axis, way), device_id_type=MESH)
        pl.semaphore_wait(bar, len(targets))

    def push(self, key, src, dst, axis, way):
        k = self.n
        self.n += 1
        copy = pltpu.make_async_remote_copy(
            src_ref=src,
            dst_ref=dst,
            send_sem=self.send.at[k],
            recv_sem=self.recv.at[k],
            device_id=self.to(axis, way),
            device_id_type=MESH,
        )
        copy.start()
        self.out.append(copy)
        self.keys[key] = copy

    def arrived(self, key):
        self.keys.pop(key).wait_recv()

    def drain(self):
        for copy in self.out:
            copy.wait_send()
        for key in list(self.keys):
            self.arrived(key)


RING_XZ = (("x", 1), ("x", -1), ("z", 1), ("z", -1), ("s", 1))
RING_Y = (("y", 1), ("y", -1))
FAR = (("x", 2), ("z", 2), ("y", 2))
SPREAD = tuple((dz, dx) for dz in (0, 1) for dx in range(4) if dz or dx) + (("s", 1),)


class Gather:
    def __init__(self, net, name, src, dst):
        self.net, self.name, self.src, self.dst = net, name, src, dst
        self.half, self.quarter = src.shape[0] // 2, src.shape[0] // 4

    def at(self, h, a, b, r0, rn):
        n = self.net
        z, x = (n.z + b, n.x + a) if h == 0 else (n.z + a, n.x + b)
        return self.dst.at[wrap(z), wrap(x), n.c, pl.ds(h * self.half + r0, rn)]

    def own(self, h):
        return self.src.at[pl.ds(h * self.half, self.half)]

    def axes(self, h):
        return ("x", "z") if h == 0 else ("z", "x")

    def begin(self, sem):
        n = self.net
        for h in (0, 1):
            for w in (1, -1):
                n.push((self.name, h, "A", w), self.own(h), self.at(h, 0, 0, 0, self.half), self.axes(h)[0], w)
        for h in (0, 1):
            for w in (1, -1):
                n.push((self.name, h, "B", 0, w), self.own(h), self.at(h, 0, 0, 0, self.half), self.axes(h)[1], w)
        whole = self.dst.at[n.z, n.x, n.c]
        n.push((self.name, "s"), self.src, whole, "s", 1)
        self.local = pltpu.make_async_copy(self.src, whole, sem)
        self.local.start()

    def spread(self, h, a):
        n = self.net
        block = self.at(h, a, 0, 0, self.half)
        for w in (1, -1):
            n.push((self.name, h, "B", a, w), block, block, self.axes(h)[1], w)
        n.push((self.name, h, "s", a, 0), block, block, "s", 1)

    def near(self):
        n = self.net
        for h in (0, 1):
            for w in (1, -1):
                n.arrived((self.name, h, "A", w))
                part = self.at(h, -w, 0, 0 if w == 1 else self.quarter, self.quarter)
                n.push((self.name, h, "AF", w), part, part, self.axes(h)[0], w)
                self.spread(h, -w)

    def far(self):
        for h in (0, 1):
            for w in (1, -1):
                self.net.arrived((self.name, h, "AF", w))
            self.spread(h, 2)

    def pass_on(self, a):
        n = self.net
        for h in (0, 1):
            for w in (1, -1):
                n.arrived((self.name, h, "B", a, w))
                part = self.at(h, a, -w, 0 if w == 1 else self.quarter, self.quarter)
                n.push((self.name, h, "BF", a, w), part, part, self.axes(h)[1], w)
                block = self.at(h, a, -w, 0, self.half)
                n.push((self.name, h, "s", a, -w), block, block, "s", 1)

    def close(self, a):
        n = self.net
        for h in (0, 1):
            for w in (1, -1):
                n.arrived((self.name, h, "BF", a, w))
            block = self.at(h, a, 2, 0, self.half)
            n.push((self.name, h, "s", a, 2), block, block, "s", 1)


def gather_kernel(count, *refs):
    srcs, dsts = refs[:count], refs[count : 2 * count]
    send, recv, local = refs[2 * count :]
    net = Net(send, recv)
    net.greet(RING_XZ)
    parts = [Gather(net, i, srcs[i], dsts[i]) for i in range(count)]
    parts[0].begin(local.at[0])
    for i in range(count):
        if i + 1 < count:
            parts[i + 1].begin(local.at[i + 1])
        parts[i].near()
        if i > 0:
            for a in (0, -1, 1):
                parts[i - 1].pass_on(a)
        parts[i].far()
        if i > 0:
            parts[i - 1].pass_on(2)
            for a in (0, -1, 1, 2):
                parts[i - 1].close(a)
    for a in (0, -1, 1, 2):
        parts[-1].pass_on(a)
    for a in (0, -1, 1, 2):
        parts[-1].close(a)
    for part in parts:
        part.local.wait()
    net.drain()


def gather(shards, cid, name):
    count = len(shards)
    outs = pl.pallas_call(
        functools.partial(gather_kernel, count),
        out_shape=[jax.ShapeDtypeStruct((4, 4, 2) + s.shape, s.dtype) for s in shards],
        in_specs=[ANY] * count,
        out_specs=[ANY] * count,
        scratch_shapes=[
            pltpu.SemaphoreType.DMA((80 * count,)),
            pltpu.SemaphoreType.DMA((80 * count,)),
            pltpu.SemaphoreType.DMA((count,)),
        ],
        compiler_params=pltpu.CompilerParams(collective_id=cid, has_side_effects=True),
        name=name,
    )(*shards)
    return [o.reshape(32 * s.shape[0], s.shape[1]) for o, s in zip(outs, shards)]


def lanes(chip):
    return pl.ds(pl.multiple_of(chip * 128, 128), 128)


def exchange_kernel(qd, kv, info, qd_out, kv_out, info_out, send, recv, local):
    net = Net(send, recv)
    net.greet(SPREAD)
    me, c = net.chip, net.c
    mine = 2 * me + c
    for dz in (1, 0):
        for dx in (2, 1, 3, 0):
            if not (dz or dx):
                continue
            other = lax.rem(lax.rem(net.z, 2) + dz, 2) * 4 + wrap(net.x + dx)
            net.push(("k", dz, dx), kv.at[:, :, lanes(other)], kv_out.at[:, mine], dz, dx)
            net.push(("i", dz, dx), info, info_out.at[mine], dz, dx)
            net.push(("q", dz, dx), qd.at[:, :, lanes(other)], qd_out.at[me], dz, dx)
    net.push("ks", kv.at[:, :, lanes(me)], kv_out.at[:, mine], "s", 1)
    net.push("is", info, info_out.at[mine], "s", 1)
    stays = [
        pltpu.make_async_copy(qd.at[:, :, lanes(me)], qd_out.at[me], local.at[0]),
        pltpu.make_async_copy(kv.at[:, :, lanes(me)], kv_out.at[:, mine], local.at[1]),
        pltpu.make_async_copy(info, info_out.at[mine], local.at[2]),
    ]
    for stay in stays:
        stay.start()
    for dz in (1, 0):
        for dx in (2, 1, 3, 0):
            if not (dz or dx):
                continue
            other = lax.rem(lax.rem(net.z, 2) + dz, 2) * 4 + wrap(net.x - dx)
            slot = 2 * other + c
            net.arrived(("k", dz, dx))
            net.push(("ks", dz, dx), kv_out.at[:, slot], kv_out.at[:, slot], "s", 1)
            net.arrived(("i", dz, dx))
            net.push(("is", dz, dx), info_out.at[slot], info_out.at[slot], "s", 1)
    for stay in stays:
        stay.wait()
    net.drain()


def exchange(qd, kv, info, cid):
    return pl.pallas_call(
        exchange_kernel,
        out_shape=[
            jax.ShapeDtypeStruct((8, 3, 128, 128), BF),
            jax.ShapeDtypeStruct((3, 16, 128, 128), BF),
            jax.ShapeDtypeStruct((16, 8, 128), jnp.int32),
        ],
        in_specs=[ANY] * 3,
        out_specs=[ANY] * 3,
        scratch_shapes=[
            pltpu.SemaphoreType.DMA((48,)),
            pltpu.SemaphoreType.DMA((48,)),
            pltpu.SemaphoreType.DMA((3,)),
        ],
        compiler_params=pltpu.CompilerParams(collective_id=cid, has_side_effects=True),
        name="heads_out",
    )(qd, kv, info)


def attend_kernel(qd, kv, info, od, dkv, seen, total):
    c = lax.rem(lax.axis_index("seq"), 2)
    lane = lax.broadcasted_iota(jnp.int32, (128, 128), 1)
    row = lax.broadcasted_iota(jnp.int32, (128, 128), 0)
    left = lane < 64
    for b in range(16):
        seen[:, b * 128 : (b + 1) * 128] = info[b]

    def sequence(s, carry):
        total[...] = jnp.zeros_like(total)
        for i in range(8):
            blocks = min(2 * i + 2, 9)
            width = blocks * 128
            own = 2 * i + c
            first = own - 8 if i >= 4 else 0
            begin = first * 128 if i < 4 else pl.multiple_of(first * 128, 128)
            tile = qd[i, s].astype(F32)
            pair = jnp.concatenate(
                [jnp.where(left, tile * (HD**-0.5), 0.0), jnp.where(left, 0.0, tile)], axis=0
            ).astype(BF)
            keys = kv[s, pl.ds(first, blocks)].reshape(width, 128)
            both = lax.dot_general(pair, keys, (((1,), (1,)), ((), ())), preferred_element_type=F32)
            asked = jnp.broadcast_to(info[own, pl.ds(3 + s, 1), :].astype(F32), (128, 128)).T
            held = seen[pl.ds(s, 1), pl.ds(begin, width)].astype(F32)
            pieces = []
            for b in range(blocks):
                fits = asked == held[:, b * 128 : (b + 1) * 128]
                if i < 4:
                    if b >= blocks - 2:
                        ahead = lane + (b - 2 * i - c) * 128 - row
                        fits = (fits | (ahead == 0)) & (ahead <= 0)
                elif b == blocks - 1:
                    fits = (fits | (lane == row)) & (lane <= row)
                elif b == 0:
                    fits = fits & (lane > row)
                pieces.append(jnp.where(fits, both[:128, b * 128 : (b + 1) * 128], -1e30))
            scores = jnp.concatenate(pieces, axis=1)
            expo = jnp.exp(scores - jnp.max(scores, axis=1, keepdims=True))
            probs = expo * (1.0 / jnp.sum(expo, axis=1, keepdims=True))
            d_probs = both[128:]
            delta = jnp.sum(probs * d_probs, axis=1, keepdims=True)
            mixed = jnp.concatenate([(probs * (d_probs - delta)).astype(BF), probs.astype(BF)], axis=0)
            back = jnp.dot(mixed, keys, preferred_element_type=F32)
            od[i, s] = jnp.where(left, back[:128] * (HD**-0.5), back[128:]).astype(BF)
            total[pl.ds(begin, width)] += lax.dot_general(
                mixed, pair, (((0,), (0,)), ((), ())), preferred_element_type=F32
            )
        dkv[s] = total[...].astype(BF).reshape(16, 128, 128)
        return carry

    lax.fori_loop(0, 3, sequence, 0)


def attend(qd, kv, info):
    return pl.pallas_call(
        attend_kernel,
        out_shape=[
            jax.ShapeDtypeStruct((8, 3, 128, 128), BF),
            jax.ShapeDtypeStruct((3, 16, 128, 128), BF),
        ],
        in_specs=[VMEM] * 3,
        out_specs=[VMEM] * 2,
        scratch_shapes=[pltpu.VMEM((8, 2048), jnp.int32), pltpu.VMEM((2048, 128), F32)],
        compiler_params=pltpu.CompilerParams(vmem_limit_bytes=48 * 2**20),
        name="attend",
    )(qd, kv, info)


def return_kernel(od, dkv, od_out, dkv_out, theirs, ours, send, recv, local):
    net = Net(send, recv)
    net.greet(SPREAD)
    me, c = net.chip, net.c
    net.push("s", dkv.at[:, :, 1 - c], theirs, "s", 1)
    mine = pltpu.make_async_copy(dkv.at[:, :, c], ours, local.at[0])
    mine.start()
    stay = pltpu.make_async_copy(od.at[me], od_out.at[:, :, lanes(me)], local.at[1])
    stay.start()
    far = [(dz, dx) for dz in (1, 0) for dx in (2, 1, 3, 0) if dz or dx]
    for dz, dx in far:
        other = lax.rem(lax.rem(net.z, 2) + dz, 2) * 4 + wrap(net.x + dx)
        net.push(("o", dz, dx), od.at[other], od_out.at[:, :, lanes(me)], dz, dx)
    mine.wait()
    net.arrived("s")
    ours[...] = ours[...] + theirs[...]
    for dz, dx in far:
        other = lax.rem(lax.rem(net.z, 2) + dz, 2) * 4 + wrap(net.x + dx)
        net.push(("k", dz, dx), ours.at[:, other], dkv_out.at[:, :, lanes(me)], dz, dx)
    last = pltpu.make_async_copy(ours.at[:, me], dkv_out.at[:, :, lanes(me)], local.at[2])
    last.start()
    stay.wait()
    last.wait()
    net.drain()


def give_back(od, dkv, cid):
    return pl.pallas_call(
        return_kernel,
        out_shape=[jax.ShapeDtypeStruct((3, 128, 1024), BF)] * 2,
        in_specs=[ANY] * 2,
        out_specs=[ANY] * 2,
        scratch_shapes=[
            pltpu.VMEM((3, 8, 128, 128), BF),
            pltpu.VMEM((3, 8, 128, 128), BF),
            pltpu.SemaphoreType.DMA((16,)),
            pltpu.SemaphoreType.DMA((16,)),
            pltpu.SemaphoreType.DMA((3,)),
        ],
        compiler_params=pltpu.CompilerParams(
            collective_id=cid, has_side_effects=True, vmem_limit_bytes=32 * 2**20
        ),
        name="heads_back",
    )(od, dkv.reshape(3, 8, 2, 128, 128))


class Scatter:
    def __init__(self, net, name, src, acc, sib, far1, near1, far2, near2, out):
        self.net, self.name, self.src, self.acc, self.sib = net, name, src, acc, sib
        self.far1, self.near1, self.far2, self.near2, self.out = far1, near1, far2, near2, out

    def axes(self, h):
        return ("z", "x") if h == 0 else ("x", "z")

    def first(self, h, d, r0, rn):
        n, rows = self.net, pl.ds(h * 32 + r0, rn)
        if h == 0:
            return self.acc.at[wrap(n.z + d), :, rows]
        return self.acc.at[:, wrap(n.x + d), rows]

    def second(self, h, d, r0, rn):
        n, rows = self.net, pl.ds(h * 32 + r0, rn)
        if h == 0:
            return self.acc.at[n.z, wrap(n.x + d), rows]
        return self.acc.at[wrap(n.z + d), n.x, rows]

    def begin(self, sems):
        n = self.net
        self.local = []
        for k in (2, 1, 3, 0):
            z = wrap(n.z + k)
            n.push((self.name, "s", k), self.src.at[z, :, 1 - n.c], self.sib.at[z], "s", 1)
            copy = pltpu.make_async_copy(self.src.at[z, :, n.c], self.acc.at[z], sems.at[k])
            copy.start()
            self.local.append(copy)

    def pair(self):
        n = self.net
        for copy, k in zip(self.local, (2, 1, 3, 0)):
            copy.wait()
            n.arrived((self.name, "s", k))
            z = wrap(n.z + k)

            def add(t, carry):
                rows = pl.ds(pl.multiple_of(lax.rem(t, 4) * 16, 16), 16)
                self.acc[z, t // 4, rows] = self.acc[z, t // 4, rows] + self.sib[z, t // 4, rows]
                return carry

            lax.fori_loop(0, 16, add, 0)
        for h in (0, 1):
            for w in (-1, 1):
                part = self.first(h, 2, 0 if w == -1 else 16, 16)
                n.push((self.name, h, "f1", w), part, self.far1.at[h, 0 if w == -1 else 1], self.axes(h)[0], w)

    def step3(self):
        n = self.net
        for h in (0, 1):
            for w in (-1, 1):
                k = 0 if w == -1 else 1
                n.arrived((self.name, h, "f1", w))
                part = self.first(h, w, 16 * k, 16)

                def add(t, carry):
                    part[t] = part[t] + self.far1[h, k, t]
                    return carry

                lax.fori_loop(0, 4, add, 0)
                n.push((self.name, h, "n1", w), self.first(h, w, 0, 32), self.near1.at[h, k], self.axes(h)[0], w)

    def step4(self):
        n = self.net
        for h in (0, 1):
            n.arrived((self.name, h, "n1", -1))
            n.arrived((self.name, h, "n1", 1))
            part = self.first(h, 0, 0, 32)

            def add(t, carry):
                for r in (0, 16):
                    rows = pl.ds(r, 16)
                    value = part[t, rows].astype(F32) + self.near1[h, 0, t, rows].astype(F32)
                    part[t, rows] = (value + self.near1[h, 1, t, rows].astype(F32)).astype(BF)
                return carry

            lax.fori_loop(0, 4, add, 0)
            for w in (-1, 1):
                k = 0 if w == -1 else 1
                n.push((self.name, h, "f2", w), self.second(h, 2, 16 * k, 16), self.far2.at[h, k], self.axes(h)[1], w)

    def step5(self):
        n = self.net
        for h in (0, 1):
            for w in (-1, 1):
                k = 0 if w == -1 else 1
                n.arrived((self.name, h, "f2", w))
                part = self.second(h, w, 16 * k, 16)
                part[...] = part[...] + self.far2[h, k]
                n.push((self.name, h, "n2", w), self.second(h, w, 0, 32), self.near2.at[h, k], self.axes(h)[1], w)

    def step6(self):
        n = self.net
        for h in (0, 1):
            n.arrived((self.name, h, "n2", -1))
            n.arrived((self.name, h, "n2", 1))
            part = self.second(h, 0, 0, 32)
            for r in (0, 16):
                rows = pl.ds(r, 16)
                value = part[rows].astype(F32) + self.near2[h, 0, rows].astype(F32)
                self.out[pl.ds(h * 32 + r, 16)] = value + self.near2[h, 1, rows].astype(F32)


class Sum:
    def __init__(self, net, name, src, acc, far, near, out):
        self.net, self.name, self.src, self.acc = net, name, src, acc
        self.far, self.near, self.out = far, near, out

    def begin(self, sem):
        self.local = pltpu.make_async_copy(self.src, self.acc, sem)
        self.local.start()

    def step1(self):
        n = self.net
        self.local.wait()
        for k, w in ((0, -1), (1, 1)):
            n.push((self.name, "f", w), self.acc.at[wrap(n.y + 2), pl.ds(48 * k, 48)], self.far.at[k], "y", w)

    def step2(self):
        n = self.net
        for k, w in ((0, -1), (1, 1)):
            n.arrived((self.name, "f", w))
            part = self.acc.at[wrap(n.y + w), pl.ds(48 * k, 48)]
            part[...] = part[...] + self.far[k]
            n.push((self.name, "n", w), self.acc.at[wrap(n.y + w)], self.near.at[k], "y", w)

    def step3(self, sem):
        n = self.net
        n.arrived((self.name, "n", -1))
        n.arrived((self.name, "n", 1))
        part = self.acc.at[n.y]
        for r in range(0, 96, 16):
            rows = pl.ds(r, 16)
            value = part[rows].astype(F32) + self.near[0, rows].astype(F32)
            part[rows] = (value + self.near[1, rows].astype(F32)).astype(BF)
        for w in (-1, 1):
            n.push((self.name, "g", w), self.acc.at[n.y], self.out.at[n.y], "y", w)
        self.last = pltpu.make_async_copy(self.acc.at[n.y], self.out.at[n.y], sem)
        self.last.start()

    def step4(self):
        n = self.net
        for k, w in ((0, -1), (1, 1)):
            n.arrived((self.name, "g", w))
            part = self.out.at[wrap(n.y - w), pl.ds(48 * k, 48)]
            n.push((self.name, "gf", w), part, part, "y", w)


def vector_sum(net, src, pairs, alongx, alongz, alongy, out):
    z, x, c, y = net.z, net.x, net.c, net.y
    pairs[c] = src[...]
    net.push("vs", pairs.at[c], pairs.at[c], "s", 1)
    yield
    net.arrived("vs")
    alongx[x] = pairs[0] + pairs[1]
    for w in (1, -1, 2):
        net.push(("vx", w), alongx.at[x], alongx.at[x], "x", w)
    yield
    for w in (1, -1, 2):
        net.arrived(("vx", w))
    alongz[z] = (alongx[0] + alongx[1]) + (alongx[2] + alongx[3])
    for w in (1, -1, 2):
        net.push(("vz", w), alongz.at[z], alongz.at[z], "z", w)
    yield
    for w in (1, -1, 2):
        net.arrived(("vz", w))
    alongy[y] = (alongz[0] + alongz[1]) + (alongz[2] + alongz[3])
    out[...] = alongy[y]
    for w in (1, -1, 2):
        net.push(("vy", w), alongy.at[y], alongy.at[y], "y", w)
    yield
    for w in (1, -1, 2):
        net.arrived(("vy", w))
    out[0:2] = (alongy[0, 0:2] + alongy[1, 0:2]) + (alongy[2, 0:2] + alongy[3, 0:2])
    yield


def reduce_kernel(count, *refs):
    srcs, shares, vecs = refs[:count], refs[count : count + 2], refs[count + 2]
    refs = refs[count + 3 :]
    outs, sums, vec_out = refs[:count], refs[count : count + 2], refs[count + 2]
    refs = refs[count + 3 :]
    bufs = [refs[6 * i : 6 * i + 6] for i in range(count)]
    refs = refs[6 * count :]
    accs, fars, nears = refs[0:2], refs[2:4], refs[4:6]
    pairs, alongx, alongz, alongy, send, recv, local = refs[6:]
    net = Net(send, recv)
    net.greet(RING_XZ + RING_Y + FAR)
    parts = [Scatter(net, ("g", i), srcs[i], *bufs[i], outs[i]) for i in range(count)]
    ys = [Sum(net, ("y", i), shares[i], accs[i], fars[i], nears[i], sums[i]) for i in range(2)]
    vec = vector_sum(net, vecs, pairs, alongx, alongz, alongy, vec_out)
    for i in (0, 1):
        ys[i].begin(local.at[4 * count + i])
    parts[0].begin(local.at[pl.ds(0, 4)])
    ys[0].step1()
    for t in range(count + 4):
        if t < count:
            if t + 1 < count:
                parts[t + 1].begin(local.at[pl.ds(4 * t + 4, 4)])
            parts[t].pair()
        if t == 0:
            next(vec)
        if t == 1:
            ys[0].step2()
            ys[1].step1()
        if t == 2:
            ys[0].step3(local.at[4 * count + 2])
            ys[1].step2()
        if t == 3:
            ys[0].step4()
            ys[1].step3(local.at[4 * count + 3])
        if t == 4:
            ys[1].step4()
        if 0 <= t - 1 < count:
            parts[t - 1].step3()
        if 0 <= t - 2 < count:
            parts[t - 2].step4()
        if 0 <= t - 3 < count:
            parts[t - 3].step5()
        if 0 <= t - 4 < count:
            parts[t - 4].step6()
        if 1 <= t <= 4:
            next(vec)
    for y in ys:
        y.last.wait()
    net.drain()


def reduce(grads, shares, vectors, cid):
    count = len(grads)
    widths = [g.shape[1] for g in grads]
    scratch = []
    for w in widths:
        scratch += [
            pltpu.VMEM((4, 4, 64, w), BF),
            pltpu.VMEM((4, 4, 64, w), BF),
            pltpu.VMEM((2, 2, 4, 16, w), BF),
            pltpu.VMEM((2, 2, 4, 32, w), BF),
            pltpu.VMEM((2, 2, 16, w), BF),
            pltpu.VMEM((2, 2, 32, w), BF),
        ]
    scratch += [pltpu.VMEM((4, 96, 2048), BF)] * 2
    scratch += [pltpu.VMEM((2, 48, 2048), BF)] * 2
    scratch += [pltpu.VMEM((2, 96, 2048), BF)] * 2
    scratch += [pltpu.VMEM((n, 8, 2048), F32) for n in (2, 4, 4, 4)]
    sems = 20 * count + 2 * 8 + 12
    scratch += [pltpu.SemaphoreType.DMA((sems,))] * 2 + [pltpu.SemaphoreType.DMA((4 * count + 4,))]
    outs = pl.pallas_call(
        functools.partial(reduce_kernel, count),
        out_shape=[jax.ShapeDtypeStruct((64, w), F32) for w in widths]
        + [jax.ShapeDtypeStruct((4, 96, 2048), BF)] * 2
        + [jax.ShapeDtypeStruct((8, 2048), F32)],
        in_specs=[ANY] * (count + 2) + [VMEM],
        out_specs=[VMEM] * count + [ANY] * 2 + [VMEM],
        scratch_shapes=scratch,
        compiler_params=pltpu.CompilerParams(
            collective_id=cid, has_side_effects=True, vmem_limit_bytes=60 * 2**20
        ),
        name="reduce_all",
    )(*[g.reshape(4, 4, 2, 64, g.shape[1]) for g in grads], *[s.reshape(4, 96, 2048) for s in shares], vectors)
    return outs[:count], [o.reshape(384, 2048) for o in outs[count : count + 2]], outs[count + 2]


def mix(tensor, cosine, sine):
    half = ROT // 2
    first, second = tensor[..., :half], tensor[..., half:ROT]
    return jnp.concatenate(
        [first * cosine - second * sine, second * cosine + first * sine, tensor[..., ROT:]], axis=-1
    )


def dot(a, b, dims):
    return lax.dot_general(a, b, (dims, ((), ())), preferred_element_type=F32)


def local(
    hidden_in, segments, keep_mask, ln_gain, ln_shift, w_qkv, b_qkv, w_dense, b_dense, w_up, b_up, w_down, b_down,
    cotangent,
):
    rows, width = 384, 2048
    kv_shard = jnp.stack([w_qkv[:, 1].reshape(64, 8, HD), w_qkv[:, 2].reshape(64, 8, HD)], axis=2)
    kv_shard = kv_shard.reshape(64, 1024).astype(BF)
    q_shard = w_qkv[:, 0].astype(BF)
    dense_shard = w_dense.T.astype(BF)
    up_shard = w_up.astype(BF)
    down_shard = w_down.T.astype(BF)
    kv_w, q_w, dense_t = gather([kv_shard, q_shard, dense_shard], 0, "gather_heads")

    hidden = hidden_in.reshape(rows, width).astype(F32)
    upstream = cotangent.reshape(rows, width)
    centered = hidden - jnp.mean(hidden, axis=-1, keepdims=True)
    inverse = lax.rsqrt(jnp.mean(centered * centered, axis=-1, keepdims=True) + 1e-05)
    standard = centered * inverse
    inputs = (standard * ln_gain + ln_shift).astype(BF)

    positions = lax.axis_index("seq") * 128 + jnp.arange(128, dtype=jnp.int32)
    half = ROT // 2
    frequency = 10000.0 ** (-(jnp.arange(half, dtype=F32) * 2.0) / ROT)
    angles = positions.astype(F32)[:, None] * frequency[None, :]
    cosine = jnp.tile(jnp.cos(angles), (3, 1))[:, None, :]
    sine = jnp.tile(jnp.sin(angles), (3, 1))[:, None, :]

    b_kv = jnp.stack([b_qkv[1].reshape(8, HD), b_qkv[2].reshape(8, HD)], axis=1).reshape(1024)
    kv = (dot(inputs, kv_w, ((1,), (0,))) + b_kv).reshape(rows, 8, 128)
    kv = jnp.concatenate([mix(kv[..., :HD], cosine, sine), kv[..., HD:]], axis=-1).astype(BF)
    queries = (dot(inputs, q_w, ((1,), (0,))) + b_qkv[0]).reshape(rows, 8, HD)
    queries = mix(queries, cosine, sine).astype(BF)
    d_attended = dot(upstream, dense_t, ((1,), (0,))).astype(BF).reshape(rows, 8, HD)
    qd = jnp.concatenate([queries, d_attended], axis=-1).reshape(3, 128, 1024)
    kv = kv.reshape(3, 128, 1024)
    info = jnp.concatenate(
        [jnp.where(keep_mask > 0, segments, -1), segments, jnp.zeros((2, 128), jnp.int32)], axis=0
    )
    qd_all, kv_all, info_all = exchange(qd, kv, info, 1)
    up_shard, down_shard, qd_all = lax.optimization_barrier((up_shard, down_shard, qd_all))
    up_w, down_t = gather([up_shard, down_shard], 2, "gather_units")
    od_all, dkv_all = attend(qd_all, kv_all, info_all)
    od, dkv = give_back(od_all, dkv_all, 3)

    od = od.reshape(rows, 8, 128)
    dkv = dkv.reshape(rows, 8, 128).astype(F32)
    attended = od[..., HD:].reshape(rows, 512)
    d_queries = mix(od[..., :HD].astype(F32), cosine, -sine).reshape(rows, 512).astype(BF)
    d_kv = jnp.concatenate([mix(dkv[..., :HD], cosine, -sine), dkv[..., HD:]], axis=-1)
    d_kv = d_kv.reshape(rows, 1024).astype(BF)

    up_pre = dot(inputs, up_w, ((1,), (0,))) + b_up
    active, pull = jax.vjp(functools.partial(jax.nn.gelu, approximate=True), up_pre)
    active = active.astype(BF)
    d_active = dot(upstream, down_t, ((1,), (0,)))
    d_up = pull(d_active)[0].astype(BF)
    shares = dot(attended, dense_t, ((1,), (1,))) + dot(active, down_t, ((1,), (1,)))
    d_shares = (
        dot(d_queries, q_w, ((1,), (1,))) + dot(d_kv, kv_w, ((1,), (1,))) + dot(d_up, up_w, ((1,), (1,)))
    )
    grads = [
        dot(inputs, d_up, ((0,), (0,))).astype(BF),
        dot(upstream, active, ((0,), (0,))).astype(BF),
        dot(inputs, d_kv, ((0,), (0,))).astype(BF),
        dot(inputs, d_queries, ((0,), (0,))).astype(BF),
        dot(upstream, attended, ((0,), (0,))).astype(BF),
    ]
    pad = jnp.zeros((512,), F32)
    vectors = jnp.stack(
        [
            jnp.sum(d_shares * standard, axis=0),
            jnp.sum(d_shares, axis=0),
            jnp.sum(upstream.astype(F32), axis=0),
            jnp.sum(d_up.astype(F32), axis=0),
            jnp.concatenate([jnp.sum(d_kv.astype(F32), axis=0), jnp.sum(d_queries.astype(F32), axis=0), pad]),
            jnp.zeros((width,), F32),
            jnp.zeros((width,), F32),
            jnp.zeros((width,), F32),
        ]
    )
    parts, (summed, d_inputs), vectors = reduce(grads, [shares.astype(BF), d_shares.astype(BF)], vectors, 4)
    grad_up, grad_down, grad_kv, grad_q, grad_dense = parts
    block_out = hidden + summed.astype(F32) + b_dense + b_down
    d_inputs = d_inputs.astype(F32)
    scaled = d_inputs * ln_gain
    back_norm = inverse * (
        scaled
        - jnp.mean(scaled, axis=-1, keepdims=True)
        - standard * jnp.mean(scaled * standard, axis=-1, keepdims=True)
    )
    input_grad = upstream.astype(F32) + back_norm
    grad_kv = grad_kv.reshape(64, 8, 2, HD)
    grad_qkv = jnp.stack([grad_q, grad_kv[:, :, 0].reshape(64, 512), grad_kv[:, :, 1].reshape(64, 512)], axis=1)
    bias_kv = vectors[4, :1024].reshape(8, 2, HD)
    grad_bqkv = jnp.stack([vectors[4, 1024:1536], bias_kv[:, 0].reshape(512), bias_kv[:, 1].reshape(512)])
    return (
        block_out.reshape(3, 128, width),
        input_grad.reshape(3, 128, width),
        vectors[0],
        vectors[1],
        grad_qkv,
        grad_bqkv,
        grad_dense.T,
        vectors[2],
        grad_up,
        vectors[3],
        grad_down.T,
        vectors[2],
    )


def solution(mesh):
    return jax.shard_map(
        local,
        mesh=mesh,
        in_specs=(
            P("dp", "seq", None),
            P("dp", "seq"),
            P("dp", "seq"),
            P(),
            P(),
            P(("dp", "seq"), None, "tp"),
            P(None, "tp"),
            P("tp", ("dp", "seq")),
            P(),
            P(("dp", "seq"), "tp"),
            P("tp"),
            P("tp", ("dp", "seq")),
            P(),
            P("dp", "seq", None),
        ),
        out_specs=(
            P("dp", "seq", None),
            P("dp", "seq", None),
            P(),
            P(),
            P(("dp", "seq"), None, "tp"),
            P(None, "tp"),
            P("tp", ("dp", "seq")),
            P(),
            P(("dp", "seq"), "tp"),
            P("tp"),
            P("tp", ("dp", "seq")),
            P(),
        ),
        check_vma=False,
    )
```

```python
import functools

import jax
import jax.numpy as jnp
from jax import lax
from jax.experimental import pallas as pl
from jax.experimental.pallas import tpu as pltpu
from jax.sharding import PartitionSpec as P

MESH = pl.DeviceIdType.MESH
HD = 64
ROT = 32
WINDOW = 1024
BF = jnp.bfloat16
F32 = jnp.float32
ANY = pl.BlockSpec(memory_space=pl.ANY)
VMEM = pl.BlockSpec(memory_space=pltpu.VMEM)


def wrap(v):
    return lax.rem(v + 4, 4)


def place():
    dp, sq, tp = lax.axis_index("dp"), lax.axis_index("seq"), lax.axis_index("tp")
    return dp * 2 + sq // 8, lax.rem(sq // 2, 4), lax.rem(sq, 2), tp


def device(z, x, c, y):
    z, x, y = wrap(z), wrap(x), wrap(y)
    return {"dp": z // 2, "seq": lax.rem(z, 2) * 8 + x * 2 + c, "tp": y}


class Net:
    def __init__(self, send, recv):
        self.send, self.recv, self.n, self.out, self.keys = send, recv, 0, {}, {}
        self.z, self.x, self.c, self.y = place()
        self.flip = 1 - 2 * lax.rem(self.z, 2)
        self.chip = lax.rem(self.z, 2) * 4 + self.x

    def to(self, axis, way):
        z, x, c, y = self.z, self.x, self.c, self.y
        if axis == "s":
            return device(z, x, 1 - c, y)
        if axis == "x":
            return device(z, x + way, c, y)
        if axis == "z":
            return device(z + way, x, c, y)
        if axis == "y":
            return device(z, x, c, y + way)
        return device(z + axis * self.flip, x + way, c, y)

    def greet(self, targets):
        bar = pltpu.get_barrier_semaphore()
        for axis, way in targets:
            pl.semaphore_signal(bar, inc=1, device_id=self.to(axis, way), device_id_type=MESH)
        pl.semaphore_wait(bar, len(targets))

    def push(self, key, src, dst, axis, way):
        k = self.n
        self.n += 1
        copy = pltpu.make_async_remote_copy(
            src_ref=src,
            dst_ref=dst,
            send_sem=self.send.at[k],
            recv_sem=self.recv.at[k],
            device_id=self.to(axis, way),
            device_id_type=MESH,
        )
        copy.start()
        self.out[key] = copy
        self.keys[key] = copy

    def arrived(self, key):
        self.keys.pop(key).wait_recv()

    def sent(self, key):
        self.out.pop(key).wait_send()

    def drain(self):
        for key in list(self.out):
            self.sent(key)
        for key in list(self.keys):
            self.arrived(key)


RING_XZ = (("x", 1), ("x", -1), ("z", 1), ("z", -1), ("s", 1))
RING_Y = (("y", 1), ("y", -1))
FAR = (("x", 2), ("z", 2), ("y", 2))
SPREAD = tuple((dz, dx) for dz in (0, 1) for dx in range(4) if dz or dx) + (("s", 1),)


class Gather:
    def __init__(self, net, name, src, dst):
        self.net, self.name, self.src, self.dst = net, name, src, dst
        self.half, self.quarter = src.shape[0] // 2, src.shape[0] // 4

    def at(self, h, a, b, r0, rn):
        n = self.net
        z, x = (n.z + b, n.x + a) if h == 0 else (n.z + a, n.x + b)
        return self.dst.at[wrap(z), wrap(x), n.c, pl.ds(h * self.half + r0, rn)]

    def own(self, h):
        return self.src.at[pl.ds(h * self.half, self.half)]

    def axes(self, h):
        return ("x", "z") if h == 0 else ("z", "x")

    def begin(self, sem):
        n = self.net
        for h in (0, 1):
            for w in (1, -1):
                n.push((self.name, h, "A", w), self.own(h), self.at(h, 0, 0, 0, self.half), self.axes(h)[0], w)
        for h in (0, 1):
            for w in (1, -1):
                n.push((self.name, h, "B", 0, w), self.own(h), self.at(h, 0, 0, 0, self.half), self.axes(h)[1], w)
        whole = self.dst.at[n.z, n.x, n.c]
        n.push((self.name, "s"), self.src, whole, "s", 1)
        self.local = pltpu.make_async_copy(self.src, whole, sem)
        self.local.start()

    def spread(self, h, a):
        n = self.net
        block = self.at(h, a, 0, 0, self.half)
        for w in (1, -1):
            n.push((self.name, h, "B", a, w), block, block, self.axes(h)[1], w)
        n.push((self.name, h, "s", a, 0), block, block, "s", 1)

    def near(self):
        n = self.net
        for h in (0, 1):
            for w in (1, -1):
                n.arrived((self.name, h, "A", w))
                part = self.at(h, -w, 0, 0 if w == 1 else self.quarter, self.quarter)
                n.push((self.name, h, "AF", w), part, part, self.axes(h)[0], w)
                self.spread(h, -w)

    def far(self):
        for h in (0, 1):
            for w in (1, -1):
                self.net.arrived((self.name, h, "AF", w))
            self.spread(h, 2)

    def pass_on(self, a):
        n = self.net
        for h in (0, 1):
            for w in (1, -1):
                n.arrived((self.name, h, "B", a, w))
                part = self.at(h, a, -w, 0 if w == 1 else self.quarter, self.quarter)
                n.push((self.name, h, "BF", a, w), part, part, self.axes(h)[1], w)
                block = self.at(h, a, -w, 0, self.half)
                n.push((self.name, h, "s", a, -w), block, block, "s", 1)

    def close(self, a):
        n = self.net
        for h in (0, 1):
            for w in (1, -1):
                n.arrived((self.name, h, "BF", a, w))
            block = self.at(h, a, 2, 0, self.half)
            n.push((self.name, h, "s", a, 2), block, block, "s", 1)


def gather_kernel(count, *refs):
    srcs, dsts = refs[:count], refs[count : 2 * count]
    send, recv, local = refs[2 * count :]
    net = Net(send, recv)
    net.greet(RING_XZ)
    parts = [Gather(net, i, srcs[i], dsts[i]) for i in range(count)]
    parts[0].begin(local.at[0])
    for i in range(count):
        if i + 1 < count:
            parts[i + 1].begin(local.at[i + 1])
        parts[i].near()
        if i > 0:
            for a in (0, -1, 1):
                parts[i - 1].pass_on(a)
        parts[i].far()
        if i > 0:
            parts[i - 1].pass_on(2)
            for a in (0, -1, 1, 2):
                parts[i - 1].close(a)
    for a in (0, -1, 1, 2):
        parts[-1].pass_on(a)
    for a in (0, -1, 1, 2):
        parts[-1].close(a)
    for part in parts:
        part.local.wait()
    net.drain()


def gather(shards, cid, name):
    count = len(shards)
    outs = pl.pallas_call(
        functools.partial(gather_kernel, count),
        out_shape=[jax.ShapeDtypeStruct((4, 4, 2) + s.shape, s.dtype) for s in shards],
        in_specs=[ANY] * count,
        out_specs=[ANY] * count,
        scratch_shapes=[
            pltpu.SemaphoreType.DMA((80 * count,)),
            pltpu.SemaphoreType.DMA((80 * count,)),
            pltpu.SemaphoreType.DMA((count,)),
        ],
        compiler_params=pltpu.CompilerParams(collective_id=cid, has_side_effects=True),
        name=name,
    )(*shards)
    return [o.reshape(32 * s.shape[0], s.shape[1]) for o, s in zip(outs, shards)]


def lanes(chip):
    return pl.ds(pl.multiple_of(chip * 128, 128), 128)


def exchange_kernel(qd, kv, info, qd_out, kv_out, info_out, send, recv, local):
    net = Net(send, recv)
    net.greet(SPREAD)
    me, c = net.chip, net.c
    mine = 2 * me + c
    for dz in (1, 0):
        for dx in (2, 1, 3, 0):
            if not (dz or dx):
                continue
            other = lax.rem(lax.rem(net.z, 2) + dz, 2) * 4 + wrap(net.x + dx)
            net.push(("k", dz, dx), kv.at[:, :, lanes(other)], kv_out.at[:, mine], dz, dx)
            net.push(("i", dz, dx), info, info_out.at[mine], dz, dx)
            net.push(("q", dz, dx), qd.at[:, :, lanes(other)], qd_out.at[me], dz, dx)
    net.push("ks", kv.at[:, :, lanes(me)], kv_out.at[:, mine], "s", 1)
    net.push("is", info, info_out.at[mine], "s", 1)
    stays = [
        pltpu.make_async_copy(qd.at[:, :, lanes(me)], qd_out.at[me], local.at[0]),
        pltpu.make_async_copy(kv.at[:, :, lanes(me)], kv_out.at[:, mine], local.at[1]),
        pltpu.make_async_copy(info, info_out.at[mine], local.at[2]),
    ]
    for stay in stays:
        stay.start()
    for dz in (1, 0):
        for dx in (2, 1, 3, 0):
            if not (dz or dx):
                continue
            other = lax.rem(lax.rem(net.z, 2) + dz, 2) * 4 + wrap(net.x - dx)
            slot = 2 * other + c
            net.arrived(("k", dz, dx))
            net.push(("ks", dz, dx), kv_out.at[:, slot], kv_out.at[:, slot], "s", 1)
            net.arrived(("i", dz, dx))
            net.push(("is", dz, dx), info_out.at[slot], info_out.at[slot], "s", 1)
    for stay in stays:
        stay.wait()
    net.drain()


def exchange(qd, kv, info, cid):
    return pl.pallas_call(
        exchange_kernel,
        out_shape=[
            jax.ShapeDtypeStruct((8, 3, 128, 128), BF),
            jax.ShapeDtypeStruct((3, 16, 128, 128), BF),
            jax.ShapeDtypeStruct((16, 8, 128), jnp.int32),
        ],
        in_specs=[ANY] * 3,
        out_specs=[ANY] * 3,
        scratch_shapes=[
            pltpu.SemaphoreType.DMA((48,)),
            pltpu.SemaphoreType.DMA((48,)),
            pltpu.SemaphoreType.DMA((3,)),
        ],
        compiler_params=pltpu.CompilerParams(collective_id=cid, has_side_effects=True),
        name="heads_out",
    )(qd, kv, info)


def attend_kernel(qd, kv, info, od, dkv, seen, total):
    c = lax.rem(lax.axis_index("seq"), 2)
    lane = lax.broadcasted_iota(jnp.int32, (128, 128), 1)
    row = lax.broadcasted_iota(jnp.int32, (128, 128), 0)
    left = lane < 64
    for b in range(16):
        seen[:, b * 128 : (b + 1) * 128] = info[b]

    def sequence(s, carry):
        total[...] = jnp.zeros_like(total)
        for i in range(8):
            blocks = min(2 * i + 2, 9)
            width = blocks * 128
            own = 2 * i + c
            first = own - 8 if i >= 4 else 0
            begin = first * 128 if i < 4 else pl.multiple_of(first * 128, 128)
            tile = qd[i, s].astype(F32)
            pair = jnp.concatenate(
                [jnp.where(left, tile * (HD**-0.5), 0.0), jnp.where(left, 0.0, tile)], axis=0
            ).astype(BF)
            keys = kv[s, pl.ds(first, blocks)].reshape(width, 128)
            both = lax.dot_general(pair, keys, (((1,), (1,)), ((), ())), preferred_element_type=F32)
            asked = jnp.broadcast_to(info[own, pl.ds(3 + s, 1), :].astype(F32), (128, 128)).T
            held = seen[pl.ds(s, 1), pl.ds(begin, width)].astype(F32)
            pieces = []
            for b in range(blocks):
                fits = asked == held[:, b * 128 : (b + 1) * 128]
                if i < 4:
                    if b >= blocks - 2:
                        ahead = lane + (b - 2 * i - c) * 128 - row
                        fits = (fits | (ahead == 0)) & (ahead <= 0)
                elif b == blocks - 1:
                    fits = (fits | (lane == row)) & (lane <= row)
                elif b == 0:
                    fits = fits & (lane > row)
                pieces.append(jnp.where(fits, both[:128, b * 128 : (b + 1) * 128], -1e30))
            scores = jnp.concatenate(pieces, axis=1)
            expo = jnp.exp(scores - jnp.max(scores, axis=1, keepdims=True))
            probs = expo * (1.0 / jnp.sum(expo, axis=1, keepdims=True))
            d_probs = both[128:]
            delta = jnp.sum(probs * d_probs, axis=1, keepdims=True)
            mixed = jnp.concatenate([(probs * (d_probs - delta)).astype(BF), probs.astype(BF)], axis=0)
            back = jnp.dot(mixed, keys, preferred_element_type=F32)
            od[i, s] = jnp.where(left, back[:128] * (HD**-0.5), back[128:]).astype(BF)
            total[pl.ds(begin, width)] += lax.dot_general(
                mixed, pair, (((0,), (0,)), ((), ())), preferred_element_type=F32
            )
        dkv[s] = total[...].astype(BF).reshape(16, 128, 128)
        return carry

    lax.fori_loop(0, 3, sequence, 0)


def attend(qd, kv, info):
    return pl.pallas_call(
        attend_kernel,
        out_shape=[
            jax.ShapeDtypeStruct((8, 3, 128, 128), BF),
            jax.ShapeDtypeStruct((3, 16, 128, 128), BF),
        ],
        in_specs=[VMEM] * 3,
        out_specs=[VMEM] * 2,
        scratch_shapes=[pltpu.VMEM((8, 2048), jnp.int32), pltpu.VMEM((2048, 128), F32)],
        compiler_params=pltpu.CompilerParams(vmem_limit_bytes=48 * 2**20),
        name="attend",
    )(qd, kv, info)


def dot(a, b, dims):
    return lax.dot_general(a, b, (dims, ((), ())), preferred_element_type=F32)


def turn(tensor, tables, rows, sign):
    cosine, low, high = tables
    moved = pltpu.roll(tensor, 16, 1) * high[rows] - pltpu.roll(tensor, 112, 1) * low[rows]
    return tensor * cosine[rows] + sign * moved


class Scatter:
    def __init__(self, net, name, acc, far1, near1, far2, near2, out):
        self.net, self.name, self.acc = net, name, acc
        self.far1, self.near1, self.far2, self.near2, self.out = far1, near1, far2, near2, out

    def axes(self, h):
        return ("z", "x") if h == 0 else ("x", "z")

    def first(self, h, d, r0, rn):
        n, rows = self.net, pl.ds(h * 32 + r0, rn)
        if h == 0:
            return self.acc.at[wrap(n.z + d), :, rows]
        return self.acc.at[:, wrap(n.x + d), rows]

    def second(self, h, d, r0, rn):
        n, rows = self.net, pl.ds(h * 32 + r0, rn)
        if h == 0:
            return self.acc.at[n.z, wrap(n.x + d), rows]
        return self.acc.at[wrap(n.z + d), n.x, rows]

    def step2(self):
        n = self.net
        for h in (0, 1):
            for k, w in ((0, -1), (1, 1)):
                n.push((self.name, h, "f1", w), self.first(h, 2, 16 * k, 16), self.far1.at[h, k], self.axes(h)[0], w)

    def step3(self):
        n = self.net
        for h in (0, 1):
            for k, w in ((0, -1), (1, 1)):
                n.arrived((self.name, h, "f1", w))
                part = self.first(h, w, 16 * k, 16)

                def add(t, carry):
                    part[t] = part[t] + self.far1[h, k, t]
                    return carry

                lax.fori_loop(0, 4, add, 0)
                n.push((self.name, h, "n1", w), self.first(h, w, 0, 32), self.near1.at[h, k], self.axes(h)[0], w)

    def step4(self):
        n = self.net
        for h in (0, 1):
            n.arrived((self.name, h, "n1", -1))
            n.arrived((self.name, h, "n1", 1))
            part = self.first(h, 0, 0, 32)

            def add(t, carry):
                for r in (0, 16):
                    rows = pl.ds(r, 16)
                    value = part[t, rows].astype(F32) + self.near1[h, 0, t, rows].astype(F32)
                    part[t, rows] = (value + self.near1[h, 1, t, rows].astype(F32)).astype(BF)
                return carry

            lax.fori_loop(0, 4, add, 0)
            for k, w in ((0, -1), (1, 1)):
                n.push((self.name, h, "f2", w), self.second(h, 2, 16 * k, 16), self.far2.at[h, k], self.axes(h)[1], w)

    def step5(self):
        n = self.net
        for h in (0, 1):
            for k, w in ((0, -1), (1, 1)):
                n.arrived((self.name, h, "f2", w))
                part = self.second(h, w, 16 * k, 16)
                part[...] = part[...] + self.far2[h, k]
                n.push((self.name, h, "n2", w), self.second(h, w, 0, 32), self.near2.at[h, k], self.axes(h)[1], w)

    def step6(self):
        n = self.net
        for h in (0, 1):
            n.arrived((self.name, h, "n2", -1))
            n.arrived((self.name, h, "n2", 1))
            part = self.second(h, 0, 0, 32)
            for r in (0, 16):
                rows = pl.ds(r, 16)
                value = part[rows].astype(F32) + self.near2[h, 0, rows].astype(F32)
                self.out[pl.ds(h * 32 + r, 16)] = value + self.near2[h, 1, rows].astype(F32)


class Sum:
    def __init__(self, net, name, acc, far, near, out):
        self.net, self.name, self.acc = net, name, acc
        self.far, self.near, self.out = far, near, out

    def block(self, d, r0, rn):
        start = pl.multiple_of(wrap(self.net.y + d) * 192 + r0, 16)
        return self.acc.at[pl.ds(start, rn)]

    def step1(self, value):
        n = self.net

        def fill(d, carry):
            for half in (0, 1):
                rows = pl.ds(pl.multiple_of(d * 192 + half * 96, 16), 96)
                held = value[pl.ds(pl.multiple_of(d * 96, 16), 96), pl.ds(half * 1024, 1024)]
                self.acc[rows] = held.astype(BF)
            return carry

        lax.fori_loop(0, 4, fill, 0)
        for k, w in ((0, -1), (1, 1)):
            n.push((self.name, "f", w), self.block(2, 96 * k, 96), self.far.at[k], "y", w)

    def step2(self):
        n = self.net
        for k, w in ((0, -1), (1, 1)):
            n.arrived((self.name, "f", w))
            part = self.block(w, 96 * k, 96)
            part[...] = part[...] + self.far[k]
            n.push((self.name, "n", w), self.block(w, 0, 192), self.near.at[k], "y", w)

    def step3(self, sem):
        n = self.net
        n.arrived((self.name, "n", -1))
        n.arrived((self.name, "n", 1))
        part = self.block(0, 0, 192)

        def add(t, carry):
            rows = pl.ds(pl.multiple_of(t * 16, 16), 16)
            value = part[rows].astype(F32) + self.near[0, rows].astype(F32)
            part[rows] = (value + self.near[1, rows].astype(F32)).astype(BF)
            return carry

        lax.fori_loop(0, 12, add, 0)
        for w in (-1, 1):
            n.push((self.name, "g", w), part, self.out.at[n.y], "y", w)
        self.last = pltpu.make_async_copy(part, self.out.at[n.y], sem)
        self.last.start()

    def step4(self):
        n = self.net
        for k, w in ((0, -1), (1, 1)):
            n.arrived((self.name, "g", w))
            part = self.out.at[wrap(n.y - w), pl.ds(96 * k, 96)]
            n.push((self.name, "gf", w), part, part, "y", w)

    def step5(self, dst, sem):
        n = self.net
        self.last.wait()
        for w in (-1, 1):
            n.arrived((self.name, "gf", w))
        copy = pltpu.make_async_copy(self.out, dst, sem)
        copy.start()
        return copy


def vector_sum(net, src, pairs, alongx, alongz, alongy, out):
    z, x, c, y = net.z, net.x, net.c, net.y
    pairs[c] = src[...]
    net.push("vs", pairs.at[c], pairs.at[c], "s", 1)
    yield
    net.arrived("vs")
    alongx[x] = pairs[0] + pairs[1]
    for w in (1, -1, 2):
        net.push(("vx", w), alongx.at[x], alongx.at[x], "x", w)
    yield
    for w in (1, -1, 2):
        net.arrived(("vx", w))
    alongz[z] = (alongx[0] + alongx[1]) + (alongx[2] + alongx[3])
    for w in (1, -1, 2):
        net.push(("vz", w), alongz.at[z], alongz.at[z], "z", w)
    yield
    for w in (1, -1, 2):
        net.arrived(("vz", w))
    alongy[y] = (alongz[0] + alongz[1]) + (alongz[2] + alongz[3])
    out[...] = alongy[y]
    for w in (1, -1, 2):
        net.push(("vy", w), alongy.at[y], alongy.at[y], "y", w)
    yield
    for w in (1, -1, 2):
        net.arrived(("vy", w))
    out[0:2] = (alongy[0, 0:2] + alongy[1, 0:2]) + (alongy[2, 0:2] + alongy[3, 0:2])
    yield


PARTS = 6
TILES = 4
FARTHER = ((1, 1), (1, 2), (1, 3))


def back_kernel(
    od, dkv, inputs, upstream, hidden, up_w, down_t, kv_w, q_w, dense_t, b_up, b_out, gain, t_cos, t_low, t_high,
    block_out, input_grad, *refs,
):
    parts_out, (vec_out, sum0, sum1), refs = refs[:PARTS], refs[PARTS : PARTS + 3], refs[PARTS + 3 :]
    accs, refs = refs[:PARTS], refs[PARTS:]
    far1, near1, far2, near2, refs = *refs[:4], refs[4:]
    weights, pair, in_t, up_t, share, d_share, od_in, dkv_in, theirs, ours, refs = *refs[:10], refs[10:]
    y_far, y_near, vecs, vec_acc, pairs, alongx, alongz, alongy, send, recv, loc, free = refs
    net = Net(send, recv)
    net.greet(RING_XZ + RING_Y + FAR + FARTHER)
    me, c = net.chip, net.c
    tables = (t_cos, t_low, t_high)
    lane = lax.broadcasted_iota(jnp.int32, (128, 128), 1)
    left = lane < 64
    mine = pl.ds(pl.multiple_of(c * 384, 128), 384)

    net.push("s", dkv.at[:, :, 1 - c], theirs, "s", 1)
    own_dkv = pltpu.make_async_copy(dkv.at[:, :, c], ours, loc.at[0])
    own_dkv.start()
    stay = pltpu.make_async_copy(od.at[me], od_in.at[:, :, lanes(me)], loc.at[1])
    stay.start()

    def weight_copies(u):
        slot = weights.at[u % 2]
        low, high = slot.at[:, pl.ds(0, 512)], slot.at[:, pl.ds(512, 512)]
        if u < TILES:
            pieces = ((up_w.at[:, pl.ds(u * 512, 512)], low), (down_t.at[:, pl.ds(u * 512, 512)], high))
        elif u == TILES:
            pieces = ((kv_w, slot),)
        else:
            pieces = ((q_w, low), (dense_t, high))
        return [pltpu.make_async_copy(a, b, loc.at[4 + 2 * u + k]) for k, (a, b) in enumerate(pieces)]

    streams = [weight_copies(u) for u in range(PARTS)]
    for copy in streams[0]:
        copy.start()
    far = [(dz, dx) for dz in (1, 0) for dx in (2, 1, 3, 0) if dz or dx]
    for dz, dx in far:
        other = lax.rem(lax.rem(net.z, 2) + dz, 2) * 4 + wrap(net.x + dx)
        net.push(("o", dz, dx), od.at[other], od_in.at[:, :, lanes(me)], dz, dx)

    staged = accs[4]

    def transpose(t, carry):
        columns = pl.ds(pl.multiple_of(t * 128, 128), 128)
        for k, (src, dst) in enumerate(((inputs, in_t), (upstream, up_t))):
            tile = src[:, columns].T
            first, second = tile[:64], tile[64:]
            dst[pl.ds(pl.multiple_of(t * 64, 64), 64), mine] = jnp.where(c == 0, first, second)
            staged[t // 4, lax.rem(t, 4), :, 384 * k : 384 * k + 384] = jnp.where(c == 0, second, first)
        return carry

    lax.fori_loop(0, 16, transpose, 0)
    theirs_t = accs[5]
    net.push("t", staged.at[:, :, :, pl.ds(0, 768)], theirs_t.at[:, :, :, pl.ds(0, 768)], "s", 1)

    own_dkv.wait()
    net.arrived("s")
    ours[...] = ours[...] + theirs[...]
    for dz, dx in far:
        other = lax.rem(lax.rem(net.z, 2) + dz, 2) * 4 + wrap(net.x + dx)
        net.push(("k", dz, dx), ours.at[:, other], dkv_in.at[:, :, lanes(me)], dz, dx)
    last = pltpu.make_async_copy(ours.at[:, me], dkv_in.at[:, :, lanes(me)], loc.at[2])
    last.start()

    parts = [
        Scatter(net, ("g", i), accs[i], far1.at[i], near1.at[i], far2.at[i], near2.at[i], parts_out[i])
        for i in range(PARTS)
    ]
    share[...] = jnp.zeros_like(share)
    d_share[...] = jnp.zeros_like(d_share)
    vecs[...] = jnp.zeros_like(vecs)

    def gradients(u, slot, first_t, second_t):
        acc = accs[u]

        def rows(z, carry):
            span = pl.ds(pl.multiple_of(z * 256, 256), 256)
            for k, factor in enumerate((first_t, second_t)):
                columns = pl.ds(k * 512, 512)
                value = dot(factor[span], pair[slot, :, columns], ((1,), (0,)))
                acc[z, :, :, columns] = value.astype(BF).reshape(4, 64, 512)
            return carry

        lax.fori_loop(0, 4, rows, 0)

    def spread(total, value_columns, slot, weight_columns):
        value = pair[slot, mine, value_columns]

        def chunk(j, carry):
            columns = pl.ds(pl.multiple_of(j * 256, 256), 256)
            total[:, columns] += dot(value, weights[slot, columns, weight_columns], ((1,), (1,)))
            return carry

        lax.fori_loop(0, 8, chunk, 0)

    LOW, HIGH, ALL = pl.ds(0, 512), pl.ds(512, 512), pl.ds(0, 1024)

    def trade(u):
        slot = u % 2
        rows = pair.at[slot, mine]
        net.push(("p", u), rows, rows, "s", 1)

    def tile(u):
        slot = u % 2
        for copy in streams[u]:
            copy.wait()
        if u >= 1:
            net.sent(("p", u - 1))
        if u + 1 < PARTS:
            for copy in streams[u + 1]:
                copy.start()
        if u >= 2:
            pl.semaphore_wait(free.at[slot], 1)

        def units(j, carry):
            offset = pl.multiple_of(j * 256, 256)
            columns = pl.ds(offset, 256)
            bias = b_up[:, pl.ds(pl.multiple_of(u * 512 + j * 256, 256), 256)]
            v = dot(inputs[...], weights[slot, :, columns], ((1,), (0,))) + bias
            d = dot(upstream[...], weights[slot, :, pl.ds(pl.multiple_of(512 + j * 256, 256), 256)], ((1,), (0,)))
            k = 0.7978845608028654
            square = v * v
            t = jnp.tanh(k * v * (1.0 + 0.044715 * square))
            half = 0.5 * (1.0 + t)
            slope = half + 0.5 * v * (1.0 - t * t) * (k * (1.0 + 0.134145 * square))
            d_up = (d * slope).astype(BF)
            pair[slot, mine, columns] = d_up
            pair[slot, mine, pl.ds(pl.multiple_of(512 + j * 256, 256), 256)] = (v * half).astype(BF)
            vecs[3:4, pl.ds(pl.multiple_of(u * 512 + j * 256, 256), 256)] = jnp.sum(
                d_up.astype(F32), axis=0, keepdims=True
            )
            return carry

        lax.fori_loop(0, 2, units, 0)
        trade(u)
        spread(d_share, LOW, slot, LOW)
        spread(share, HIGH, slot, HIGH)
        if u == 0:
            net.arrived("t")

            def place_t(t, carry):
                rows = pl.ds(pl.multiple_of(t * 64, 64), 64)
                for k, dst in enumerate((in_t, up_t)):
                    dst[rows, pl.ds(pl.multiple_of((1 - c) * 384, 128), 384)] = theirs_t[
                        t // 4, lax.rem(t, 4), :, 384 * k : 384 * k + 384
                    ]
                return carry

            lax.fori_loop(0, 16, place_t, 0)
        net.arrived(("p", u))
        gradients(u, slot, in_t, up_t)
        if u + 2 < PARTS:
            pl.semaphore_signal(free.at[slot], inc=1, device_id=net.to("s", 1), device_id_type=MESH)

    def heads():
        stay.wait()
        last.wait()
        for dz, dx in far:
            net.arrived(("o", dz, dx))
            net.arrived(("k", dz, dx))
        net.sent("t")
        for copy in streams[TILES + 1]:
            copy.start()

        def rows_of(s, carry):
            rows = pl.ds(pl.multiple_of(s * 128, 128), 128)
            own = pl.ds(pl.multiple_of(c * 384 + s * 128, 128), 128)
            for h in range(8):
                columns = pl.ds(h * 128, 128)
                value = dkv_in[s, :, columns].astype(F32)
                pair[0, own, columns] = jnp.where(left, turn(value, tables, rows, -1.0), value).astype(BF)
            for h in range(4):
                a = od_in[s, :, 256 * h : 256 * h + 128].astype(F32)
                b = od_in[s, :, 256 * h + 128 : 256 * h + 256].astype(F32)
                asked = jnp.where(left, a, pltpu.roll(b, 64, 1))
                pair[1, own, pl.ds(h * 128, 128)] = turn(asked, tables, rows, -1.0).astype(BF)
                got = jnp.where(left, pltpu.roll(a, 64, 1), b)
                pair[1, own, pl.ds(512 + h * 128, 128)] = got.astype(BF)
            return carry

        net.sent(("p", TILES - 1))
        for slot in (0, 1):
            pl.semaphore_wait(free.at[slot], 1)
        lax.fori_loop(0, 3, rows_of, 0)
        trade(TILES)
        trade(TILES + 1)
        own = pair[0, mine].astype(F32)
        vecs[4:5, 0:1024] = jnp.sum(own, axis=0, keepdims=True)
        vecs[4:5, 1024:1536] = jnp.sum(pair[1, mine, LOW].astype(F32), axis=0, keepdims=True)
        for copy in streams[TILES]:
            copy.wait()
        spread(d_share, ALL, 0, ALL)
        net.arrived(("p", TILES))
        gradients(TILES, 0, in_t, in_t)

    def rest():
        for copy in streams[TILES + 1]:
            copy.wait()
        spread(d_share, LOW, 1, LOW)
        spread(share, HIGH, 1, HIGH)
        net.arrived(("p", TILES + 1))
        gradients(TILES + 1, 1, in_t, up_t)

    def normed(rows):
        value = hidden[rows].astype(F32)
        value = value - jnp.mean(value, axis=1, keepdims=True)
        inverse = lax.rsqrt(jnp.mean(value * value, axis=1, keepdims=True) + 1e-05)
        return value * inverse, inverse

    def vectors():
        vec_acc[...] = jnp.zeros_like(vec_acc)

        def chunk(t, carry):
            rows = pl.ds(pl.multiple_of(t * 16, 16), 16)
            standard, _ = normed(rows)
            value = d_share[rows]
            for k, item in enumerate((value * standard, value, upstream[rows].astype(F32))):
                vec_acc[k] += item[:8] + item[8:]
            return carry

        lax.fori_loop(0, 24, chunk, 0)
        for k in range(3):
            vecs[k : k + 1] = jnp.sum(vec_acc[k], axis=0, keepdims=True)

    def finish_out():
        def chunk(t, carry):
            rows = pl.ds(pl.multiple_of(t * 16, 16), 16)
            base = t // 6 * 192 + lax.rem(t, 6) * 16
            for half in (0, 1):
                columns = pl.ds(half * 1024, 1024)
                got = weights[1, pl.ds(pl.multiple_of(768 + base + 96 * half, 16), 16)].astype(F32)
                share[rows, columns] = hidden[rows, columns].astype(F32) + got + b_out[:, columns]
            return carry

        lax.fori_loop(0, 24, chunk, 0)

    def finish_in():
        def chunk(t, carry):
            rows = pl.ds(pl.multiple_of(t * 16, 16), 16)
            base = t // 6 * 192 + lax.rem(t, 6) * 16
            standard, inverse = normed(rows)
            got = [weights[1, pl.ds(pl.multiple_of(base + 96 * k, 16), 16)].astype(F32) for k in (0, 1)]
            scaled = jnp.concatenate(got, axis=1) * gain[...]
            mean = jnp.mean(scaled, axis=1, keepdims=True)
            along = jnp.mean(scaled * standard, axis=1, keepdims=True)
            d_share[rows] = upstream[rows].astype(F32) + inverse * (scaled - mean - standard * along)
            return carry

        lax.fori_loop(0, 24, chunk, 0)

    ys = [
        Sum(net, "yi", weights.at[0, pl.ds(0, 768)], y_far.at[0], y_near.at[0], sum0),
        Sum(net, "yo", weights.at[0, pl.ds(768, 768)], y_far.at[1], y_near.at[1], sum1),
    ]

    tile(0)
    parts[0].step2()
    tile(1)
    parts[0].step3()
    parts[1].step2()
    tile(2)
    parts[0].step4()
    parts[1].step3()
    parts[2].step2()
    tile(3)
    parts[0].step5()
    parts[1].step4()
    parts[2].step3()
    parts[3].step2()
    heads()
    parts[4].step2()
    rest()
    parts[5].step2()
    vectors()
    vec = vector_sum(net, vecs, pairs, alongx, alongz, alongy, vec_out)
    ys[0].step1(d_share)
    ys[1].step1(share)
    next(vec)
    parts[0].step6()
    parts[1].step5()
    parts[2].step4()
    parts[3].step3()
    ys[0].step2()
    next(vec)
    ys[1].step2()
    parts[1].step6()
    parts[2].step5()
    parts[3].step4()
    parts[4].step3()
    next(vec)
    ys[0].step3(loc.at[20])
    ys[1].step3(loc.at[21])
    parts[2].step6()
    parts[3].step5()
    parts[4].step4()
    parts[5].step3()
    next(vec)
    ys[0].step4()
    ys[1].step4()
    parts[3].step6()
    parts[4].step5()
    parts[5].step4()
    next(vec)
    got0 = ys[0].step5(weights.at[1, pl.ds(0, 768)].reshape(4, 192, 1024), loc.at[22])
    parts[4].step6()
    got0.wait()
    finish_in()
    out0 = pltpu.make_async_copy(d_share, input_grad, loc.at[24])
    out0.start()
    got1 = ys[1].step5(weights.at[1, pl.ds(768, 768)].reshape(4, 192, 1024), loc.at[23])
    parts[5].step5()
    got1.wait()
    finish_out()
    out1 = pltpu.make_async_copy(share, block_out, loc.at[25])
    out1.start()
    parts[5].step6()
    out0.wait()
    out1.wait()
    net.drain()


def backward(od, dkv, inputs, upstream, hidden, weights, b_up, b_out, gain, tables, cid):
    wide = jax.ShapeDtypeStruct((384, 2048), F32)
    outs = pl.pallas_call(
        back_kernel,
        out_shape=[wide, wide]
        + [jax.ShapeDtypeStruct((64, 1024), F32)] * PARTS
        + [jax.ShapeDtypeStruct((8, 2048), F32)]
        + [jax.ShapeDtypeStruct((4, 192, 1024), BF)] * 2,
        in_specs=[ANY] * 2 + [VMEM] * 3 + [ANY] * 5 + [VMEM] * 6,
        out_specs=[ANY] * 2 + [VMEM] * (PARTS + 1) + [ANY] * 2,
        scratch_shapes=[pltpu.VMEM((4, 4, 64, 1024), BF)] * PARTS
        + [
            pltpu.VMEM((PARTS, 2, 2, 4, 16, 1024), BF),
            pltpu.VMEM((PARTS, 2, 2, 4, 32, 1024), BF),
            pltpu.VMEM((PARTS, 2, 2, 16, 1024), BF),
            pltpu.VMEM((PARTS, 2, 2, 32, 1024), BF),
            pltpu.VMEM((2, 2048, 1024), BF),
            pltpu.VMEM((2, 768, 1024), BF),
            pltpu.VMEM((1024, 768), BF),
            pltpu.VMEM((1024, 768), BF),
            pltpu.VMEM((384, 2048), F32),
            pltpu.VMEM((384, 2048), F32),
            pltpu.VMEM((3, 128, 1024), BF),
            pltpu.VMEM((3, 128, 1024), BF),
            pltpu.VMEM((3, 8, 128, 128), BF),
            pltpu.VMEM((3, 8, 128, 128), BF),
            pltpu.VMEM((2, 2, 96, 1024), BF),
            pltpu.VMEM((2, 2, 192, 1024), BF),
            pltpu.VMEM((8, 2048), F32),
            pltpu.VMEM((3, 8, 2048), F32),
            pltpu.VMEM((2, 8, 2048), F32),
            pltpu.VMEM((4, 8, 2048), F32),
            pltpu.VMEM((4, 8, 2048), F32),
            pltpu.VMEM((4, 8, 2048), F32),
            pltpu.SemaphoreType.DMA((160,)),
            pltpu.SemaphoreType.DMA((160,)),
            pltpu.SemaphoreType.DMA((26,)),
            pltpu.SemaphoreType.REGULAR((2,)),
        ],
        compiler_params=pltpu.CompilerParams(
            collective_id=cid, has_side_effects=True, vmem_limit_bytes=63 * 2**20
        ),
        name="backward",
    )(od, dkv.reshape(3, 8, 2, 128, 128), inputs, upstream, hidden, *weights, b_up, b_out, gain, *tables)
    return outs[0], outs[1], outs[2 : 2 + PARTS], outs[2 + PARTS]


def mix(tensor, cosine, sine):
    half = ROT // 2
    first, second = tensor[..., :half], tensor[..., half:ROT]
    return jnp.concatenate(
        [first * cosine - second * sine, second * cosine + first * sine, tensor[..., ROT:]], axis=-1
    )


def dot(a, b, dims):
    return lax.dot_general(a, b, (dims, ((), ())), preferred_element_type=F32)


def local(
    hidden_in, segments, keep_mask, ln_gain, ln_shift, w_qkv, b_qkv, w_dense, b_dense, w_up, b_up, w_down, b_down,
    cotangent,
):
    rows, width = 384, 2048
    kv_shard = jnp.stack([w_qkv[:, 1].reshape(64, 8, HD), w_qkv[:, 2].reshape(64, 8, HD)], axis=2)
    kv_shard = kv_shard.reshape(64, 1024).astype(BF)
    q_shard = w_qkv[:, 0].astype(BF)
    dense_shard = w_dense.T.astype(BF)
    up_shard = w_up.astype(BF)
    down_shard = w_down.T.astype(BF)
    kv_w, q_w, dense_t = gather([kv_shard, q_shard, dense_shard], 0, "gather_heads")

    hidden = hidden_in.reshape(rows, width).astype(F32)
    upstream = cotangent.reshape(rows, width)
    centered = hidden - jnp.mean(hidden, axis=-1, keepdims=True)
    inverse = lax.rsqrt(jnp.mean(centered * centered, axis=-1, keepdims=True) + 1e-05)
    standard = centered * inverse
    inputs = (standard * ln_gain + ln_shift).astype(BF)

    positions = lax.axis_index("seq") * 128 + jnp.arange(128, dtype=jnp.int32)
    half = ROT // 2
    frequency = 10000.0 ** (-(jnp.arange(half, dtype=F32) * 2.0) / ROT)
    angles = positions.astype(F32)[:, None] * frequency[None, :]
    cosine = jnp.tile(jnp.cos(angles), (3, 1))[:, None, :]
    sine = jnp.tile(jnp.sin(angles), (3, 1))[:, None, :]

    b_kv = jnp.stack([b_qkv[1].reshape(8, HD), b_qkv[2].reshape(8, HD)], axis=1).reshape(1024)
    kv = (dot(inputs, kv_w, ((1,), (0,))) + b_kv).reshape(rows, 8, 128)
    kv = jnp.concatenate([mix(kv[..., :HD], cosine, sine), kv[..., HD:]], axis=-1).astype(BF)
    queries = (dot(inputs, q_w, ((1,), (0,))) + b_qkv[0]).reshape(rows, 8, HD)
    queries = mix(queries, cosine, sine).astype(BF)
    d_attended = dot(upstream, dense_t, ((1,), (0,))).astype(BF).reshape(rows, 8, HD)
    qd = jnp.concatenate([queries, d_attended], axis=-1).reshape(3, 128, 1024)
    kv = kv.reshape(3, 128, 1024)
    info = jnp.concatenate(
        [jnp.where(keep_mask > 0, segments, -1), segments, jnp.zeros((2, 128), jnp.int32)], axis=0
    )
    qd_all, kv_all, info_all = exchange(qd, kv, info, 1)
    up_shard, down_shard, qd_all = lax.optimization_barrier((up_shard, down_shard, qd_all))
    up_w, down_t = gather([up_shard, down_shard], 2, "gather_units")
    od_all, dkv_all = attend(qd_all, kv_all, info_all)
    quiet = jnp.zeros((HD - ROT,), F32)
    places = jnp.arange(128, dtype=jnp.int32) % HD
    turned = positions.astype(F32)[:, None] * jnp.concatenate([frequency, frequency, quiet] * 2)[None, :]
    t_cos = jnp.cos(turned)
    t_low = jnp.where(places < half, jnp.sin(turned), 0.0)
    t_high = jnp.where(places >= half, jnp.sin(turned), 0.0)
    tables = [jnp.tile(t, (3, 1)) for t in (t_cos, t_low, t_high)]
    block_out, input_grad, parts, vectors = backward(
        od_all,
        dkv_all,
        inputs,
        upstream,
        hidden_in.reshape(rows, width),
        (up_w, down_t, kv_w, q_w, dense_t),
        b_up[None],
        (b_dense + b_down)[None],
        ln_gain[None],
        tables,
        3,
    )
    grad_up = jnp.concatenate([p[:, :512] for p in parts[:TILES]], axis=1)
    grad_down = jnp.concatenate([p[:, 512:] for p in parts[:TILES]], axis=1)
    grad_q, grad_dense = parts[5][:, :512], parts[5][:, 512:]
    grad_kv = parts[4].reshape(64, 8, 2, HD)
    grad_qkv = jnp.stack([grad_q, grad_kv[:, :, 0].reshape(64, 512), grad_kv[:, :, 1].reshape(64, 512)], axis=1)
    bias_kv = vectors[4, :1024].reshape(8, 2, HD)
    grad_bqkv = jnp.stack([vectors[4, 1024:1536], bias_kv[:, 0].reshape(512), bias_kv[:, 1].reshape(512)])
    return (
        block_out.reshape(3, 128, width),
        input_grad.reshape(3, 128, width),
        vectors[0],
        vectors[1],
        grad_qkv,
        grad_bqkv,
        grad_dense.T,
        vectors[2],
        grad_up,
        vectors[3],
        grad_down.T,
        vectors[2],
    )


def solution(mesh):
    return jax.shard_map(
        local,
        mesh=mesh,
        in_specs=(
            P("dp", "seq", None),
            P("dp", "seq"),
            P("dp", "seq"),
            P(),
            P(),
            P(("dp", "seq"), None, "tp"),
            P(None, "tp"),
            P("tp", ("dp", "seq")),
            P(),
            P(("dp", "seq"), "tp"),
            P("tp"),
            P("tp", ("dp", "seq")),
            P(),
            P("dp", "seq", None),
        ),
        out_specs=(
            P("dp", "seq", None),
            P("dp", "seq", None),
            P(),
            P(),
            P(("dp", "seq"), None, "tp"),
            P(None, "tp"),
            P("tp", ("dp", "seq")),
            P(),
            P(("dp", "seq"), "tp"),
            P("tp"),
            P("tp", ("dp", "seq")),
            P(),
        ),
        check_vma=False,
    )
```

```python
import functools

import jax
import jax.numpy as jnp
from jax import lax
from jax.experimental import pallas as pl
from jax.experimental.pallas import tpu as pltpu
from jax.sharding import PartitionSpec as P

MESH = pl.DeviceIdType.MESH
HD = 64
ROT = 32
WINDOW = 1024
BF = jnp.bfloat16
F32 = jnp.float32
ANY = pl.BlockSpec(memory_space=pl.ANY)
VMEM = pl.BlockSpec(memory_space=pltpu.VMEM)


def wrap(v):
    return lax.rem(v + 4, 4)


def place():
    dp, sq, tp = lax.axis_index("dp"), lax.axis_index("seq"), lax.axis_index("tp")
    return dp * 2 + sq // 8, lax.rem(sq // 2, 4), lax.rem(sq, 2), tp


def device(z, x, c, y):
    z, x, y = wrap(z), wrap(x), wrap(y)
    return {"dp": z // 2, "seq": lax.rem(z, 2) * 8 + x * 2 + c, "tp": y}


class Net:
    def __init__(self, send, recv):
        self.send, self.recv, self.n, self.out, self.keys = send, recv, 0, {}, {}
        self.z, self.x, self.c, self.y = place()
        self.flip = 1 - 2 * lax.rem(self.z, 2)
        self.chip = lax.rem(self.z, 2) * 4 + self.x

    def to(self, axis, way):
        z, x, c, y = self.z, self.x, self.c, self.y
        if axis == "s":
            return device(z, x, 1 - c, y)
        if axis == "x":
            return device(z, x + way, c, y)
        if axis == "z":
            return device(z + way, x, c, y)
        if axis == "y":
            return device(z, x, c, y + way)
        return device(z + axis * self.flip, x + way, c, y)

    def greet(self, targets):
        bar = pltpu.get_barrier_semaphore()
        for axis, way in targets:
            pl.semaphore_signal(bar, inc=1, device_id=self.to(axis, way), device_id_type=MESH)
        pl.semaphore_wait(bar, len(targets))

    def chip_at(self, dz, dx):
        return lax.rem(lax.rem(self.z, 2) + dz, 2) * 4 + wrap(self.x + dx)

    def push(self, key, src, dst, axis, way):
        k = self.n
        self.n += 1
        copy = pltpu.make_async_remote_copy(
            src_ref=src,
            dst_ref=dst,
            send_sem=self.send.at[k],
            recv_sem=self.recv.at[k],
            device_id=self.to(axis, way),
            device_id_type=MESH,
        )
        copy.start()
        self.out[key] = copy
        self.keys[key] = copy

    def arrived(self, key):
        self.keys.pop(key).wait_recv()

    def sent(self, key):
        self.out.pop(key).wait_send()

    def drain(self):
        for key in list(self.out):
            self.sent(key)
        for key in list(self.keys):
            self.arrived(key)


def lanes(chip):
    return pl.ds(pl.multiple_of(chip * 128, 128), 128)


def dot(a, b, dims):
    return lax.dot_general(a, b, (dims, ((), ())), preferred_element_type=F32)


def span(start, size, unit=128):
    return pl.ds(pl.multiple_of(start, unit), size)


RING_XZ = (("x", 1), ("x", -1), ("z", 1), ("z", -1), ("s", 1))
RING_Y = (("y", 1), ("y", -1))
FAR = (("x", 2), ("z", 2), ("y", 2))
FARTHER = ((1, 1), (1, 2), (1, 3))
OTHERS = tuple((dz, dx) for dz in (1, 0) for dx in (2, 1, 3, 0) if dz or dx)
PARTS = 6
TILES = 4
LOW, HIGH, ALL = pl.ds(0, 512), pl.ds(512, 512), pl.ds(0, 1024)


class Gather:
    def __init__(self, net, name, src, dst):
        self.net, self.name, self.src, self.dst = net, name, src, dst
        self.half, self.quarter = src.shape[0] // 2, src.shape[0] // 4

    def at(self, h, a, b, r0, rn):
        n = self.net
        z, x = (n.z + b, n.x + a) if h == 0 else (n.z + a, n.x + b)
        return self.dst.at[wrap(z), wrap(x), n.c, pl.ds(h * self.half + r0, rn)]

    def own(self, h):
        return self.src.at[pl.ds(h * self.half, self.half)]

    def axes(self, h):
        return ("x", "z") if h == 0 else ("z", "x")

    def begin(self, sem):
        n = self.net
        for h in (0, 1):
            for w in (1, -1):
                n.push((self.name, h, "A", w), self.own(h), self.at(h, 0, 0, 0, self.half), self.axes(h)[0], w)
        for h in (0, 1):
            for w in (1, -1):
                n.push((self.name, h, "B", 0, w), self.own(h), self.at(h, 0, 0, 0, self.half), self.axes(h)[1], w)
        whole = self.dst.at[n.z, n.x, n.c]
        n.push((self.name, "s"), self.src, whole, "s", 1)
        self.local = pltpu.make_async_copy(self.src, whole, sem)
        self.local.start()

    def spread(self, h, a):
        n = self.net
        block = self.at(h, a, 0, 0, self.half)
        for w in (1, -1):
            n.push((self.name, h, "B", a, w), block, block, self.axes(h)[1], w)
        n.push((self.name, h, "s", a, 0), block, block, "s", 1)

    def near(self):
        n = self.net
        for h in (0, 1):
            for w in (1, -1):
                n.arrived((self.name, h, "A", w))
                part = self.at(h, -w, 0, 0 if w == 1 else self.quarter, self.quarter)
                n.push((self.name, h, "AF", w), part, part, self.axes(h)[0], w)
                self.spread(h, -w)

    def far(self):
        for h in (0, 1):
            for w in (1, -1):
                self.net.arrived((self.name, h, "AF", w))
            self.spread(h, 2)

    def pass_on(self, a):
        n = self.net
        for h in (0, 1):
            for w in (1, -1):
                n.arrived((self.name, h, "B", a, w))
                part = self.at(h, a, -w, 0 if w == 1 else self.quarter, self.quarter)
                n.push((self.name, h, "BF", a, w), part, part, self.axes(h)[1], w)
                block = self.at(h, a, -w, 0, self.half)
                n.push((self.name, h, "s", a, -w), block, block, "s", 1)

    def close(self, a):
        n = self.net
        for h in (0, 1):
            for w in (1, -1):
                n.arrived((self.name, h, "BF", a, w))
            block = self.at(h, a, 2, 0, self.half)
            n.push((self.name, h, "s", a, 2), block, block, "s", 1)


    def landed(self):
        n = self.net
        self.local.wait()
        n.arrived((self.name, "s"))
        for h in (0, 1):
            for a in (-1, 1, 2):
                n.arrived((self.name, h, "s", a, 0))
            for a in (0, -1, 1, 2):
                for b in (-1, 1, 2):
                    n.arrived((self.name, h, "s", a, b))


def turn(tensor, tables, sign):
    cosine, low, high = tables
    moved = pltpu.roll(tensor, 16, 1) * high[...] - pltpu.roll(tensor, 112, 1) * low[...]
    return tensor * cosine[...] + sign * moved


class Scatter:
    def __init__(self, net, name, acc, far1, near1, far2, near2, out):
        self.net, self.name, self.acc = net, name, acc
        self.far1, self.near1, self.far2, self.near2, self.out = far1, near1, far2, near2, out

    def axes(self, h):
        return ("z", "x") if h == 0 else ("x", "z")

    def first(self, h, d, r0, rn):
        n, rows = self.net, pl.ds(h * 32 + r0, rn)
        if h == 0:
            return self.acc.at[wrap(n.z + d), :, rows]
        return self.acc.at[:, wrap(n.x + d), rows]

    def second(self, h, d, r0, rn):
        n, rows = self.net, pl.ds(h * 32 + r0, rn)
        if h == 0:
            return self.acc.at[n.z, wrap(n.x + d), rows]
        return self.acc.at[wrap(n.z + d), n.x, rows]

    def step2(self):
        n = self.net
        for h in (0, 1):
            for k, w in ((0, -1), (1, 1)):
                n.push((self.name, h, "f1", w), self.first(h, 2, 16 * k, 16), self.far1.at[h, k], self.axes(h)[0], w)

    def step3(self):
        n = self.net
        for h in (0, 1):
            for k, w in ((0, -1), (1, 1)):
                n.arrived((self.name, h, "f1", w))
                part = self.first(h, w, 16 * k, 16)

                def add(t, carry):
                    part[t] = part[t] + self.far1[h, k, t]
                    return carry

                lax.fori_loop(0, 4, add, 0)
                n.push((self.name, h, "n1", w), self.first(h, w, 0, 32), self.near1.at[h, k], self.axes(h)[0], w)

    def step4(self):
        n = self.net
        for h in (0, 1):
            n.arrived((self.name, h, "n1", -1))
            n.arrived((self.name, h, "n1", 1))
            part = self.first(h, 0, 0, 32)

            def add(t, carry):
                for r in (0, 16):
                    rows = pl.ds(r, 16)
                    value = part[t, rows].astype(F32) + self.near1[h, 0, t, rows].astype(F32)
                    part[t, rows] = (value + self.near1[h, 1, t, rows].astype(F32)).astype(BF)
                return carry

            lax.fori_loop(0, 4, add, 0)
            for k, w in ((0, -1), (1, 1)):
                n.push((self.name, h, "f2", w), self.second(h, 2, 16 * k, 16), self.far2.at[h, k], self.axes(h)[1], w)

    def step5(self):
        n = self.net
        for h in (0, 1):
            for k, w in ((0, -1), (1, 1)):
                n.arrived((self.name, h, "f2", w))
                part = self.second(h, w, 16 * k, 16)
                part[...] = part[...] + self.far2[h, k]
                n.push((self.name, h, "n2", w), self.second(h, w, 0, 32), self.near2.at[h, k], self.axes(h)[1], w)

    def step6(self):
        n = self.net
        for h in (0, 1):
            n.arrived((self.name, h, "n2", -1))
            n.arrived((self.name, h, "n2", 1))
            part = self.second(h, 0, 0, 32)
            for r in (0, 16):
                rows = pl.ds(r, 16)
                value = part[rows].astype(F32) + self.near2[h, 0, rows].astype(F32)
                self.out[pl.ds(h * 32 + r, 16)] = value + self.near2[h, 1, rows].astype(F32)


class Sum:
    def __init__(self, net, name, acc, far, near, out):
        self.net, self.name, self.acc = net, name, acc
        self.far, self.near, self.out = far, near, out

    def block(self, d, r0, rn):
        start = pl.multiple_of(wrap(self.net.y + d) * 192 + r0, 16)
        return self.acc.at[pl.ds(start, rn)]

    def step1(self, value):
        n = self.net

        def fill(d, carry):
            for half in (0, 1):
                rows = pl.ds(pl.multiple_of(d * 192 + half * 96, 16), 96)
                held = value[pl.ds(pl.multiple_of(d * 96, 16), 96), pl.ds(half * 1024, 1024)]
                self.acc[rows] = held.astype(BF)
            return carry

        lax.fori_loop(0, 4, fill, 0)
        for k, w in ((0, -1), (1, 1)):
            n.push((self.name, "f", w), self.block(2, 96 * k, 96), self.far.at[k], "y", w)

    def step2(self):
        n = self.net
        for k, w in ((0, -1), (1, 1)):
            n.arrived((self.name, "f", w))
            part = self.block(w, 96 * k, 96)
            part[...] = part[...] + self.far[k]
            n.push((self.name, "n", w), self.block(w, 0, 192), self.near.at[k], "y", w)

    def step3(self, sem):
        n = self.net
        n.arrived((self.name, "n", -1))
        n.arrived((self.name, "n", 1))
        part = self.block(0, 0, 192)

        def add(t, carry):
            rows = pl.ds(pl.multiple_of(t * 16, 16), 16)
            value = part[rows].astype(F32) + self.near[0, rows].astype(F32)
            part[rows] = (value + self.near[1, rows].astype(F32)).astype(BF)
            return carry

        lax.fori_loop(0, 12, add, 0)
        for w in (-1, 1):
            n.push((self.name, "g", w), part, self.out.at[n.y], "y", w)
        self.last = pltpu.make_async_copy(part, self.out.at[n.y], sem)
        self.last.start()

    def step4(self):
        n = self.net
        for k, w in ((0, -1), (1, 1)):
            n.arrived((self.name, "g", w))
            part = self.out.at[wrap(n.y - w), pl.ds(96 * k, 96)]
            n.push((self.name, "gf", w), part, part, "y", w)

    def step5(self):
        self.last.wait()
        for w in (-1, 1):
            self.net.arrived((self.name, "gf", w))


def vector_sum(net, src, pairs, alongx, alongz, alongy, out):
    z, x, c, y = net.z, net.x, net.c, net.y
    pairs[c] = src[...]
    net.push("vs", pairs.at[c], pairs.at[c], "s", 1)
    yield
    net.arrived("vs")
    alongx[x] = pairs[0] + pairs[1]
    for w in (1, -1, 2):
        net.push(("vx", w), alongx.at[x], alongx.at[x], "x", w)
    yield
    for w in (1, -1, 2):
        net.arrived(("vx", w))
    alongz[z] = (alongx[0] + alongx[1]) + (alongx[2] + alongx[3])
    for w in (1, -1, 2):
        net.push(("vz", w), alongz.at[z], alongz.at[z], "z", w)
    yield
    for w in (1, -1, 2):
        net.arrived(("vz", w))
    alongy[y] = (alongz[0] + alongz[1]) + (alongz[2] + alongz[3])
    out[...] = alongy[y]
    for w in (1, -1, 2):
        net.push(("vy", w), alongy.at[y], alongy.at[y], "y", w)
    yield
    for w in (1, -1, 2):
        net.arrived(("vy", w))
    out[0:2] = (alongy[0, 0:2] + alongy[1, 0:2]) + (alongy[2, 0:2] + alongy[3, 0:2])
    yield


def halves(a, b, left):
    return jnp.where(left, a, pltpu.roll(b, 64, 1)), jnp.where(left, pltpu.roll(a, 64, 1), b)


def front_kernel(
    hidden, upstream, gain, shift, w_qkv, b_qkv, w_dense, w_up, b_up, w_down, info, t_cos, t_low, t_high, *refs
):
    gathered, refs = refs[:PARTS], refs[PARTS:]
    in_t, up_t, pairs, od_in, dkv_in, share, d_share, bias_up, refs = *refs[:8], refs[8:]
    shards, inputs, staged, kept, weights, qd, kv, qd_all, kv_all, info_all, seen, total, refs = *refs[:12], refs[12:]
    od, dkv, theirs, ours, pair, send, recv, loc = refs
    net = Net(send, recv)
    me, c = net.chip, net.c
    tables = (t_cos, t_low, t_high)
    lane = lax.broadcasted_iota(jnp.int32, (128, 128), 1)
    row = lax.broadcasted_iota(jnp.int32, (128, 128), 0)
    left = lane < 64
    mine = span(c * 384, 384)
    sems = iter(range(40))

    def here(src, dst):
        copy = pltpu.make_async_copy(src, dst, loc.at[next(sems)])
        copy.start()
        return copy

    for k in range(4):
        columns = pl.ds(k * 128, 128)
        pieces = halves(w_qkv[1, :, columns], w_qkv[2, :, columns], left[:64])
        for j in (0, 1):
            shards[0, :, pl.ds(256 * k + 128 * j, 128)] = pieces[j].astype(BF)
        shards[1, :, columns] = w_qkv[0, :, columns].astype(BF)
        shards[1, :, pl.ds(512 + 128 * k, 128)] = w_dense[:, columns].astype(BF)
    net.greet(RING_XZ + FARTHER + (("x", 2),))
    parts = [Gather(net, u, shards.at[u], gathered[u]) for u in range(PARTS)]
    parts[0].begin(loc.at[next(sems)])
    parts[1].begin(loc.at[next(sems)])
    for u in range(TILES):
        shards[2 + u, :, LOW] = w_up[:, pl.ds(u * 512, 512)].astype(BF)
        shards[2 + u, :, HIGH] = w_down[:, pl.ds(u * 512, 512)].astype(BF)

    def norm(t, carry):
        rows = span(t * 16, 16, 16)
        value = hidden[rows].astype(F32)
        value = value - jnp.mean(value, axis=1, keepdims=True)
        value = value * lax.rsqrt(jnp.mean(value * value, axis=1, keepdims=True) + 1e-05)
        inputs[rows] = (value * gain[...] + shift[...]).astype(BF)
        return carry

    lax.fori_loop(0, 24, norm, 0)

    def transpose(t, carry):
        columns, rows = span(t * 128, 128), span(t * 64, 64, 64)
        for k, src in enumerate((inputs, upstream)):
            tile = src[:, columns].T
            first, second = tile[:64], tile[64:]
            kept[k, rows] = jnp.where(c == 0, first, second)
            staged[k, rows] = jnp.where(c == 0, second, first)
        return carry

    lax.fori_loop(0, 16, transpose, 0)
    stays = []
    for k, dst in enumerate((in_t, up_t)):
        stays.append(here(kept.at[k], dst.at[c]))
        net.push(("t", k), staged.at[k], dst.at[c], "s", 1)

    def load(u):
        parts[u].landed()
        return here(gathered[u], weights.at[u % 4].reshape(4, 4, 2, 64, 1024))

    for u in (0, 1):
        parts[u].near()
    parts[2].begin(loc.at[next(sems)])
    for u in (0, 1):
        parts[u].far()
    for a in (0, -1, 1, 2):
        for u in (0, 1):
            parts[u].pass_on(a)
    for a in (0, -1, 1, 2):
        for u in (0, 1):
            parts[u].close(a)
    parts[2].near()
    parts[3].begin(loc.at[next(sems)])
    loads = {u: load(u) for u in (0, 1)}

    loads[0].wait()

    def keys_values(h, carry):
        columns = span(h * 256, 256)
        value = dot(inputs[...], weights[0, :, columns], ((1,), (0,)))
        bk, bv = b_qkv[1:2, span(h * 128, 128)], b_qkv[2:3, span(h * 128, 128)]
        bias = halves(bk, bv, left[:1])
        for j in (0, 1):
            tile = value[:, 128 * j : 128 * j + 128] + bias[j]
            for s in range(3):
                piece = tile[128 * s : 128 * s + 128]
                kv[s, :, span(h * 256 + 128 * j, 128)] = jnp.where(left, turn(piece, tables, 1.0), piece).astype(BF)
        return carry

    lax.fori_loop(0, 4, keys_values, 0)
    for dz, dx in OTHERS:
        other = net.chip_at(dz, dx)
        net.push(("k", dz, dx), kv.at[:, :, lanes(other)], kv_all.at[:, 2 * me + c], dz, dx)
        net.push(("i", dz, dx), info, info_all.at[2 * me + c], dz, dx)
    net.push("ks", kv.at[:, :, lanes(me)], kv_all.at[:, 2 * me + c], "s", 1)
    net.push("is", info, info_all.at[2 * me + c], "s", 1)
    stays.append(here(kv.at[:, :, lanes(me)], kv_all.at[:, 2 * me + c]))
    stays.append(here(info, info_all.at[2 * me + c]))
    loads[1].wait()

    def queries(h, carry):
        columns = span(h * 128, 128)
        q = dot(inputs[...], weights[1, :, columns], ((1,), (0,))) + b_qkv[0:1, columns]
        d = dot(upstream[...], weights[1, :, span(512 + h * 128, 128)], ((1,), (0,)))
        for s in range(3):
            pieces = halves(turn(q[128 * s : 128 * s + 128], tables, 1.0), d[128 * s : 128 * s + 128], left)
            for j in (0, 1):
                qd[s, :, span(h * 256 + 128 * j, 128)] = pieces[j].astype(BF)
        return carry

    lax.fori_loop(0, 4, queries, 0)
    for dz, dx in OTHERS:
        net.push(("q", dz, dx), qd.at[:, :, lanes(net.chip_at(dz, dx))], qd_all.at[me], dz, dx)
    stays.append(here(qd.at[:, :, lanes(me)], qd_all.at[me]))

    def units(u):
        slot = (2 + u) % 4
        loads[2 + u].wait()

        def some(j, carry):
            low, high = span(j * 256, 256), span(512 + j * 256, 256)
            unit = span(u * 512 + j * 256, 256)
            v = dot(inputs[...], weights[slot, :, low], ((1,), (0,))) + b_up[:, unit]
            d = dot(upstream[...], weights[slot, :, high], ((1,), (0,)))
            k = 0.7978845608028654
            square = v * v
            t = jnp.tanh(k * v * (1.0 + 0.044715 * square))
            half = 0.5 * (1.0 + t)
            slope = half + 0.5 * v * (1.0 - t * t) * (k * (1.0 + 0.134145 * square))
            d_up = (d * slope).astype(BF)
            pair[u, :, low] = d_up
            pair[u, :, high] = (v * half).astype(BF)
            bias_up[:, unit] = jnp.sum(d_up.astype(F32), axis=0, keepdims=True)
            return carry

        lax.fori_loop(0, 2, some, 0)
        net.push(("p", u), pair.at[u], pairs.at[u, mine], "s", 1)
        stays.append(here(pair.at[u], pairs.at[u, mine]))
        for total_ref, columns in ((d_share, LOW), (share, HIGH)):
            value = pair[u, :, columns]

            def spread(j, carry):
                rows = span(j * 512, 512)
                added = dot(value, weights[slot, rows, columns], ((1,), (1,)))
                if u == 0:
                    total_ref[:, rows] = added
                else:
                    total_ref[:, rows] += added
                return carry

            lax.fori_loop(0, 4, spread, 0)

    def attend(s, i, blocks, own, first):
        width = blocks * 128
        begin = first * 128 if isinstance(first, int) else pl.multiple_of(first * 128, 128)
        tile = qd_all[i, s].astype(F32)
        both_halves = [jnp.where(left, tile * (HD**-0.5), 0.0), jnp.where(left, 0.0, tile)]
        asking = jnp.concatenate(both_halves, axis=0).astype(BF)
        keys = kv_all[s, pl.ds(first, blocks)].reshape(width, 128)
        both = dot(asking, keys, ((1,), (1,)))
        asked = jnp.broadcast_to(info_all[own, pl.ds(3 + s, 1), :].astype(F32), (128, 128)).T
        held = seen[pl.ds(s, 1), pl.ds(begin, width)].astype(F32)
        pieces = []
        for b in range(blocks):
            fits = asked == held[:, b * 128 : (b + 1) * 128]
            if isinstance(first, int):
                if b >= blocks - 2:
                    ahead = lane + (b * 128 - own * 128) - row
                    fits = (fits | (ahead == 0)) & (ahead <= 0)
            elif b == blocks - 1:
                fits = (fits | (lane == row)) & (lane <= row)
            elif b == 0:
                fits = fits & (lane > row)
            pieces.append(jnp.where(fits, both[:128, b * 128 : (b + 1) * 128], -1e30))
        scores = jnp.concatenate(pieces, axis=1)
        expo = jnp.exp(scores - jnp.max(scores, axis=1, keepdims=True))
        probs = expo * (1.0 / jnp.sum(expo, axis=1, keepdims=True))
        d_probs = both[128:]
        delta = jnp.sum(probs * d_probs, axis=1, keepdims=True)
        mixed = jnp.concatenate([(probs * (d_probs - delta)).astype(BF), probs.astype(BF)], axis=0)
        back = dot(mixed, keys, ((1,), (0,)))
        od[i, s] = jnp.where(left, back[:128] * (HD**-0.5), back[128:]).astype(BF)
        total[pl.ds(begin, width)] += dot(mixed, asking, ((0,), (0,)))

    def sequence(s):
        total[...] = jnp.zeros_like(total)
        for i in range(4):
            attend(s, i, 2 * i + 2, 2 * i + c, 0)

        def late(i, carry):
            attend(s, i, 9, 2 * i + c, 2 * i + c - 8)
            return carry

        lax.fori_loop(4, 8, late, 0)
        dkv[s] = total[...].astype(BF).reshape(8, 2, 128, 128)

    parts[2].far()
    for a in (0, -1, 1, 2):
        parts[2].pass_on(a)
    parts[3].near()
    parts[4].begin(loc.at[next(sems)])
    for a in (0, -1, 1, 2):
        parts[2].close(a)
    for dz, dx in OTHERS:
        slot = 2 * net.chip_at(dz, -dx) + c
        net.arrived(("k", dz, dx))
        net.push(("ks", dz, dx), kv_all.at[:, slot], kv_all.at[:, slot], "s", 1)
        net.arrived(("i", dz, dx))
        net.push(("is", dz, dx), info_all.at[slot], info_all.at[slot], "s", 1)
    parts[3].far()
    loads[2] = load(2)
    for a in (0, -1, 1, 2):
        parts[3].pass_on(a)
    parts[4].near()
    parts[5].begin(loc.at[next(sems)])
    for dz, dx in OTHERS:
        for kind in ("q", "ks", "is"):
            net.arrived((kind, dz, dx))
    net.arrived("ks")
    net.arrived("is")
    for copy in stays:
        copy.wait()
    stays.clear()
    for b in range(16):
        seen[:, b * 128 : (b + 1) * 128] = info_all[b]
    sequence(0)
    for a in (0, -1, 1, 2):
        parts[3].close(a)
    parts[4].far()
    for a in (0, -1, 1):
        parts[4].pass_on(a)
    parts[5].near()
    parts[4].pass_on(2)
    sequence(1)
    parts[5].far()
    for a in (0, -1, 1, 2):
        parts[4].close(a)
    for a in (0, -1, 1):
        parts[5].pass_on(a)
    sequence(2)
    net.push("b", dkv.at[:, :, 1 - c], theirs, "s", 1)
    mixed = here(dkv.at[:, :, c], ours)
    stays.append(here(od.at[me], od_in.at[:, :, lanes(me)]))
    for dz, dx in OTHERS:
        net.push(("o", dz, dx), od.at[net.chip_at(dz, dx)], od_in.at[:, :, lanes(me)], dz, dx)
    mixed.wait()
    net.arrived("b")
    ours[...] = ours[...] + theirs[...]
    for dz, dx in OTHERS:
        net.push(("d", dz, dx), ours.at[:, net.chip_at(dz, dx)], dkv_in.at[:, :, lanes(me)], dz, dx)
    stays.append(here(ours.at[:, me], dkv_in.at[:, :, lanes(me)]))
    parts[5].pass_on(2)
    for a in (0, -1, 1, 2):
        parts[5].close(a)
    loads[3] = load(3)
    loads[4] = load(4)
    units(0)
    units(1)
    loads[5] = load(5)
    units(2)
    units(3)
    for copy in stays:
        copy.wait()
    net.drain()


def forward(args, cid):
    big = jax.ShapeDtypeStruct((4, 4, 2, 64, 1024), BF)
    factor = jax.ShapeDtypeStruct((2, 1024, 384), BF)
    heads = jax.ShapeDtypeStruct((3, 128, 1024), BF)
    wide = jax.ShapeDtypeStruct((384, 2048), F32)
    return pl.pallas_call(
        front_kernel,
        out_shape=[big] * PARTS
        + [factor, factor, jax.ShapeDtypeStruct((TILES, 768, 1024), BF), heads, heads]
        + [wide, wide, jax.ShapeDtypeStruct((1, 2048), F32)],
        in_specs=[VMEM] * len(args),
        out_specs=[ANY] * (PARTS + 5) + [VMEM] * 3,
        scratch_shapes=[
            pltpu.VMEM((PARTS, 64, 1024), BF),
            pltpu.VMEM((384, 2048), BF),
            pltpu.VMEM((2, 1024, 384), BF),
            pltpu.VMEM((2, 1024, 384), BF),
            pltpu.VMEM((4, 2048, 1024), BF),
            pltpu.VMEM((3, 128, 1024), BF),
            pltpu.VMEM((3, 128, 1024), BF),
            pltpu.VMEM((8, 3, 128, 128), BF),
            pltpu.VMEM((3, 16, 128, 128), BF),
            pltpu.VMEM((16, 8, 128), jnp.int32),
            pltpu.VMEM((8, 2048), jnp.int32),
            pltpu.VMEM((2048, 128), F32),
            pltpu.VMEM((8, 3, 128, 128), BF),
            pltpu.VMEM((3, 8, 2, 128, 128), BF),
            pltpu.VMEM((3, 8, 128, 128), BF),
            pltpu.VMEM((3, 8, 128, 128), BF),
            pltpu.VMEM((TILES, 384, 1024), BF),
            pltpu.SemaphoreType.DMA((540,)),
            pltpu.SemaphoreType.DMA((540,)),
            pltpu.SemaphoreType.DMA((40,)),
        ],
        compiler_params=pltpu.CompilerParams(
            collective_id=cid, has_side_effects=True, vmem_limit_bytes=62 * 2**20
        ),
        name="forward",
    )(*args)


def back_kernel(
    od_in, dkv_in, upstream, hidden, in_t, up_t, pairs, heads_w0, heads_w1, share_in, d_share_in, bias_up, gain, t_cos,
    t_low, t_high, input_grad, sum0, sum1, done, vec_out, *refs,
):
    accs, refs = refs[:PARTS], refs[PARTS:]
    far1, near1, far2, near2, refs = *refs[:4], refs[4:]
    weights, pair, factors, share, d_share, refs = *refs[:5], refs[5:]
    y_far, y_near, vecs, vec_acc, cores, alongx, alongz, alongy, send, recv, loc = refs
    net = Net(send, recv)
    c = net.c
    tables = (t_cos, t_low, t_high)
    left = lax.broadcasted_iota(jnp.int32, (128, 128), 1) < 64
    mine = span(c * 384, 384)
    sems = iter(range(40))

    def here(src, dst):
        copy = pltpu.make_async_copy(src, dst, loc.at[next(sems)])
        copy.start()
        return copy

    factor_loads = [here(src.at[k], factors.at[j, :, pl.ds(384 * k, 384)]) for j, src in enumerate((in_t, up_t)) for k in (0, 1)]
    pair_loads = {u: here(pairs.at[u], pair.at[u]) for u in (0, 1)}
    weight_loads = [here(src, weights.at[k]) for k, src in enumerate((heads_w0, heads_w1))]
    share_loads = [here(d_share_in, d_share), here(share_in, share)]
    net.greet(RING_XZ + RING_Y + FAR)
    parts = [
        Scatter(net, ("g", i), accs[i], far1.at[i], near1.at[i], far2.at[i], near2.at[i], done.at[i])
        for i in range(PARTS)
    ]

    def rows_of(s, carry):
        own = span(c * 384 + s * 128, 128)
        for h in range(8):
            columns = pl.ds(h * 128, 128)
            value = dkv_in[s, :, columns].astype(F32)
            pair[2, own, columns] = jnp.where(left, turn(value, tables, -1.0), value).astype(BF)
        for h in range(4):
            a = od_in[s, :, 256 * h : 256 * h + 128].astype(F32)
            b = od_in[s, :, 256 * h + 128 : 256 * h + 256].astype(F32)
            asked, got = halves(a, b, left)
            pair[3, own, pl.ds(h * 128, 128)] = turn(asked, tables, -1.0).astype(BF)
            pair[3, own, pl.ds(512 + h * 128, 128)] = got.astype(BF)
        return carry

    lax.fori_loop(0, 3, rows_of, 0)
    for slot in (2, 3):
        rows = pair.at[slot, mine]
        net.push(("p", slot), rows, rows, "s", 1)

    def gradients(u, slot, first_t, second_t):
        acc = accs[u]

        def some(z, carry):
            rows = span(z * 256, 256)
            for k, j in enumerate((first_t, second_t)):
                columns = pl.ds(k * 512, 512)
                value = dot(factors[j, rows], pair[slot, :, columns], ((1,), (0,)))
                acc[z, :, :, columns] = value.astype(BF).reshape(4, 64, 512)
            return carry

        lax.fori_loop(0, 4, some, 0)
        parts[u].step2()

    def tile(u):
        pair_loads[u].wait()
        gradients(u, u % 2, 0, 1)
        if u + 2 < TILES:
            pair_loads[u + 2] = here(pairs.at[u + 2], pair.at[u % 2])

    def spread(total, slot, columns):
        value = pair[slot, mine, columns]

        def chunk(j, carry):
            rows = span(j * 512, 512)
            total[:, rows] += dot(value, weights[slot - 2, rows, columns], ((1,), (1,)))
            return carry

        lax.fori_loop(0, 4, chunk, 0)

    def normed(rows):
        value = hidden[rows].astype(F32)
        value = value - jnp.mean(value, axis=1, keepdims=True)
        inverse = lax.rsqrt(jnp.mean(value * value, axis=1, keepdims=True) + 1e-05)
        return value * inverse, inverse

    def vectors():
        vec_acc[...] = jnp.zeros_like(vec_acc)
        vecs[...] = jnp.zeros_like(vecs)

        def chunk(t, carry):
            rows = span(t * 16, 16, 16)
            standard, _ = normed(rows)
            value = d_share[rows]
            for k, item in enumerate((value * standard, value, upstream[rows].astype(F32))):
                vec_acc[k] += item[:8] + item[8:]
            return carry

        lax.fori_loop(0, 24, chunk, 0)
        for k in range(3):
            vecs[k : k + 1] = jnp.sum(vec_acc[k], axis=0, keepdims=True)
        vecs[3:4] = bias_up[...]
        for k in range(4):
            columns = pl.ds(k * 256, 256)
            vecs[4:5, columns] = jnp.sum(pair[2, mine, columns].astype(F32), axis=0, keepdims=True)
        vecs[4:5, 1024:1536] = jnp.sum(pair[3, mine, LOW].astype(F32), axis=0, keepdims=True)

    def finish_in():
        def chunk(t, carry):
            rows = span(t * 16, 16, 16)
            base = t // 6 * 192 + lax.rem(t, 6) * 16
            standard, inverse = normed(rows)
            got = [weights[1, span(base + 96 * k, 16, 16)].astype(F32) for k in (0, 1)]
            scaled = jnp.concatenate(got, axis=1) * gain[...]
            mean = jnp.mean(scaled, axis=1, keepdims=True)
            along = jnp.mean(scaled * standard, axis=1, keepdims=True)
            d_share[rows] = upstream[rows].astype(F32) + inverse * (scaled - mean - standard * along)
            return carry

        lax.fori_loop(0, 24, chunk, 0)

    ys = [
        Sum(net, "yi", weights.at[0, pl.ds(0, 768)], y_far.at[0], y_near.at[0], sum0),
        Sum(net, "yo", weights.at[0, pl.ds(768, 768)], y_far.at[1], y_near.at[1], sum1),
    ]
    for copy in factor_loads:
        copy.wait()
    tile(0)
    tile(1)
    for copy in weight_loads + share_loads:
        copy.wait()
    spread(d_share, 2, ALL)
    spread(d_share, 3, LOW)
    ys[0].step1(d_share)
    spread(share, 3, HIGH)
    ys[1].step1(share)
    parts[0].step3()
    for slot in (2, 3):
        net.arrived(("p", slot))
    gradients(4, 2, 0, 0)
    ys[0].step2()
    parts[1].step3()
    gradients(5, 3, 0, 1)
    ys[1].step2()
    vectors()
    vec = vector_sum(net, vecs, cores, alongx, alongz, alongy, vec_out)
    next(vec)
    parts[0].step4()
    ys[0].step3(loc.at[next(sems)])
    tile(2)
    parts[4].step3()
    parts[1].step4()
    next(vec)
    ys[1].step3(loc.at[next(sems)])
    tile(3)
    parts[0].step5()
    parts[5].step3()
    ys[0].step4()
    parts[4].step4()
    next(vec)
    parts[1].step5()
    parts[0].step6()
    parts[2].step3()
    ys[1].step4()
    parts[5].step4()
    next(vec)
    parts[4].step5()
    parts[1].step6()
    parts[3].step3()
    ys[0].step5()
    got0 = here(sum0, weights.at[1, pl.ds(0, 768)].reshape(4, 192, 1024))
    parts[2].step4()
    next(vec)
    parts[5].step5()
    parts[4].step6()
    got0.wait()
    finish_in()
    out0 = here(d_share, input_grad)
    parts[3].step4()
    parts[2].step5()
    parts[5].step6()
    ys[1].step5()
    parts[3].step5()
    parts[2].step6()
    parts[3].step6()
    out0.wait()
    net.drain()


def backward(args, cid):
    wide = jax.ShapeDtypeStruct((384, 2048), F32)
    return pl.pallas_call(
        back_kernel,
        out_shape=[wide]
        + [jax.ShapeDtypeStruct((4, 192, 1024), BF)] * 2
        + [jax.ShapeDtypeStruct((PARTS, 64, 1024), F32), jax.ShapeDtypeStruct((8, 2048), F32)],
        in_specs=[VMEM] * 4 + [ANY] * 7 + [VMEM] * 5,
        out_specs=[ANY] * 3 + [VMEM] * 2,
        scratch_shapes=[pltpu.VMEM((4, 4, 64, 1024), BF)] * PARTS
        + [
            pltpu.VMEM((PARTS, 2, 2, 4, 16, 1024), BF),
            pltpu.VMEM((PARTS, 2, 2, 4, 32, 1024), BF),
            pltpu.VMEM((PARTS, 2, 2, 16, 1024), BF),
            pltpu.VMEM((PARTS, 2, 2, 32, 1024), BF),
            pltpu.VMEM((2, 2048, 1024), BF),
            pltpu.VMEM((4, 768, 1024), BF),
            pltpu.VMEM((2, 1024, 768), BF),
            pltpu.VMEM((384, 2048), F32),
            pltpu.VMEM((384, 2048), F32),
            pltpu.VMEM((2, 2, 96, 1024), BF),
            pltpu.VMEM((2, 2, 192, 1024), BF),
            pltpu.VMEM((8, 2048), F32),
            pltpu.VMEM((3, 8, 2048), F32),
            pltpu.VMEM((2, 8, 2048), F32),
            pltpu.VMEM((4, 8, 2048), F32),
            pltpu.VMEM((4, 8, 2048), F32),
            pltpu.VMEM((4, 8, 2048), F32),
            pltpu.SemaphoreType.DMA((140,)),
            pltpu.SemaphoreType.DMA((140,)),
            pltpu.SemaphoreType.DMA((40,)),
        ],
        compiler_params=pltpu.CompilerParams(
            collective_id=cid, has_side_effects=True, vmem_limit_bytes=63 * 2**20
        ),
        name="backward",
    )(*args)


def finish_kernel(
    hidden, summed, b_dense, b_down, grad, done, vecs, block_out, input_grad, g_qkv, g_dense, g_up, g_down, v_gain,
    v_shift, v_out, v_up, v_qkv, v_out2,
):
    for half in (0, 1):
        columns = pl.ds(half * 1024, 1024)
        bias = b_dense[:, columns] + b_down[:, columns]
        got = summed[0, pl.ds(96 * half, 96)].astype(F32)
        block_out[:, columns] = hidden[:, columns].astype(F32) + got + bias
    input_grad[...] = grad[...]

    @pl.when(pl.program_id(0) == 0)
    def _():
        left = lax.broadcasted_iota(jnp.int32, (64, 128), 1) < 64
        for u in range(TILES):
            g_up[:, pl.ds(u * 512, 512)] = done[u, :, :512]
            g_down[:, pl.ds(u * 512, 512)] = done[u, :, 512:]
        g_qkv[0] = done[5, :, :512]
        g_dense[...] = done[5, :, 512:]
        v_qkv[0:1] = vecs[4:5, 1024:1536]
        for k in range(4):
            a, b = pl.ds(256 * k, 128), pl.ds(256 * k + 128, 128)
            pieces = halves(done[4, :, a], done[4, :, b], left)
            rows = halves(vecs[4:5, a], vecs[4:5, b], left[:1])
            for j in (0, 1):
                g_qkv[1 + j, :, pl.ds(k * 128, 128)] = pieces[j]
                v_qkv[1 + j : 2 + j, pl.ds(k * 128, 128)] = rows[j]
        for k, dst in ((0, v_gain), (1, v_shift), (2, v_out), (2, v_out2), (3, v_up)):
            dst[...] = vecs[k]


def finish(hidden, summed, b_dense, b_down, grad, done, vecs):
    wide, row = jax.ShapeDtypeStruct((384, 2048), F32), jax.ShapeDtypeStruct((2048,), F32)
    rows = pl.BlockSpec((96, 2048), lambda i: (i, 0))
    small = [
        jax.ShapeDtypeStruct((3, 64, 512), F32),
        jax.ShapeDtypeStruct((64, 512), F32),
        jax.ShapeDtypeStruct((64, 2048), F32),
        jax.ShapeDtypeStruct((64, 2048), F32),
        row,
        row,
        row,
        row,
        jax.ShapeDtypeStruct((3, 512), F32),
        row,
    ]

    def whole(shape):
        return pl.BlockSpec(shape, lambda i: (0,) * len(shape))

    return pl.pallas_call(
        finish_kernel,
        grid=(4,),
        out_shape=[wide, wide] + small,
        in_specs=[rows, pl.BlockSpec((1, 192, 1024), lambda i: (i, 0, 0)), whole((1, 2048)), whole((1, 2048)), rows]
        + [whole((PARTS, 64, 1024)), whole((8, 2048))],
        out_specs=[rows, rows] + [whole(s.shape) for s in small],
        compiler_params=pltpu.CompilerParams(vmem_limit_bytes=62 * 2**20),
        name="finish",
    )(hidden, summed, b_dense, b_down, grad, done, vecs)


def local(
    hidden_in, segments, keep_mask, ln_gain, ln_shift, w_qkv, b_qkv, w_dense, b_dense, w_up, b_up, w_down, b_down,
    cotangent,
):
    rows, width = 384, 2048
    positions = lax.axis_index("seq") * 128 + jnp.arange(128, dtype=jnp.int32)
    half = ROT // 2
    frequency = 10000.0 ** (-(jnp.arange(half, dtype=F32) * 2.0) / ROT)
    quiet = jnp.zeros((HD - ROT,), F32)
    places = jnp.arange(128, dtype=jnp.int32) % HD
    turned = positions.astype(F32)[:, None] * jnp.concatenate([frequency, frequency, quiet] * 2)[None, :]
    t_cos = jnp.cos(turned)
    t_low = jnp.where(places < half, jnp.sin(turned), 0.0)
    t_high = jnp.where(places >= half, jnp.sin(turned), 0.0)
    tables = [t_cos, t_low, t_high]
    info = jnp.concatenate(
        [jnp.where(keep_mask > 0, segments, -1), segments, jnp.zeros((2, 128), jnp.int32)], axis=0
    )
    hidden = hidden_in.reshape(rows, width)
    upstream = cotangent.reshape(rows, width)
    outs = forward(
        [hidden, upstream, ln_gain[None], ln_shift[None], w_qkv.transpose(1, 0, 2), b_qkv, w_dense.T, w_up]
        + [b_up[None], w_down.T, info, *tables],
        0,
    )
    heads_w = [w.reshape(2048, 1024) for w in outs[:2]]
    in_t, up_t, pairs, od_in, dkv_in, share, d_share, bias_up = outs[PARTS:]
    input_grad, _, summed, done, vectors = backward(
        [od_in, dkv_in, upstream, hidden, in_t, up_t, pairs, *heads_w, share, d_share, bias_up, ln_gain[None], *tables], 1
    )
    block_out, input_grad, grad_qkv, grad_dense, grad_up, grad_down, gain, shift, out, up, grad_bqkv, out2 = finish(
        hidden, summed, b_dense[None], b_down[None], input_grad, done, vectors
    )
    return (
        block_out.reshape(3, 128, width),
        input_grad.reshape(3, 128, width),
        gain,
        shift,
        grad_qkv.transpose(1, 0, 2),
        grad_bqkv,
        grad_dense.T,
        out,
        grad_up,
        up,
        grad_down.T,
        out2,
    )


def solution(mesh):
    return jax.shard_map(
        local,
        mesh=mesh,
        in_specs=(
            P("dp", "seq", None),
            P("dp", "seq"),
            P("dp", "seq"),
            P(),
            P(),
            P(("dp", "seq"), None, "tp"),
            P(None, "tp"),
            P("tp", ("dp", "seq")),
            P(),
            P(("dp", "seq"), "tp"),
            P("tp"),
            P("tp", ("dp", "seq")),
            P(),
            P("dp", "seq", None),
        ),
        out_specs=(
            P("dp", "seq", None),
            P("dp", "seq", None),
            P(),
            P(),
            P(("dp", "seq"), None, "tp"),
            P(None, "tp"),
            P("tp", ("dp", "seq")),
            P(),
            P(("dp", "seq"), "tp"),
            P("tp"),
            P("tp", ("dp", "seq")),
            P(),
        ),
        check_vma=False,
    )
```

```python
import functools

import jax
import jax.numpy as jnp
import numpy as np
from jax import lax
from jax.experimental import pallas as pl
from jax.experimental.pallas import tpu as pltpu
from jax.sharding import PartitionSpec as P

MESH = pl.DeviceIdType.MESH
HD = 64
ROT = 32
WINDOW = 1024
BF = jnp.bfloat16
F32 = jnp.float32
ANY = pl.BlockSpec(memory_space=pl.ANY)
VMEM = pl.BlockSpec(memory_space=pltpu.VMEM)


def wrap(v):
    return lax.rem(v + 4, 4)


def place():
    dp, sq, tp = lax.axis_index("dp"), lax.axis_index("seq"), lax.axis_index("tp")
    return dp * 2 + sq // 8, lax.rem(sq // 2, 4), lax.rem(sq, 2), tp


def device(z, x, c, y):
    z, x, y = wrap(z), wrap(x), wrap(y)
    return {"dp": z // 2, "seq": lax.rem(z, 2) * 8 + x * 2 + c, "tp": y}


class Net:
    def __init__(self, send, recv):
        self.send, self.recv, self.n, self.out, self.keys = send, recv, 0, {}, {}
        self.z, self.x, self.c, self.y = place()
        self.flip = 1 - 2 * lax.rem(self.z, 2)
        self.chip = lax.rem(self.z, 2) * 4 + self.x

    def to(self, axis, way):
        z, x, c, y = self.z, self.x, self.c, self.y
        if axis == "s":
            return device(z, x, 1 - c, y)
        if axis == "x":
            return device(z, x + way, c, y)
        if axis == "z":
            return device(z + way, x, c, y)
        if axis == "y":
            return device(z, x, c, y + way)
        return device(z + axis * self.flip, x + way, c, y)

    def greet(self, targets):
        bar = pltpu.get_barrier_semaphore()
        for axis, way in targets:
            pl.semaphore_signal(bar, inc=1, device_id=self.to(axis, way), device_id_type=MESH)
        pl.semaphore_wait(bar, len(targets))

    def chip_at(self, dz, dx):
        return lax.rem(lax.rem(self.z, 2) + dz, 2) * 4 + wrap(self.x + dx)

    def push(self, key, src, dst, axis, way):
        k = self.n
        self.n += 1
        copy = pltpu.make_async_remote_copy(
            src_ref=src,
            dst_ref=dst,
            send_sem=self.send.at[k],
            recv_sem=self.recv.at[k],
            device_id=self.to(axis, way),
            device_id_type=MESH,
        )
        copy.start()
        self.out[key] = copy
        self.keys[key] = copy

    def arrived(self, key):
        self.keys.pop(key).wait_recv()

    def sent(self, key):
        self.out.pop(key).wait_send()

    def drain(self):
        for key in list(self.out):
            self.sent(key)
        for key in list(self.keys):
            self.arrived(key)


def lanes(chip):
    return pl.ds(pl.multiple_of(chip * 128, 128), 128)


def dot(a, b, dims):
    return lax.dot_general(a, b, (dims, ((), ())), preferred_element_type=F32)


def span(start, size, unit=128):
    return pl.ds(pl.multiple_of(start, unit), size)


RING_XZ = (("x", 1), ("x", -1), ("z", 1), ("z", -1), ("s", 1))
RING_Y = (("y", 1), ("y", -1))
FAR = (("x", 2), ("z", 2), ("y", 2))
FARTHER = ((1, 1), (1, 2), (1, 3))
OTHERS = tuple((dz, dx) for dz in (1, 0) for dx in (2, 1, 3, 0) if dz or dx)
PARTS = 6
TILES = 4
LOW, HIGH, ALL = pl.ds(0, 512), pl.ds(512, 512), pl.ds(0, 1024)


class Gather:
    def __init__(self, net, name, src, dst):
        self.net, self.name, self.src, self.dst = net, name, src, dst
        self.half, self.quarter = src.shape[0] // 2, src.shape[0] // 4

    def axes(self, h):
        return ("x", "z") if h == 0 else ("z", "x")

    def block(self, h, a, r0, rn):
        n, rows = self.net, pl.ds(h * self.half + r0, rn)
        if h == 0:
            return self.dst.at[n.z, wrap(n.x + a), n.c, rows]
        return self.dst.at[wrap(n.z + a), n.x, n.c, rows]

    def line(self, h, b, r0, rn):
        n, rows = self.net, pl.ds(h * self.half + r0, rn)
        if h == 0:
            return self.dst.at[wrap(n.z + b), :, n.c, rows]
        return self.dst.at[:, wrap(n.x + b), n.c, rows]

    def begin(self, sem):
        n = self.net
        for h in (0, 1):
            own = self.src.at[pl.ds(h * self.half, self.half)]
            for w in (1, -1):
                n.push((self.name, h, "A", w), own, self.block(h, 0, 0, self.half), self.axes(h)[0], w)
        self.local = pltpu.make_async_copy(self.src, self.dst.at[n.z, n.x, n.c], sem)
        self.local.start()

    def near(self):
        n = self.net
        for h in (0, 1):
            for w in (1, -1):
                n.arrived((self.name, h, "A", w))
                part = self.block(h, -w, 0 if w == 1 else self.quarter, self.quarter)
                n.push((self.name, h, "AF", w), part, part, self.axes(h)[0], w)

    def far(self):
        n = self.net
        self.local.wait()
        for h in (0, 1):
            for w in (1, -1):
                n.arrived((self.name, h, "AF", w))
            line = self.line(h, 0, 0, self.half)
            for w in (1, -1):
                n.push((self.name, h, "B", w), line, line, self.axes(h)[1], w)
            n.push((self.name, h, "s", 0), line, line, "s", 1)

    def pass_on(self):
        n = self.net
        for h in (0, 1):
            for w in (1, -1):
                n.arrived((self.name, h, "B", w))
                part = self.line(h, -w, 0 if w == 1 else self.quarter, self.quarter)
                n.push((self.name, h, "BF", w), part, part, self.axes(h)[1], w)
                line = self.line(h, -w, 0, self.half)
                n.push((self.name, h, "s", -w), line, line, "s", 1)

    def close(self):
        n = self.net
        for h in (0, 1):
            for w in (1, -1):
                n.arrived((self.name, h, "BF", w))
            line = self.line(h, 2, 0, self.half)
            n.push((self.name, h, "s", 2), line, line, "s", 1)

    def landed(self):
        for h in (0, 1):
            for b in (0, -1, 1, 2):
                self.net.arrived((self.name, h, "s", b))


class FineGather:
    def __init__(self, net, name, src, dst):
        self.net, self.name, self.src, self.dst = net, name, src, dst
        self.half, self.quarter = src.shape[0] // 2, src.shape[0] // 4

    def at(self, h, a, b, r0, rn):
        n = self.net
        z, x = (n.z + b, n.x + a) if h == 0 else (n.z + a, n.x + b)
        return self.dst.at[wrap(z), wrap(x), n.c, pl.ds(h * self.half + r0, rn)]

    def own(self, h):
        return self.src.at[pl.ds(h * self.half, self.half)]

    def axes(self, h):
        return ("x", "z") if h == 0 else ("z", "x")

    def begin(self, sem):
        n = self.net
        for h in (0, 1):
            for w in (1, -1):
                n.push((self.name, h, "A", w), self.own(h), self.at(h, 0, 0, 0, self.half), self.axes(h)[0], w)
        for h in (0, 1):
            for w in (1, -1):
                n.push((self.name, h, "B", 0, w), self.own(h), self.at(h, 0, 0, 0, self.half), self.axes(h)[1], w)
        whole = self.dst.at[n.z, n.x, n.c]
        n.push((self.name, "s"), self.src, whole, "s", 1)
        self.local = pltpu.make_async_copy(self.src, whole, sem)
        self.local.start()

    def spread(self, h, a):
        n = self.net
        block = self.at(h, a, 0, 0, self.half)
        for w in (1, -1):
            n.push((self.name, h, "B", a, w), block, block, self.axes(h)[1], w)
        n.push((self.name, h, "s", a, 0), block, block, "s", 1)

    def near(self):
        n = self.net
        for h in (0, 1):
            for w in (1, -1):
                n.arrived((self.name, h, "A", w))
                part = self.at(h, -w, 0, 0 if w == 1 else self.quarter, self.quarter)
                n.push((self.name, h, "AF", w), part, part, self.axes(h)[0], w)
                self.spread(h, -w)

    def far(self):
        for h in (0, 1):
            for w in (1, -1):
                self.net.arrived((self.name, h, "AF", w))
            self.spread(h, 2)

    def pass_on(self, a):
        n = self.net
        for h in (0, 1):
            for w in (1, -1):
                n.arrived((self.name, h, "B", a, w))
                part = self.at(h, a, -w, 0 if w == 1 else self.quarter, self.quarter)
                n.push((self.name, h, "BF", a, w), part, part, self.axes(h)[1], w)
                block = self.at(h, a, -w, 0, self.half)
                n.push((self.name, h, "s", a, -w), block, block, "s", 1)

    def close(self, a):
        n = self.net
        for h in (0, 1):
            for w in (1, -1):
                n.arrived((self.name, h, "BF", a, w))
            block = self.at(h, a, 2, 0, self.half)
            n.push((self.name, h, "s", a, 2), block, block, "s", 1)

    def landed(self):
        n = self.net
        self.local.wait()
        n.arrived((self.name, "s"))
        for h in (0, 1):
            for a in (-1, 1, 2):
                n.arrived((self.name, h, "s", a, 0))
            for a in (0, -1, 1, 2):
                for b in (-1, 1, 2):
                    n.arrived((self.name, h, "s", a, b))


def fill_tables(tables, near_cos, near_sin, base_cos, base_sin):
    own = pl.ds(lax.axis_index("seq"), 1)
    cosine, sine = base_cos[own], base_sin[own]
    place_in = lax.rem(lax.broadcasted_iota(jnp.int32, (128, 128), 1), HD)
    tables[0][...] = near_cos[...] * cosine - near_sin[...] * sine
    total = near_sin[...] * cosine + near_cos[...] * sine
    tables[1][...] = jnp.where(place_in < ROT // 2, total, 0.0)
    tables[2][...] = jnp.where(place_in < ROT // 2, 0.0, total)


def turn(tensor, tables, sign):
    cosine, low, high = tables
    moved = pltpu.roll(tensor, 16, 1) * high[...] - pltpu.roll(tensor, 112, 1) * low[...]
    return tensor * cosine[...] + sign * moved


class Scatter:
    def __init__(self, net, name, acc, far1, near1, far2, near2, out):
        self.net, self.name, self.acc = net, name, acc
        self.far1, self.near1, self.far2, self.near2, self.out = far1, near1, far2, near2, out

    def axes(self, h):
        return ("z", "x") if h == 0 else ("x", "z")

    def first(self, h, d, r0, rn):
        n, rows = self.net, pl.ds(h * 32 + r0, rn)
        if h == 0:
            return self.acc.at[wrap(n.z + d), :, rows]
        return self.acc.at[:, wrap(n.x + d), rows]

    def second(self, h, d, r0, rn):
        n, rows = self.net, pl.ds(h * 32 + r0, rn)
        if h == 0:
            return self.acc.at[n.z, wrap(n.x + d), rows]
        return self.acc.at[wrap(n.z + d), n.x, rows]

    def step2(self):
        n = self.net
        for h in (0, 1):
            for k, w in ((0, -1), (1, 1)):
                n.push((self.name, h, "f1", w), self.first(h, 2, 16 * k, 16), self.far1.at[h, k], self.axes(h)[0], w)

    def step3(self):
        n = self.net
        for h in (0, 1):
            for k, w in ((0, -1), (1, 1)):
                n.arrived((self.name, h, "f1", w))
                part = self.first(h, w, 16 * k, 16)

                def add(t, carry):
                    part[t] = part[t] + self.far1[h, k, t]
                    return carry

                lax.fori_loop(0, 4, add, 0)
                n.push((self.name, h, "n1", w), self.first(h, w, 0, 32), self.near1.at[h, k], self.axes(h)[0], w)

    def step4(self):
        n = self.net
        for h in (0, 1):
            n.arrived((self.name, h, "n1", -1))
            n.arrived((self.name, h, "n1", 1))
            part = self.first(h, 0, 0, 32)

            def add(t, carry):
                for r in (0, 16):
                    rows = pl.ds(r, 16)
                    value = part[t, rows].astype(F32) + self.near1[h, 0, t, rows].astype(F32)
                    part[t, rows] = (value + self.near1[h, 1, t, rows].astype(F32)).astype(BF)
                return carry

            lax.fori_loop(0, 4, add, 0)
            for k, w in ((0, -1), (1, 1)):
                n.push((self.name, h, "f2", w), self.second(h, 2, 16 * k, 16), self.far2.at[h, k], self.axes(h)[1], w)

    def step5(self):
        n = self.net
        for h in (0, 1):
            for k, w in ((0, -1), (1, 1)):
                n.arrived((self.name, h, "f2", w))
                part = self.second(h, w, 16 * k, 16)
                part[...] = part[...] + self.far2[h, k]
                n.push((self.name, h, "n2", w), self.second(h, w, 0, 32), self.near2.at[h, k], self.axes(h)[1], w)

    def step6(self):
        n = self.net
        for h in (0, 1):
            n.arrived((self.name, h, "n2", -1))
            n.arrived((self.name, h, "n2", 1))
            part = self.second(h, 0, 0, 32)
            for r in (0, 16):
                rows = pl.ds(r, 16)
                value = part[rows].astype(F32) + self.near2[h, 0, rows].astype(F32)
                self.out[pl.ds(h * 32 + r, 16)] = value + self.near2[h, 1, rows].astype(F32)


class Sum:
    def __init__(self, net, name, acc, far, near, out):
        self.net, self.name, self.acc = net, name, acc
        self.far, self.near, self.out = far, near, out

    def block(self, d, r0, rn):
        start = pl.multiple_of(wrap(self.net.y + d) * 192 + r0, 16)
        return self.acc.at[pl.ds(start, rn)]

    def step1(self, value):
        n = self.net

        def fill(d, carry):
            for half in (0, 1):
                rows = pl.ds(pl.multiple_of(d * 192 + half * 96, 16), 96)
                held = value[pl.ds(pl.multiple_of(d * 96, 16), 96), pl.ds(half * 1024, 1024)]
                self.acc[rows] = held.astype(BF)
            return carry

        lax.fori_loop(0, 4, fill, 0)
        for k, w in ((0, -1), (1, 1)):
            n.push((self.name, "f", w), self.block(2, 96 * k, 96), self.far.at[k], "y", w)

    def step2(self):
        n = self.net
        for k, w in ((0, -1), (1, 1)):
            n.arrived((self.name, "f", w))
            part = self.block(w, 96 * k, 96)
            part[...] = part[...] + self.far[k]
            n.push((self.name, "n", w), self.block(w, 0, 192), self.near.at[k], "y", w)

    def step3(self, sem):
        n = self.net
        n.arrived((self.name, "n", -1))
        n.arrived((self.name, "n", 1))
        part = self.block(0, 0, 192)

        def add(t, carry):
            rows = pl.ds(pl.multiple_of(t * 16, 16), 16)
            value = part[rows].astype(F32) + self.near[0, rows].astype(F32)
            part[rows] = (value + self.near[1, rows].astype(F32)).astype(BF)
            return carry

        lax.fori_loop(0, 12, add, 0)
        for w in (-1, 1):
            n.push((self.name, "g", w), part, self.out.at[n.y], "y", w)
        self.last = pltpu.make_async_copy(part, self.out.at[n.y], sem)
        self.last.start()

    def step4(self):
        n = self.net
        for k, w in ((0, -1), (1, 1)):
            n.arrived((self.name, "g", w))
            part = self.out.at[wrap(n.y - w), pl.ds(96 * k, 96)]
            n.push((self.name, "gf", w), part, part, "y", w)

    def step5(self):
        self.last.wait()
        for w in (-1, 1):
            self.net.arrived((self.name, "gf", w))


def vector_sum(net, src, pairs, alongx, alongz, alongy, out):
    z, x, c, y = net.z, net.x, net.c, net.y
    pairs[c] = src[...]
    net.push("vs", pairs.at[c], pairs.at[c], "s", 1)
    yield
    net.arrived("vs")
    alongx[x] = pairs[0] + pairs[1]
    for w in (1, -1, 2):
        net.push(("vx", w), alongx.at[x], alongx.at[x], "x", w)
    yield
    for w in (1, -1, 2):
        net.arrived(("vx", w))
    alongz[z] = (alongx[0] + alongx[1]) + (alongx[2] + alongx[3])
    for w in (1, -1, 2):
        net.push(("vz", w), alongz.at[z], alongz.at[z], "z", w)
    yield
    for w in (1, -1, 2):
        net.arrived(("vz", w))
    alongy[y] = (alongz[0] + alongz[1]) + (alongz[2] + alongz[3])
    out[...] = alongy[y]
    for w in (1, -1, 2):
        net.push(("vy", w), alongy.at[y], alongy.at[y], "y", w)
    yield
    for w in (1, -1, 2):
        net.arrived(("vy", w))
    out[0:2] = (alongy[0, 0:2] + alongy[1, 0:2]) + (alongy[2, 0:2] + alongy[3, 0:2])
    yield


def halves(a, b, left):
    return jnp.where(left, a, pltpu.roll(b, 64, 1)), jnp.where(left, pltpu.roll(a, 64, 1), b)


def front_kernel(
    hidden_in, upstream_in, w_up_in, w_down_in, gain, shift, w_qkv, b_qkv, w_dense, b_up, segments, keep,
    near_cos, near_sin, base_cos, base_sin, *refs,
):
    gathered, refs = refs[:PARTS], refs[PARTS:]
    in_t, up_t, pairs, od_in, dkv_in, share_out, d_share_out, bias_up, refs = *refs[:8], refs[8:]
    shards, inputs, staged, kept, weights, qd, kv, qd_all, kv_all, info_all, seen, total, refs = *refs[:12], refs[12:]
    od, dkv, theirs, ours, pair, share, d_share, hidden, upstream, w_up, w_down, info, refs = *refs[:12], refs[12:]
    t_cos, t_low, t_high, send, recv, loc = refs
    net = Net(send, recv)
    me, c = net.chip, net.c
    tables = (t_cos, t_low, t_high)
    lane = lax.broadcasted_iota(jnp.int32, (128, 128), 1)
    row = lax.broadcasted_iota(jnp.int32, (128, 128), 0)
    left = lane < 64
    mine = span(c * 384, 384)
    sems = iter(range(60))

    def here(src, dst):
        copy = pltpu.make_async_copy(src, dst, loc.at[next(sems)])
        copy.start()
        return copy

    reads = [here(a, b) for a, b in ((hidden_in, hidden), (upstream_in, upstream), (w_up_in, w_up), (w_down_in, w_down))]

    for k in range(4):
        columns = pl.ds(k * 128, 128)
        pieces = halves(w_qkv[1, :, columns], w_qkv[2, :, columns], left[:64])
        for j in (0, 1):
            shards[0, :, pl.ds(256 * k + 128 * j, 128)] = pieces[j].astype(BF)
    net.greet(RING_XZ + FARTHER + (("x", 2),))
    parts = [(FineGather if u < 2 else Gather)(net, u, shards.at[u], gathered[u]) for u in range(PARTS)]
    parts[0].begin(loc.at[next(sems)])
    shards[1, :, LOW] = w_qkv[0].astype(BF)
    shards[1, :, HIGH] = w_dense[...].astype(BF)
    parts[1].begin(loc.at[next(sems)])
    fill_tables(tables, near_cos, near_sin, base_cos, base_sin)
    info[0:3] = jnp.where(keep[...] > 0, segments[...], -1)
    info[3:6] = segments[...]
    info[6:8] = jnp.zeros((2, 128), jnp.int32)

    def norm(t, carry):
        rows = span(t * 16, 16, 16)
        value = hidden[rows].astype(F32)
        value = value - jnp.mean(value, axis=1, keepdims=True)
        value = value * lax.rsqrt(jnp.mean(value * value, axis=1, keepdims=True) + 1e-05)
        inputs[rows] = (value * gain[...] + shift[...]).astype(BF)
        return carry

    reads[0].wait()
    lax.fori_loop(0, 24, norm, 0)

    def transpose(t, carry):
        columns, rows = span(t * 128, 128), span(t * 64, 64, 64)
        for k, src in enumerate((inputs, upstream)):
            tile = src[:, columns].T
            first, second = tile[:64], tile[64:]
            kept[k, rows] = jnp.where(c == 0, first, second)
            staged[k, rows] = jnp.where(c == 0, second, first)
        return carry

    stays = []

    def factors():
        lax.fori_loop(0, 16, transpose, 0)
        for k, dst in enumerate((in_t, up_t)):
            stays.append(here(kept.at[k], dst.at[c]))
            net.push(("t", k), staged.at[k], dst.at[c], "s", 1)

    def load(u):
        parts[u].landed()
        return here(gathered[u], weights.at[u % 4].reshape(4, 4, 2, 64, 1024))

    first, second = parts[:2]
    first.near()
    first.pass_on(0)
    second.near()
    first.far()
    second.pass_on(0)
    reads[2].wait()
    reads[3].wait()
    for u in range(TILES):
        shards[2 + u, :, LOW] = w_up[:, pl.ds(u * 512, 512)].astype(BF)
        shards[2 + u, :, HIGH] = w_down[:, pl.ds(u * 512, 512)].astype(BF)
    first.pass_on(-1)
    first.pass_on(1)
    second.far()
    parts[2].begin(loc.at[next(sems)])
    first.pass_on(2)
    first.close(0)
    second.pass_on(-1)
    second.pass_on(1)
    parts[3].begin(loc.at[next(sems)])
    for a in (-1, 1, 2):
        first.close(a)
    second.pass_on(2)
    parts[2].near()
    parts[3].near()
    loads = {0: load(0)}
    second.close(0)
    second.close(-1)
    parts[4].begin(loc.at[next(sems)])
    parts[5].begin(loc.at[next(sems)])
    parts[2].far()

    loads[0].wait()

    def keys_values(h, carry):
        columns = span(h * 256, 256)
        value = dot(inputs[...], weights[0, :, columns], ((1,), (0,)))
        bk, bv = b_qkv[1:2, span(h * 128, 128)], b_qkv[2:3, span(h * 128, 128)]
        bias = halves(bk, bv, left[:1])
        for j in (0, 1):
            tile = value[:, 128 * j : 128 * j + 128] + bias[j]
            for s in range(3):
                piece = tile[128 * s : 128 * s + 128]
                kv[s, :, span(h * 256 + 128 * j, 128)] = jnp.where(left, turn(piece, tables, 1.0), piece).astype(BF)
        return carry

    lax.fori_loop(0, 4, keys_values, 0)
    pairs_of = kv_all.reshape(3, 8, 2, 128, 128)
    for dz, dx in OTHERS:
        net.push(("i", dz, dx), info, info_all.at[2 * me + c], dz, dx)
    for s in range(3):
        for dz, dx in OTHERS:
            net.push(("k", s, dz, dx), kv.at[s, :, lanes(net.chip_at(dz, dx))], kv_all.at[s, 2 * me + c], dz, dx)
        stays.append(here(kv.at[s, :, lanes(me)], kv_all.at[s, 2 * me + c]))
    stays.append(here(info, info_all.at[2 * me + c]))
    second.close(1)
    second.close(2)
    loads[1] = load(1)
    reads[1].wait()
    loads[1].wait()

    def queries(h, carry):
        columns = span(h * 128, 128)
        q = dot(inputs[...], weights[1, :, columns], ((1,), (0,))) + b_qkv[0:1, columns]
        d = dot(upstream[...], weights[1, :, span(512 + h * 128, 128)], ((1,), (0,)))
        for s in range(3):
            pieces = halves(turn(q[128 * s : 128 * s + 128], tables, 1.0), d[128 * s : 128 * s + 128], left)
            for j in (0, 1):
                qd[s, :, span(h * 256 + 128 * j, 128)] = pieces[j].astype(BF)
        return carry

    lax.fori_loop(0, 4, queries, 0)
    for s in range(3):
        for dz, dx in OTHERS:
            net.push(("q", s, dz, dx), qd.at[s, :, lanes(net.chip_at(dz, dx))], qd_all.at[me, s], dz, dx)
        stays.append(here(qd.at[s, :, lanes(me)], qd_all.at[me, s]))

    def units(u):
        slot = (2 + u) % 4
        loads[2 + u].wait()

        def some(j, carry):
            low, high = span(j * 256, 256), span(512 + j * 256, 256)
            unit = span(u * 512 + j * 256, 256)
            v = dot(inputs[...], weights[slot, :, low], ((1,), (0,))) + b_up[:, unit]
            d = dot(upstream[...], weights[slot, :, high], ((1,), (0,)))
            k = 0.7978845608028654
            square = v * v
            t = jnp.tanh(k * v * (1.0 + 0.044715 * square))
            half = 0.5 * (1.0 + t)
            slope = half + 0.5 * v * (1.0 - t * t) * (k * (1.0 + 0.134145 * square))
            d_up = (d * slope).astype(BF)
            pair[u, :, low] = d_up
            pair[u, :, high] = (v * half).astype(BF)
            bias_up[:, unit] = jnp.sum(d_up.astype(F32), axis=0, keepdims=True)
            return carry

        lax.fori_loop(0, 2, some, 0)
        net.push(("p", u), pair.at[u], pairs.at[u, mine], "s", 1)
        stays.append(here(pair.at[u], pairs.at[u, mine]))
        for total_ref, columns in ((d_share, LOW), (share, HIGH)):
            value = pair[u, :, columns]

            def spread(j, carry):
                rows = span(j * 512, 512)
                added = dot(value, weights[slot, rows, columns], ((1,), (1,)))
                if u == 0:
                    total_ref[:, rows] = added
                else:
                    total_ref[:, rows] += added
                return carry

            lax.fori_loop(0, 4, spread, 0)
            if u == TILES - 1:
                stays.append(here(total_ref, share_out if total_ref is share else d_share_out))

    def attend(s, i, blocks, own, first):
        width = blocks * 128
        begin = first * 128 if isinstance(first, int) else pl.multiple_of(first * 128, 128)
        tile = qd_all[i, s].astype(F32)
        both_halves = [jnp.where(left, tile * (HD**-0.5), 0.0), jnp.where(left, 0.0, tile)]
        asking = jnp.concatenate(both_halves, axis=0).astype(BF)
        keys = kv_all[s, pl.ds(first, blocks)].reshape(width, 128)
        both = dot(asking, keys, ((1,), (1,)))
        asked = jnp.broadcast_to(info_all[own, pl.ds(3 + s, 1), :].astype(F32), (128, 128)).T
        held = seen[pl.ds(s, 1), pl.ds(begin, width)].astype(F32)
        pieces = []
        for b in range(blocks):
            fits = asked == held[:, b * 128 : (b + 1) * 128]
            if isinstance(first, int):
                if b >= blocks - 2:
                    ahead = lane + (b * 128 - own * 128) - row
                    fits = (fits | (ahead == 0)) & (ahead <= 0)
            elif b == blocks - 1:
                fits = (fits | (lane == row)) & (lane <= row)
            elif b == 0:
                fits = fits & (lane > row)
            pieces.append(jnp.where(fits, both[:128, b * 128 : (b + 1) * 128], -1e30))
        scores = jnp.concatenate(pieces, axis=1)
        expo = jnp.exp(scores - jnp.max(scores, axis=1, keepdims=True))
        probs = expo * (1.0 / jnp.sum(expo, axis=1, keepdims=True))
        d_probs = both[128:]
        delta = jnp.sum(probs * d_probs, axis=1, keepdims=True)
        mixed = jnp.concatenate([(probs * (d_probs - delta)).astype(BF), probs.astype(BF)], axis=0)
        back = dot(mixed, keys, ((1,), (0,)))
        od[i, s] = jnp.where(left, back[:128] * (HD**-0.5), back[128:]).astype(BF)
        total[pl.ds(begin, width)] += dot(mixed, asking, ((0,), (0,)))

    def early(s):
        total[...] = jnp.zeros_like(total)
        for i in range(4):
            attend(s, i, 2 * i + 2, 2 * i + c, 0)

    def late(s):
        def some(i, carry):
            attend(s, i, 9, 2 * i + c, 2 * i + c - 8)
            return carry

        lax.fori_loop(4, 8, some, 0)
        dkv[s] = total[...].astype(BF).reshape(8, 2, 128, 128)

    def relay(s):
        for dz, dx in OTHERS:
            net.arrived(("k", s, dz, dx))
        held = pairs_of.at[s, :, c]
        net.push(("ks", s), held, held, "s", 1)

    def ready(s):
        net.arrived(("ks", s))
        for dz, dx in OTHERS:
            net.arrived(("q", s, dz, dx))

    def give(s):
        net.push(("b", s), dkv.at[s, :, 1 - c], theirs.at[s], "s", 1)
        stays.append(here(od.at[me, s], od_in.at[s, :, lanes(me)]))
        for dz, dx in OTHERS:
            net.push(("o", s, dz, dx), od.at[net.chip_at(dz, dx), s], od_in.at[s, :, lanes(me)], dz, dx)

    def give_more(s):
        net.arrived(("b", s))
        ours[s] = dkv[s, :, c] + theirs[s]
        for dz, dx in OTHERS:
            net.push(("d", s, dz, dx), ours.at[s, net.chip_at(dz, dx)], dkv_in.at[s, :, lanes(me)], dz, dx)
        stays.append(here(ours.at[s, me], dkv_in.at[s, :, lanes(me)]))

    parts[4].near()
    parts[5].near()
    factors()
    parts[2].pass_on()
    for copy in stays:
        copy.wait()
    stays.clear()
    for dz, dx in OTHERS:
        net.arrived(("i", dz, dx))
    held_info = info_all.reshape(8, 2, 8, 128).at[:, c]
    net.push("is", held_info, held_info, "s", 1)
    relay(0)
    relay(1)
    relay(2)
    net.arrived("is")
    for b in range(16):
        seen[:, b * 128 : (b + 1) * 128] = info_all[b]
    parts[3].far()
    parts[2].close()
    ready(0)
    early(0)
    parts[3].pass_on()
    late(0)
    give(0)
    parts[4].far()
    loads[2] = load(2)
    units(0)
    ready(1)
    parts[3].close()
    early(1)
    parts[4].pass_on()
    give_more(0)
    parts[5].far()
    late(1)
    give(1)
    loads[3] = load(3)
    units(1)
    ready(2)
    parts[4].close()
    early(2)
    parts[5].pass_on()
    give_more(1)
    late(2)
    give(2)
    loads[4] = load(4)
    parts[5].close()
    give_more(2)
    units(2)
    loads[5] = load(5)
    units(3)
    for copy in stays:
        copy.wait()
    net.drain()


def forward(args, cid):
    big = jax.ShapeDtypeStruct((4, 4, 2, 64, 1024), BF)
    factor = jax.ShapeDtypeStruct((2, 1024, 384), BF)
    heads = jax.ShapeDtypeStruct((3, 128, 1024), BF)
    wide = jax.ShapeDtypeStruct((384, 2048), F32)
    return pl.pallas_call(
        front_kernel,
        out_shape=[big] * PARTS
        + [factor, factor, jax.ShapeDtypeStruct((TILES, 768, 1024), BF), heads, heads]
        + [wide, wide, jax.ShapeDtypeStruct((1, 2048), F32)],
        in_specs=[ANY] * 4 + [VMEM] * (len(args) - 4),
        out_specs=[ANY] * (PARTS + 7) + [VMEM],
        scratch_shapes=[
            pltpu.VMEM((PARTS, 64, 1024), BF),
            pltpu.VMEM((384, 2048), BF),
            pltpu.VMEM((2, 1024, 384), BF),
            pltpu.VMEM((2, 1024, 384), BF),
            pltpu.VMEM((4, 2048, 1024), BF),
            pltpu.VMEM((3, 128, 1024), BF),
            pltpu.VMEM((3, 128, 1024), BF),
            pltpu.VMEM((8, 3, 128, 128), BF),
            pltpu.VMEM((3, 16, 128, 128), BF),
            pltpu.VMEM((16, 8, 128), jnp.int32),
            pltpu.VMEM((8, 2048), jnp.int32),
            pltpu.VMEM((2048, 128), F32),
            pltpu.VMEM((8, 3, 128, 128), BF),
            pltpu.VMEM((3, 8, 2, 128, 128), BF),
            pltpu.VMEM((3, 8, 128, 128), BF),
            pltpu.VMEM((3, 8, 128, 128), BF),
            pltpu.VMEM((TILES, 384, 1024), BF),
            pltpu.VMEM((384, 2048), F32),
            pltpu.VMEM((384, 2048), F32),
            pltpu.VMEM((384, 2048), BF),
            pltpu.VMEM((384, 2048), BF),
            pltpu.VMEM((64, 2048), F32),
            pltpu.VMEM((64, 2048), F32),
            pltpu.VMEM((8, 128), jnp.int32),
            pltpu.VMEM((128, 128), F32),
            pltpu.VMEM((128, 128), F32),
            pltpu.VMEM((128, 128), F32),
            pltpu.SemaphoreType.DMA((370,)),
            pltpu.SemaphoreType.DMA((370,)),
            pltpu.SemaphoreType.DMA((60,)),
        ],
        compiler_params=pltpu.CompilerParams(
            collective_id=cid, has_side_effects=True, vmem_limit_bytes=62 * 2**20
        ),
        name="forward",
    )(*args)


def back_kernel(
    od_in, dkv_in, upstream, hidden, in_t, up_t, pairs, heads_w0, heads_w1, share_in, d_share_in, bias_up, gain, near_cos,
    near_sin, base_cos, base_sin, input_grad, sum0, sum1, done, vec_out, *refs,
):
    accs, refs = refs[:PARTS], refs[PARTS:]
    far1, near1, far2, near2, refs = *refs[:4], refs[4:]
    weights, pair, factors, share, d_share, refs = *refs[:5], refs[5:]
    y_far, y_near, vecs, vec_acc, cores, alongx, alongz, alongy, t_cos, t_low, t_high, send, recv, loc = refs
    net = Net(send, recv)
    c = net.c
    tables = (t_cos, t_low, t_high)
    left = lax.broadcasted_iota(jnp.int32, (128, 128), 1) < 64
    mine = span(c * 384, 384)
    sems = iter(range(40))

    def here(src, dst):
        copy = pltpu.make_async_copy(src, dst, loc.at[next(sems)])
        copy.start()
        return copy

    factor_loads = [here(src.at[k], factors.at[j, :, pl.ds(384 * k, 384)]) for j, src in enumerate((in_t, up_t)) for k in (0, 1)]
    pair_loads = {u: here(pairs.at[u], pair.at[u]) for u in (0, 1)}
    weight_loads = [here(src, weights.at[k]) for k, src in enumerate((heads_w0, heads_w1))]
    share_loads = [here(d_share_in, d_share), here(share_in, share)]
    net.greet(RING_XZ + RING_Y + FAR)
    parts = [
        Scatter(net, ("g", i), accs[i], far1.at[i], near1.at[i], far2.at[i], near2.at[i], done.at[i])
        for i in range(PARTS)
    ]

    fill_tables(tables, near_cos, near_sin, base_cos, base_sin)

    def rows_of(s, carry):
        own = span(c * 384 + s * 128, 128)
        for h in range(8):
            columns = pl.ds(h * 128, 128)
            value = dkv_in[s, :, columns].astype(F32)
            pair[2, own, columns] = jnp.where(left, turn(value, tables, -1.0), value).astype(BF)
        for h in range(4):
            a = od_in[s, :, 256 * h : 256 * h + 128].astype(F32)
            b = od_in[s, :, 256 * h + 128 : 256 * h + 256].astype(F32)
            asked, got = halves(a, b, left)
            pair[3, own, pl.ds(h * 128, 128)] = turn(asked, tables, -1.0).astype(BF)
            pair[3, own, pl.ds(512 + h * 128, 128)] = got.astype(BF)
        return carry

    lax.fori_loop(0, 3, rows_of, 0)
    for slot in (2, 3):
        rows = pair.at[slot, mine]
        net.push(("p", slot), rows, rows, "s", 1)

    def gradients(u, slot, first_t, second_t):
        acc = accs[u]

        def some(z, carry):
            rows = span(z * 256, 256)
            for k, j in enumerate((first_t, second_t)):
                columns = pl.ds(k * 512, 512)
                value = dot(factors[j, rows], pair[slot, :, columns], ((1,), (0,)))
                acc[z, :, :, columns] = value.astype(BF).reshape(4, 64, 512)
            return carry

        lax.fori_loop(0, 4, some, 0)
        parts[u].step2()

    def tile(u):
        pair_loads[u].wait()
        gradients(u, u % 2, 0, 1)
        if u + 2 < TILES:
            pair_loads[u + 2] = here(pairs.at[u + 2], pair.at[u % 2])

    def spread(total, slot, columns):
        value = pair[slot, mine, columns]

        def chunk(j, carry):
            rows = span(j * 512, 512)
            total[:, rows] += dot(value, weights[slot - 2, rows, columns], ((1,), (1,)))
            return carry

        lax.fori_loop(0, 4, chunk, 0)

    def normed(rows):
        value = hidden[rows].astype(F32)
        value = value - jnp.mean(value, axis=1, keepdims=True)
        inverse = lax.rsqrt(jnp.mean(value * value, axis=1, keepdims=True) + 1e-05)
        return value * inverse, inverse

    def vectors():
        vec_acc[...] = jnp.zeros_like(vec_acc)
        vecs[...] = jnp.zeros_like(vecs)

        def chunk(t, carry):
            rows = span(t * 16, 16, 16)
            standard, _ = normed(rows)
            value = d_share[rows]
            for k, item in enumerate((value * standard, value, upstream[rows].astype(F32))):
                vec_acc[k] += item[:8] + item[8:]
            return carry

        lax.fori_loop(0, 24, chunk, 0)
        for k in range(3):
            vecs[k : k + 1] = jnp.sum(vec_acc[k], axis=0, keepdims=True)
        vecs[3:4] = bias_up[...]
        for k in range(4):
            columns = pl.ds(k * 256, 256)
            vecs[4:5, columns] = jnp.sum(pair[2, mine, columns].astype(F32), axis=0, keepdims=True)
        vecs[4:5, 1024:1536] = jnp.sum(pair[3, mine, LOW].astype(F32), axis=0, keepdims=True)

    def finish_in():
        def chunk(t, carry):
            rows = span(t * 16, 16, 16)
            base = t // 6 * 192 + lax.rem(t, 6) * 16
            standard, inverse = normed(rows)
            got = [weights[1, span(base + 96 * k, 16, 16)].astype(F32) for k in (0, 1)]
            scaled = jnp.concatenate(got, axis=1) * gain[...]
            mean = jnp.mean(scaled, axis=1, keepdims=True)
            along = jnp.mean(scaled * standard, axis=1, keepdims=True)
            d_share[rows] = upstream[rows].astype(F32) + inverse * (scaled - mean - standard * along)
            return carry

        lax.fori_loop(0, 24, chunk, 0)

    ys = [
        Sum(net, "yi", weights.at[0, pl.ds(0, 768)], y_far.at[0], y_near.at[0], sum0),
        Sum(net, "yo", weights.at[0, pl.ds(768, 768)], y_far.at[1], y_near.at[1], sum1),
    ]
    for copy in factor_loads:
        copy.wait()
    tile(0)
    tile(1)
    for copy in weight_loads + share_loads:
        copy.wait()
    spread(d_share, 2, ALL)
    spread(d_share, 3, LOW)
    ys[0].step1(d_share)
    spread(share, 3, HIGH)
    ys[1].step1(share)
    parts[0].step3()
    for slot in (2, 3):
        net.arrived(("p", slot))
    gradients(4, 2, 0, 0)
    ys[0].step2()
    parts[1].step3()
    gradients(5, 3, 0, 1)
    ys[1].step2()
    vectors()
    vec = vector_sum(net, vecs, cores, alongx, alongz, alongy, vec_out)
    next(vec)
    parts[0].step4()
    ys[0].step3(loc.at[next(sems)])
    tile(2)
    parts[4].step3()
    parts[1].step4()
    next(vec)
    ys[1].step3(loc.at[next(sems)])
    tile(3)
    parts[0].step5()
    parts[5].step3()
    ys[0].step4()
    parts[4].step4()
    next(vec)
    parts[1].step5()
    parts[0].step6()
    parts[2].step3()
    ys[1].step4()
    parts[5].step4()
    next(vec)
    parts[4].step5()
    parts[1].step6()
    parts[3].step3()
    ys[0].step5()
    got0 = here(sum0, weights.at[1, pl.ds(0, 768)].reshape(4, 192, 1024))
    parts[2].step4()
    next(vec)
    parts[5].step5()
    parts[4].step6()
    got0.wait()
    finish_in()
    out0 = here(d_share, input_grad)
    parts[3].step4()
    parts[2].step5()
    parts[5].step6()
    ys[1].step5()
    parts[3].step5()
    parts[2].step6()
    parts[3].step6()
    out0.wait()
    net.drain()


def backward(args, cid):
    wide = jax.ShapeDtypeStruct((384, 2048), F32)
    return pl.pallas_call(
        back_kernel,
        out_shape=[wide]
        + [jax.ShapeDtypeStruct((4, 192, 1024), BF)] * 2
        + [jax.ShapeDtypeStruct((PARTS, 64, 1024), F32), jax.ShapeDtypeStruct((8, 2048), F32)],
        in_specs=[VMEM] * 4 + [ANY] * 7 + [VMEM] * 6,
        out_specs=[ANY] * 3 + [VMEM] * 2,
        scratch_shapes=[pltpu.VMEM((4, 4, 64, 1024), BF)] * PARTS
        + [
            pltpu.VMEM((PARTS, 2, 2, 4, 16, 1024), BF),
            pltpu.VMEM((PARTS, 2, 2, 4, 32, 1024), BF),
            pltpu.VMEM((PARTS, 2, 2, 16, 1024), BF),
            pltpu.VMEM((PARTS, 2, 2, 32, 1024), BF),
            pltpu.VMEM((2, 2048, 1024), BF),
            pltpu.VMEM((4, 768, 1024), BF),
            pltpu.VMEM((2, 1024, 768), BF),
            pltpu.VMEM((384, 2048), F32),
            pltpu.VMEM((384, 2048), F32),
            pltpu.VMEM((2, 2, 96, 1024), BF),
            pltpu.VMEM((2, 2, 192, 1024), BF),
            pltpu.VMEM((8, 2048), F32),
            pltpu.VMEM((3, 8, 2048), F32),
            pltpu.VMEM((2, 8, 2048), F32),
            pltpu.VMEM((4, 8, 2048), F32),
            pltpu.VMEM((4, 8, 2048), F32),
            pltpu.VMEM((4, 8, 2048), F32),
            pltpu.VMEM((128, 128), F32),
            pltpu.VMEM((128, 128), F32),
            pltpu.VMEM((128, 128), F32),
            pltpu.SemaphoreType.DMA((140,)),
            pltpu.SemaphoreType.DMA((140,)),
            pltpu.SemaphoreType.DMA((40,)),
        ],
        compiler_params=pltpu.CompilerParams(
            collective_id=cid, has_side_effects=True, vmem_limit_bytes=63 * 2**20
        ),
        name="backward",
    )(*args)


def finish_kernel(
    hidden, summed, b_dense, b_down, grad, done, vecs, block_out, input_grad, g_qkv, g_dense, g_up, g_down, v_gain,
    v_shift, v_out, v_up, v_qkv, v_out2,
):
    for half in (0, 1):
        columns = pl.ds(half * 1024, 1024)
        bias = b_dense[:, columns] + b_down[:, columns]
        got = summed[0, pl.ds(96 * half, 96)].astype(F32)
        block_out[:, columns] = hidden[:, columns].astype(F32) + got + bias
    input_grad[...] = grad[...]

    @pl.when(pl.program_id(0) == 0)
    def _():
        left = lax.broadcasted_iota(jnp.int32, (64, 128), 1) < 64
        for u in range(TILES):
            g_up[:, pl.ds(u * 512, 512)] = done[u, :, :512]
            g_down[:, pl.ds(u * 512, 512)] = done[u, :, 512:]
        g_qkv[0] = done[5, :, :512]
        g_dense[...] = done[5, :, 512:]
        v_qkv[0:1] = vecs[4:5, 1024:1536]
        for k in range(4):
            a, b = pl.ds(256 * k, 128), pl.ds(256 * k + 128, 128)
            pieces = halves(done[4, :, a], done[4, :, b], left)
            rows = halves(vecs[4:5, a], vecs[4:5, b], left[:1])
            for j in (0, 1):
                g_qkv[1 + j, :, pl.ds(k * 128, 128)] = pieces[j]
                v_qkv[1 + j : 2 + j, pl.ds(k * 128, 128)] = rows[j]
        for k, dst in ((0, v_gain), (1, v_shift), (2, v_out), (2, v_out2), (3, v_up)):
            dst[...] = vecs[k]


def finish(hidden, summed, b_dense, b_down, grad, done, vecs):
    wide, row = jax.ShapeDtypeStruct((384, 2048), F32), jax.ShapeDtypeStruct((2048,), F32)
    rows = pl.BlockSpec((96, 2048), lambda i: (i, 0))
    small = [
        jax.ShapeDtypeStruct((3, 64, 512), F32),
        jax.ShapeDtypeStruct((64, 512), F32),
        jax.ShapeDtypeStruct((64, 2048), F32),
        jax.ShapeDtypeStruct((64, 2048), F32),
        row,
        row,
        row,
        row,
        jax.ShapeDtypeStruct((3, 512), F32),
        row,
    ]

    def whole(shape):
        return pl.BlockSpec(shape, lambda i: (0,) * len(shape))

    return pl.pallas_call(
        finish_kernel,
        grid=(4,),
        out_shape=[wide, wide] + small,
        in_specs=[rows, pl.BlockSpec((1, 192, 1024), lambda i: (i, 0, 0)), whole((1, 2048)), whole((1, 2048)), rows]
        + [whole((PARTS, 64, 1024)), whole((8, 2048))],
        out_specs=[rows, rows] + [whole(s.shape) for s in small],
        compiler_params=pltpu.CompilerParams(vmem_limit_bytes=62 * 2**20),
        name="finish",
    )(hidden, summed, b_dense, b_down, grad, done, vecs)


def local(
    hidden_in, segments, keep_mask, ln_gain, ln_shift, w_qkv, b_qkv, w_dense, b_dense, w_up, b_up, w_down, b_down,
    cotangent,
):
    rows, width = 384, 2048
    lanes_of = np.arange(128) % HD
    frequency = np.float32(10000.0) ** (-(np.arange(ROT // 2, dtype=np.float32) * 2.0) / ROT)
    frequency = np.where(lanes_of < ROT, np.resize(frequency.astype(np.float64), 128), 0.0)
    near, base = np.arange(128)[:, None] * frequency, 128 * np.arange(16)[:, None] * frequency
    tables = [jnp.asarray(t.astype(np.float32)) for t in (np.cos(near), np.sin(near), np.cos(base), np.sin(base))]
    hidden = hidden_in.reshape(rows, width)
    upstream = cotangent.reshape(rows, width)
    outs = forward(
        [hidden, upstream, w_up, w_down.T, ln_gain[None], ln_shift[None], w_qkv.transpose(1, 0, 2), b_qkv, w_dense.T]
        + [b_up[None], segments, keep_mask, *tables],
        0,
    )
    heads_w = [w.reshape(2048, 1024) for w in outs[:2]]
    in_t, up_t, pairs, od_in, dkv_in, share, d_share, bias_up = outs[PARTS:]
    input_grad, _, summed, done, vectors = backward(
        [od_in, dkv_in, upstream, hidden, in_t, up_t, pairs, *heads_w, share, d_share, bias_up, ln_gain[None], *tables], 1
    )
    block_out, input_grad, grad_qkv, grad_dense, grad_up, grad_down, gain, shift, out, up, grad_bqkv, out2 = finish(
        hidden, summed, b_dense[None], b_down[None], input_grad, done, vectors
    )
    return (
        block_out.reshape(3, 128, width),
        input_grad.reshape(3, 128, width),
        gain,
        shift,
        grad_qkv.transpose(1, 0, 2),
        grad_bqkv,
        grad_dense.T,
        out,
        grad_up,
        up,
        grad_down.T,
        out2,
    )


def solution(mesh):
    return jax.shard_map(
        local,
        mesh=mesh,
        in_specs=(
            P("dp", "seq", None),
            P("dp", "seq"),
            P("dp", "seq"),
            P(),
            P(),
            P(("dp", "seq"), None, "tp"),
            P(None, "tp"),
            P("tp", ("dp", "seq")),
            P(),
            P(("dp", "seq"), "tp"),
            P("tp"),
            P("tp", ("dp", "seq")),
            P(),
            P("dp", "seq", None),
        ),
        out_specs=(
            P("dp", "seq", None),
            P("dp", "seq", None),
            P(),
            P(),
            P(("dp", "seq"), None, "tp"),
            P(None, "tp"),
            P("tp", ("dp", "seq")),
            P(),
            P(("dp", "seq"), "tp"),
            P("tp"),
            P("tp", ("dp", "seq")),
            P(),
        ),
        check_vma=False,
    )
```

```python
import functools

import jax
import jax.numpy as jnp
import numpy as np
from jax import lax
from jax.experimental import pallas as pl
from jax.experimental.pallas import tpu as pltpu
from jax.sharding import PartitionSpec as P

MESH = pl.DeviceIdType.MESH
HD = 64
ROT = 32
WINDOW = 1024
BF = jnp.bfloat16
F32 = jnp.float32
ANY = pl.BlockSpec(memory_space=pl.ANY)
VMEM = pl.BlockSpec(memory_space=pltpu.VMEM)


def wrap(v):
    return lax.rem(v + 4, 4)


def place():
    dp, sq, tp = lax.axis_index("dp"), lax.axis_index("seq"), lax.axis_index("tp")
    return dp * 2 + sq // 8, lax.rem(sq // 2, 4), lax.rem(sq, 2), tp


def device(z, x, c, y):
    z, x, y = wrap(z), wrap(x), wrap(y)
    return {"dp": z // 2, "seq": lax.rem(z, 2) * 8 + x * 2 + c, "tp": y}


class Net:
    def __init__(self, send, recv):
        self.send, self.recv, self.n, self.out, self.keys = send, recv, 0, {}, {}
        self.z, self.x, self.c, self.y = place()
        self.flip = 1 - 2 * lax.rem(self.z, 2)
        self.chip = lax.rem(self.z, 2) * 4 + self.x

    def to(self, axis, way):
        z, x, c, y = self.z, self.x, self.c, self.y
        if axis == "s":
            return device(z, x, 1 - c, y)
        if axis == "x":
            return device(z, x + way, c, y)
        if axis == "z":
            return device(z + way, x, c, y)
        if axis == "y":
            return device(z, x, c, y + way)
        return device(z + axis * self.flip, x + way, c, y)

    def greet(self, targets):
        bar = pltpu.get_barrier_semaphore()
        for axis, way in targets:
            pl.semaphore_signal(bar, inc=1, device_id=self.to(axis, way), device_id_type=MESH)
        pl.semaphore_wait(bar, len(targets))

    def chip_at(self, dz, dx):
        return lax.rem(lax.rem(self.z, 2) + dz, 2) * 4 + wrap(self.x + dx)

    def push(self, key, src, dst, axis, way):
        k = self.n
        self.n += 1
        copy = pltpu.make_async_remote_copy(
            src_ref=src,
            dst_ref=dst,
            send_sem=self.send.at[k],
            recv_sem=self.recv.at[k],
            device_id=self.to(axis, way),
            device_id_type=MESH,
        )
        copy.start()
        self.out[key] = copy
        self.keys[key] = copy

    def arrived(self, key):
        self.keys.pop(key).wait_recv()

    def sent(self, key):
        self.out.pop(key).wait_send()

    def settle(self, keep=0):
        for key in list(self.out)[: len(self.out) - keep]:
            self.sent(key)

    def drain(self):
        for key in list(self.out):
            self.sent(key)
        for key in list(self.keys):
            self.arrived(key)


def lanes(chip):
    return pl.ds(pl.multiple_of(chip * 128, 128), 128)


def dot(a, b, dims):
    return lax.dot_general(a, b, (dims, ((), ())), preferred_element_type=F32)


def span(start, size, unit=128):
    return pl.ds(pl.multiple_of(start, unit), size)


RING_XZ = (("x", 1), ("x", -1), ("z", 1), ("z", -1), ("s", 1))
RING_Y = (("y", 1), ("y", -1))
FAR = (("x", 2), ("z", 2), ("y", 2))
FARTHER = ((1, 1), (1, 2), (1, 3))
OTHERS = tuple((dz, dx) for dz in (1, 0) for dx in (2, 1, 3, 0) if dz or dx)
PARTS = 6
TILES = 4
EARLY = 3
LOW, HIGH, ALL = pl.ds(0, 512), pl.ds(512, 512), pl.ds(0, 1024)


class Gather:
    def __init__(self, net, name, src, dst):
        self.net, self.name, self.src, self.dst = net, name, src, dst
        self.half, self.quarter = src.shape[0] // 2, src.shape[0] // 4

    def axes(self, h):
        return ("x", "z") if h == 0 else ("z", "x")

    def block(self, h, a, r0, rn):
        n, rows = self.net, pl.ds(h * self.half + r0, rn)
        if h == 0:
            return self.dst.at[n.z, wrap(n.x + a), n.c, rows]
        return self.dst.at[wrap(n.z + a), n.x, n.c, rows]

    def line(self, h, b, r0, rn):
        n, rows = self.net, pl.ds(h * self.half + r0, rn)
        if h == 0:
            return self.dst.at[wrap(n.z + b), :, n.c, rows]
        return self.dst.at[:, wrap(n.x + b), n.c, rows]

    def begin(self, sem):
        n = self.net
        for h in (0, 1):
            own = self.src.at[pl.ds(h * self.half, self.half)]
            for w in (1, -1):
                n.push((self.name, h, "A", w), own, self.block(h, 0, 0, self.half), self.axes(h)[0], w)
        self.local = pltpu.make_async_copy(self.src, self.dst.at[n.z, n.x, n.c], sem)
        self.local.start()

    def near(self):
        n = self.net
        for h in (0, 1):
            for w in (1, -1):
                n.arrived((self.name, h, "A", w))
                part = self.block(h, -w, 0 if w == 1 else self.quarter, self.quarter)
                n.push((self.name, h, "AF", w), part, part, self.axes(h)[0], w)

    def far(self):
        n = self.net
        self.local.wait()
        for h in (0, 1):
            for w in (1, -1):
                n.arrived((self.name, h, "AF", w))
            line = self.line(h, 0, 0, self.half)
            for w in (1, -1):
                n.push((self.name, h, "B", w), line, line, self.axes(h)[1], w)
            n.push((self.name, h, "s", 0), line, line, "s", 1)

    def pass_on(self):
        n = self.net
        for h in (0, 1):
            for w in (1, -1):
                n.arrived((self.name, h, "B", w))
                part = self.line(h, -w, 0 if w == 1 else self.quarter, self.quarter)
                n.push((self.name, h, "BF", w), part, part, self.axes(h)[1], w)
                line = self.line(h, -w, 0, self.half)
                n.push((self.name, h, "s", -w), line, line, "s", 1)

    def close(self):
        n = self.net
        for h in (0, 1):
            for w in (1, -1):
                n.arrived((self.name, h, "BF", w))
            line = self.line(h, 2, 0, self.half)
            n.push((self.name, h, "s", 2), line, line, "s", 1)

    def landed(self):
        for h in (0, 1):
            for b in (0, -1, 1, 2):
                self.net.arrived((self.name, h, "s", b))


class FineGather:
    def __init__(self, net, name, src, dst):
        self.net, self.name, self.src, self.dst = net, name, src, dst
        self.half, self.quarter = src.shape[0] // 2, src.shape[0] // 4

    def at(self, h, a, b, r0, rn):
        n = self.net
        z, x = (n.z + b, n.x + a) if h == 0 else (n.z + a, n.x + b)
        return self.dst.at[wrap(z), wrap(x), n.c, pl.ds(h * self.half + r0, rn)]

    def own(self, h):
        return self.src.at[pl.ds(h * self.half, self.half)]

    def axes(self, h):
        return ("x", "z") if h == 0 else ("z", "x")

    def begin(self, sem):
        n = self.net
        for h in (0, 1):
            for w in (1, -1):
                n.push((self.name, h, "A", w), self.own(h), self.at(h, 0, 0, 0, self.half), self.axes(h)[0], w)
        for h in (0, 1):
            for w in (1, -1):
                n.push((self.name, h, "B", 0, w), self.own(h), self.at(h, 0, 0, 0, self.half), self.axes(h)[1], w)
        whole = self.dst.at[n.z, n.x, n.c]
        n.push((self.name, "s"), self.src, whole, "s", 1)
        self.local = pltpu.make_async_copy(self.src, whole, sem)
        self.local.start()

    def spread(self, h, a):
        n = self.net
        block = self.at(h, a, 0, 0, self.half)
        for w in (1, -1):
            n.push((self.name, h, "B", a, w), block, block, self.axes(h)[1], w)
        n.push((self.name, h, "s", a, 0), block, block, "s", 1)

    def near(self):
        n = self.net
        for h in (0, 1):
            for w in (1, -1):
                n.arrived((self.name, h, "A", w))
                part = self.at(h, -w, 0, 0 if w == 1 else self.quarter, self.quarter)
                n.push((self.name, h, "AF", w), part, part, self.axes(h)[0], w)
                self.spread(h, -w)

    def far(self):
        for h in (0, 1):
            for w in (1, -1):
                self.net.arrived((self.name, h, "AF", w))
            self.spread(h, 2)

    def pass_on(self, a):
        n = self.net
        for h in (0, 1):
            for w in (1, -1):
                n.arrived((self.name, h, "B", a, w))
                part = self.at(h, a, -w, 0 if w == 1 else self.quarter, self.quarter)
                n.push((self.name, h, "BF", a, w), part, part, self.axes(h)[1], w)
                block = self.at(h, a, -w, 0, self.half)
                n.push((self.name, h, "s", a, -w), block, block, "s", 1)

    def close(self, a):
        n = self.net
        for h in (0, 1):
            for w in (1, -1):
                n.arrived((self.name, h, "BF", a, w))
            block = self.at(h, a, 2, 0, self.half)
            n.push((self.name, h, "s", a, 2), block, block, "s", 1)

    def landed(self):
        n = self.net
        self.local.wait()
        n.arrived((self.name, "s"))
        for h in (0, 1):
            for a in (-1, 1, 2):
                n.arrived((self.name, h, "s", a, 0))
            for a in (0, -1, 1, 2):
                for b in (-1, 1, 2):
                    n.arrived((self.name, h, "s", a, b))


def gelu_both(v, d):
    k = 0.7978845608028654
    square = v * v
    t = jnp.tanh(k * v * (1.0 + 0.044715 * square))
    half = 0.5 * (1.0 + t)
    slope = half + 0.5 * v * (1.0 - t * t) * (k * (1.0 + 0.134145 * square))
    return (d * slope).astype(BF), (v * half).astype(BF)


def fill_tables(tables, near_cos, near_sin, base_cos, base_sin):
    own = pl.ds(lax.axis_index("seq"), 1)
    cosine, sine = base_cos[own], base_sin[own]
    place_in = lax.rem(lax.broadcasted_iota(jnp.int32, (128, 128), 1), HD)
    tables[0][...] = near_cos[...] * cosine - near_sin[...] * sine
    total = near_sin[...] * cosine + near_cos[...] * sine
    tables[1][...] = jnp.where(place_in < ROT // 2, total, 0.0)
    tables[2][...] = jnp.where(place_in < ROT // 2, 0.0, total)


def turn(tensor, tables, sign):
    cosine, low, high = tables
    moved = pltpu.roll(tensor, 16, 1) * high[...] - pltpu.roll(tensor, 112, 1) * low[...]
    return tensor * cosine[...] + sign * moved


class Scatter:
    def __init__(self, net, name, acc, far1, near1, far2, near2, out):
        self.net, self.name, self.acc = net, name, acc
        self.far1, self.near1, self.far2, self.near2, self.out = far1, near1, far2, near2, out

    def axes(self, h):
        return ("z", "x") if h == 0 else ("x", "z")

    def first(self, h, d, r0, rn):
        n, rows = self.net, pl.ds(h * 32 + r0, rn)
        if h == 0:
            return self.acc.at[wrap(n.z + d), :, rows]
        return self.acc.at[:, wrap(n.x + d), rows]

    def second(self, h, d, r0, rn):
        n, rows = self.net, pl.ds(h * 32 + r0, rn)
        if h == 0:
            return self.acc.at[n.z, wrap(n.x + d), rows]
        return self.acc.at[wrap(n.z + d), n.x, rows]

    def step2(self):
        n = self.net
        for h in (0, 1):
            for k, w in ((0, -1), (1, 1)):
                n.push((self.name, h, "f1", w), self.first(h, 2, 16 * k, 16), self.far1.at[h, k], self.axes(h)[0], w)

    def step3(self):
        n = self.net
        for h in (0, 1):
            for k, w in ((0, -1), (1, 1)):
                n.arrived((self.name, h, "f1", w))
                part = self.first(h, w, 16 * k, 16)

                def add(t, carry):
                    part[t] = part[t] + self.far1[h, k, t]
                    return carry

                lax.fori_loop(0, 4, add, 0)
                n.push((self.name, h, "n1", w), self.first(h, w, 0, 32), self.near1.at[h, k], self.axes(h)[0], w)

    def step4(self):
        n = self.net
        for h in (0, 1):
            n.arrived((self.name, h, "n1", -1))
            n.arrived((self.name, h, "n1", 1))
            part = self.first(h, 0, 0, 32)

            def add(t, carry):
                for r in (0, 16):
                    rows = pl.ds(r, 16)
                    value = part[t, rows].astype(F32) + self.near1[h, 0, t, rows].astype(F32)
                    part[t, rows] = (value + self.near1[h, 1, t, rows].astype(F32)).astype(BF)
                return carry

            lax.fori_loop(0, 4, add, 0)
            for k, w in ((0, -1), (1, 1)):
                n.push((self.name, h, "f2", w), self.second(h, 2, 16 * k, 16), self.far2.at[h, k], self.axes(h)[1], w)

    def step5(self):
        n = self.net
        for h in (0, 1):
            for k, w in ((0, -1), (1, 1)):
                n.arrived((self.name, h, "f2", w))
                part = self.second(h, w, 16 * k, 16)
                part[...] = part[...] + self.far2[h, k]
                n.push((self.name, h, "n2", w), self.second(h, w, 0, 32), self.near2.at[h, k], self.axes(h)[1], w)

    def step6(self):
        n = self.net
        for h in (0, 1):
            n.arrived((self.name, h, "n2", -1))
            n.arrived((self.name, h, "n2", 1))
            part = self.second(h, 0, 0, 32)
            for r in (0, 16):
                rows = pl.ds(r, 16)
                value = part[rows].astype(F32) + self.near2[h, 0, rows].astype(F32)
                self.out[pl.ds(h * 32 + r, 16)] = value + self.near2[h, 1, rows].astype(F32)


class Sum:
    def __init__(self, net, name, acc, far, near, out):
        self.net, self.name, self.acc = net, name, acc
        self.far, self.near, self.out = far, near, out

    def block(self, d, r0, rn):
        start = pl.multiple_of(wrap(self.net.y + d) * 192 + r0, 16)
        return self.acc.at[pl.ds(start, rn)]

    def step1(self, value):
        n = self.net

        def fill(d, carry):
            for half in (0, 1):
                rows = pl.ds(pl.multiple_of(d * 192 + half * 96, 16), 96)
                held = value[pl.ds(pl.multiple_of(d * 96, 16), 96), pl.ds(half * 1024, 1024)]
                self.acc[rows] = held.astype(BF)
            return carry

        lax.fori_loop(0, 4, fill, 0)
        for k, w in ((0, -1), (1, 1)):
            n.push((self.name, "f", w), self.block(2, 96 * k, 96), self.far.at[k], "y", w)

    def step2(self):
        n = self.net
        for k, w in ((0, -1), (1, 1)):
            n.arrived((self.name, "f", w))
            part = self.block(w, 96 * k, 96)
            part[...] = part[...] + self.far[k]
            n.push((self.name, "n", w), self.block(w, 0, 192), self.near.at[k], "y", w)

    def step3(self, sem):
        n = self.net
        n.arrived((self.name, "n", -1))
        n.arrived((self.name, "n", 1))
        part = self.block(0, 0, 192)

        def add(t, carry):
            rows = pl.ds(pl.multiple_of(t * 16, 16), 16)
            value = part[rows].astype(F32) + self.near[0, rows].astype(F32)
            part[rows] = (value + self.near[1, rows].astype(F32)).astype(BF)
            return carry

        lax.fori_loop(0, 12, add, 0)
        for w in (-1, 1):
            n.push((self.name, "g", w), part, self.out.at[n.y], "y", w)
        self.last = pltpu.make_async_copy(part, self.out.at[n.y], sem)
        self.last.start()

    def step4(self):
        n = self.net
        for k, w in ((0, -1), (1, 1)):
            n.arrived((self.name, "g", w))
            part = self.out.at[wrap(n.y - w), pl.ds(96 * k, 96)]
            n.push((self.name, "gf", w), part, part, "y", w)

    def step5(self):
        self.last.wait()
        for w in (-1, 1):
            self.net.arrived((self.name, "gf", w))


def vector_sum(net, src, pairs, alongx, alongz, alongy, out):
    z, x, c, y = net.z, net.x, net.c, net.y
    pairs[c] = src[...]
    net.push("vs", pairs.at[c], pairs.at[c], "s", 1)
    yield
    net.arrived("vs")
    alongx[x] = pairs[0] + pairs[1]
    for w in (1, -1, 2):
        net.push(("vx", w), alongx.at[x], alongx.at[x], "x", w)
    yield
    for w in (1, -1, 2):
        net.arrived(("vx", w))
    alongz[z] = (alongx[0] + alongx[1]) + (alongx[2] + alongx[3])
    for w in (1, -1, 2):
        net.push(("vz", w), alongz.at[z], alongz.at[z], "z", w)
    yield
    for w in (1, -1, 2):
        net.arrived(("vz", w))
    alongy[y] = (alongz[0] + alongz[1]) + (alongz[2] + alongz[3])
    out[...] = alongy[y]
    for w in (1, -1, 2):
        net.push(("vy", w), alongy.at[y], alongy.at[y], "y", w)
    yield
    for w in (1, -1, 2):
        net.arrived(("vy", w))
    out[0:2] = (alongy[0, 0:2] + alongy[1, 0:2]) + (alongy[2, 0:2] + alongy[3, 0:2])
    yield


def halves(a, b, left):
    return jnp.where(left, a, pltpu.roll(b, 64, 1)), jnp.where(left, pltpu.roll(a, 64, 1), b)


def front_kernel(
    hidden_in, upstream_in, w_up_in, w_down_in, gain, shift, w_qkv, b_qkv, w_dense, b_up, segments, keep,
    near_cos, near_sin, base_cos, base_sin, *refs,
):
    gathered, refs = refs[:PARTS], refs[PARTS:]
    in_t, up_t, pairs, od_in, dkv_in, inputs_out, share_out, d_share_out, bias_up, refs = *refs[:9], refs[9:]
    shards, inputs, staged, kept, weights, qd, kv, qd_all, kv_all, info_all, seen, total, refs = *refs[:12], refs[12:]
    od, dkv, theirs, ours, pair, share, d_share, hidden, upstream, w_up, w_down, info, refs = *refs[:12], refs[12:]
    t_cos, t_low, t_high, send, recv, loc = refs
    net = Net(send, recv)
    me, c = net.chip, net.c
    tables = (t_cos, t_low, t_high)
    lane = lax.broadcasted_iota(jnp.int32, (128, 128), 1)
    row = lax.broadcasted_iota(jnp.int32, (128, 128), 0)
    left = lane < 64
    mine = span(c * 384, 384)
    sems = iter(range(60))

    def here(src, dst):
        copy = pltpu.make_async_copy(src, dst, loc.at[next(sems)])
        copy.start()
        return copy

    reads = [here(a, b) for a, b in ((hidden_in, hidden), (upstream_in, upstream), (w_up_in, w_up), (w_down_in, w_down))]

    for k in range(4):
        columns = pl.ds(k * 128, 128)
        pieces = halves(w_qkv[1, :, columns], w_qkv[2, :, columns], left[:64])
        for j in (0, 1):
            shards[0, :, pl.ds(256 * k + 128 * j, 128)] = pieces[j].astype(BF)
    net.greet(RING_XZ + FARTHER + (("x", 2),))
    parts = [(FineGather if u < 2 else Gather)(net, u, shards.at[u], gathered[u]) for u in range(PARTS)]
    parts[0].begin(loc.at[next(sems)])
    shards[1, :, LOW] = w_qkv[0].astype(BF)
    shards[1, :, HIGH] = w_dense[...].astype(BF)
    parts[1].begin(loc.at[next(sems)])
    fill_tables(tables, near_cos, near_sin, base_cos, base_sin)
    info[0:3] = jnp.where(keep[...] > 0, segments[...], -1)
    info[3:6] = segments[...]
    info[6:8] = jnp.zeros((2, 128), jnp.int32)

    def norm(t, carry):
        rows = span(t * 16, 16, 16)
        value = hidden[rows].astype(F32)
        value = value - jnp.mean(value, axis=1, keepdims=True)
        value = value * lax.rsqrt(jnp.mean(value * value, axis=1, keepdims=True) + 1e-05)
        inputs[rows] = (value * gain[...] + shift[...]).astype(BF)
        return carry

    reads[0].wait()
    lax.fori_loop(0, 24, norm, 0)

    def transpose(t, carry):
        columns, rows = span(t * 128, 128), span(t * 64, 64, 64)
        for k, src in enumerate((inputs, upstream)):
            tile = src[:, columns].T
            first, second = tile[:64], tile[64:]
            kept[k, rows] = jnp.where(c == 0, first, second)
            staged[k, rows] = jnp.where(c == 0, second, first)
        return carry

    stays = [here(inputs, inputs_out)]

    def factors():
        lax.fori_loop(0, 16, transpose, 0)
        for k, dst in enumerate((in_t, up_t)):
            stays.append(here(kept.at[k], dst.at[c]))
            net.push(("t", k), staged.at[k], dst.at[c], "s", 1)

    def load(u):
        parts[u].landed()
        return here(gathered[u], weights.at[u % 4].reshape(4, 4, 2, 64, 1024))

    first, second = parts[:2]
    first.near()
    first.pass_on(0)
    second.near()
    first.far()
    second.pass_on(0)
    reads[2].wait()
    reads[3].wait()
    for u in range(TILES):
        shards[2 + u, :, LOW] = w_up[:, pl.ds(u * 512, 512)].astype(BF)
        shards[2 + u, :, HIGH] = w_down[:, pl.ds(u * 512, 512)].astype(BF)
    first.pass_on(-1)
    first.pass_on(1)
    second.far()
    parts[2].begin(loc.at[next(sems)])
    first.pass_on(2)
    first.close(0)
    second.pass_on(-1)
    second.pass_on(1)
    parts[3].begin(loc.at[next(sems)])
    for a in (-1, 1, 2):
        first.close(a)
    second.pass_on(2)
    parts[2].near()
    parts[3].near()
    loads = {0: load(0)}
    second.close(0)
    second.close(-1)
    parts[4].begin(loc.at[next(sems)])
    parts[5].begin(loc.at[next(sems)])
    parts[2].far()

    loads[0].wait()

    def keys_values(h, carry):
        columns = span(h * 256, 256)
        value = dot(inputs[...], weights[0, :, columns], ((1,), (0,)))
        bk, bv = b_qkv[1:2, span(h * 128, 128)], b_qkv[2:3, span(h * 128, 128)]
        bias = halves(bk, bv, left[:1])
        for j in (0, 1):
            tile = value[:, 128 * j : 128 * j + 128] + bias[j]
            for s in range(3):
                piece = tile[128 * s : 128 * s + 128]
                kv[s, :, span(h * 256 + 128 * j, 128)] = jnp.where(left, turn(piece, tables, 1.0), piece).astype(BF)
        return carry

    lax.fori_loop(0, 4, keys_values, 0)
    pairs_of = kv_all.reshape(3, 8, 2, 128, 128)
    for dz, dx in OTHERS:
        net.push(("i", dz, dx), info, info_all.at[2 * me + c], dz, dx)
    for s in range(3):
        for dz, dx in OTHERS:
            net.push(("k", s, dz, dx), kv.at[s, :, lanes(net.chip_at(dz, dx))], kv_all.at[s, 2 * me + c], dz, dx)
        stays.append(here(kv.at[s, :, lanes(me)], kv_all.at[s, 2 * me + c]))
    stays.append(here(info, info_all.at[2 * me + c]))
    second.close(1)
    second.close(2)
    loads[1] = load(1)
    reads[1].wait()
    loads[1].wait()

    def queries(h, carry):
        columns = span(h * 128, 128)
        q = dot(inputs[...], weights[1, :, columns], ((1,), (0,))) + b_qkv[0:1, columns]
        d = dot(upstream[...], weights[1, :, span(512 + h * 128, 128)], ((1,), (0,)))
        for s in range(3):
            pieces = halves(turn(q[128 * s : 128 * s + 128], tables, 1.0), d[128 * s : 128 * s + 128], left)
            for j in (0, 1):
                qd[s, :, span(h * 256 + 128 * j, 128)] = pieces[j].astype(BF)
        return carry

    lax.fori_loop(0, 4, queries, 0)
    for s in range(3):
        for dz, dx in OTHERS:
            net.push(("q", s, dz, dx), qd.at[s, :, lanes(net.chip_at(dz, dx))], qd_all.at[me, s], dz, dx)
        stays.append(here(qd.at[s, :, lanes(me)], qd_all.at[me, s]))

    def units(u):
        slot = (2 + u) % 4
        loads[2 + u].wait()

        def some(j, carry):
            low, high = span(j * 256, 256), span(512 + j * 256, 256)
            unit = span(u * 512 + j * 256, 256)
            v = dot(inputs[...], weights[slot, :, low], ((1,), (0,))) + b_up[:, unit]
            d = dot(upstream[...], weights[slot, :, high], ((1,), (0,)))
            d_up, active = gelu_both(v, d)
            pair[u, :, low] = d_up
            pair[u, :, high] = active
            bias_up[:, unit] = jnp.sum(d_up.astype(F32), axis=0, keepdims=True)
            return carry

        lax.fori_loop(0, 2, some, 0)
        net.push(("p", u), pair.at[u], pairs.at[u, mine], "s", 1)
        stays.append(here(pair.at[u], pairs.at[u, mine]))
        for total_ref, columns in ((d_share, LOW), (share, HIGH)):
            value = pair[u, :, columns]

            def spread(j, carry):
                rows = span(j * 512, 512)
                added = dot(value, weights[slot, rows, columns], ((1,), (1,)))
                if u == 0:
                    total_ref[:, rows] = added
                else:
                    total_ref[:, rows] += added
                return carry

            lax.fori_loop(0, 4, spread, 0)
            if u == EARLY - 1:
                stays.append(here(total_ref, share_out if total_ref is share else d_share_out))

    def attend(s, i, blocks, own, first):
        width = blocks * 128
        begin = first * 128 if isinstance(first, int) else pl.multiple_of(first * 128, 128)
        tile = qd_all[i, s].astype(F32)
        both_halves = [jnp.where(left, tile * (HD**-0.5), 0.0), jnp.where(left, 0.0, tile)]
        asking = jnp.concatenate(both_halves, axis=0).astype(BF)
        keys = kv_all[s, pl.ds(first, blocks)].reshape(width, 128)
        both = dot(asking, keys, ((1,), (1,)))
        asked = jnp.broadcast_to(info_all[own, pl.ds(3 + s, 1), :].astype(F32), (128, 128)).T
        held = seen[pl.ds(s, 1), pl.ds(begin, width)].astype(F32)
        pieces = []
        for b in range(blocks):
            fits = asked == held[:, b * 128 : (b + 1) * 128]
            if isinstance(first, int):
                if b >= blocks - 2:
                    ahead = lane + (b * 128 - own * 128) - row
                    fits = (fits | (ahead == 0)) & (ahead <= 0)
            elif b == blocks - 1:
                fits = (fits | (lane == row)) & (lane <= row)
            elif b == 0:
                fits = fits & (lane > row)
            pieces.append(jnp.where(fits, both[:128, b * 128 : (b + 1) * 128], -1e30))
        scores = jnp.concatenate(pieces, axis=1)
        expo = jnp.exp(scores - jnp.max(scores, axis=1, keepdims=True))
        probs = expo * (1.0 / jnp.sum(expo, axis=1, keepdims=True))
        d_probs = both[128:]
        delta = jnp.sum(probs * d_probs, axis=1, keepdims=True)
        mixed = jnp.concatenate([(probs * (d_probs - delta)).astype(BF), probs.astype(BF)], axis=0)
        back = dot(mixed, keys, ((1,), (0,)))
        od[i, s] = jnp.where(left, back[:128] * (HD**-0.5), back[128:]).astype(BF)
        total[pl.ds(begin, width)] += dot(mixed, asking, ((0,), (0,)))

    def early(s):
        total[...] = jnp.zeros_like(total)
        for i in range(4):
            attend(s, i, 2 * i + 2, 2 * i + c, 0)

    def late(s):
        def some(i, carry):
            attend(s, i, 9, 2 * i + c, 2 * i + c - 8)
            return carry

        lax.fori_loop(4, 8, some, 0)
        dkv[s] = total[...].astype(BF).reshape(8, 2, 128, 128)

    def relay(s):
        for dz, dx in OTHERS:
            net.arrived(("k", s, dz, dx))
        held = pairs_of.at[s, :, c]
        net.push(("ks", s), held, held, "s", 1)

    def ready(s):
        net.arrived(("ks", s))
        for dz, dx in OTHERS:
            net.arrived(("q", s, dz, dx))

    def give(s):
        net.push(("b", s), dkv.at[s, :, 1 - c], theirs.at[s], "s", 1)
        stays.append(here(od.at[me, s], od_in.at[s, :, lanes(me)]))
        for dz, dx in OTHERS:
            net.push(("o", s, dz, dx), od.at[net.chip_at(dz, dx), s], od_in.at[s, :, lanes(me)], dz, dx)

    def give_more(s):
        net.arrived(("b", s))
        ours[s] = dkv[s, :, c] + theirs[s]
        for dz, dx in OTHERS:
            net.push(("d", s, dz, dx), ours.at[s, net.chip_at(dz, dx)], dkv_in.at[s, :, lanes(me)], dz, dx)
        stays.append(here(ours.at[s, me], dkv_in.at[s, :, lanes(me)]))

    parts[4].near()
    parts[5].near()
    factors()
    parts[2].pass_on()
    for copy in stays:
        copy.wait()
    stays.clear()
    for dz, dx in OTHERS:
        net.arrived(("i", dz, dx))
    held_info = info_all.reshape(8, 2, 8, 128).at[:, c]
    net.push("is", held_info, held_info, "s", 1)
    relay(0)
    relay(1)
    relay(2)
    net.arrived("is")
    for b in range(16):
        seen[:, b * 128 : (b + 1) * 128] = info_all[b]
    parts[3].far()
    parts[2].close()
    net.settle(60)
    ready(0)
    early(0)
    parts[3].pass_on()
    late(0)
    give(0)
    parts[4].far()
    loads[2] = load(2)
    units(0)
    net.settle(50)
    ready(1)
    parts[3].close()
    early(1)
    parts[4].pass_on()
    give_more(0)
    parts[5].far()
    late(1)
    give(1)
    loads[3] = load(3)
    units(1)
    net.settle(50)
    ready(2)
    parts[4].close()
    early(2)
    parts[5].pass_on()
    give_more(1)
    late(2)
    give(2)
    loads[4] = load(4)
    net.settle(40)
    parts[5].close()
    give_more(2)
    units(2)
    parts[5].landed()
    for copy in stays:
        copy.wait()
    net.drain()


def forward(args, cid):
    big = jax.ShapeDtypeStruct((4, 4, 2, 64, 1024), BF)
    factor = jax.ShapeDtypeStruct((2, 1024, 384), BF)
    heads = jax.ShapeDtypeStruct((3, 128, 1024), BF)
    wide = jax.ShapeDtypeStruct((384, 2048), F32)
    return pl.pallas_call(
        front_kernel,
        out_shape=[big] * PARTS
        + [factor, factor, jax.ShapeDtypeStruct((EARLY, 768, 1024), BF), heads, heads]
        + [jax.ShapeDtypeStruct((384, 2048), BF)]
        + [wide, wide, jax.ShapeDtypeStruct((1, 2048), F32)],
        in_specs=[ANY] * 4 + [VMEM] * (len(args) - 4),
        out_specs=[ANY] * (PARTS + 8) + [VMEM],
        scratch_shapes=[
            pltpu.VMEM((PARTS, 64, 1024), BF),
            pltpu.VMEM((384, 2048), BF),
            pltpu.VMEM((2, 1024, 384), BF),
            pltpu.VMEM((2, 1024, 384), BF),
            pltpu.VMEM((4, 2048, 1024), BF),
            pltpu.VMEM((3, 128, 1024), BF),
            pltpu.VMEM((3, 128, 1024), BF),
            pltpu.VMEM((8, 3, 128, 128), BF),
            pltpu.VMEM((3, 16, 128, 128), BF),
            pltpu.VMEM((16, 8, 128), jnp.int32),
            pltpu.VMEM((8, 2048), jnp.int32),
            pltpu.VMEM((2048, 128), F32),
            pltpu.VMEM((8, 3, 128, 128), BF),
            pltpu.VMEM((3, 8, 2, 128, 128), BF),
            pltpu.VMEM((3, 8, 128, 128), BF),
            pltpu.VMEM((3, 8, 128, 128), BF),
            pltpu.VMEM((EARLY, 384, 1024), BF),
            pltpu.VMEM((384, 2048), F32),
            pltpu.VMEM((384, 2048), F32),
            pltpu.VMEM((384, 2048), BF),
            pltpu.VMEM((384, 2048), BF),
            pltpu.VMEM((64, 2048), F32),
            pltpu.VMEM((64, 2048), F32),
            pltpu.VMEM((8, 128), jnp.int32),
            pltpu.VMEM((128, 128), F32),
            pltpu.VMEM((128, 128), F32),
            pltpu.VMEM((128, 128), F32),
            pltpu.SemaphoreType.DMA((370,)),
            pltpu.SemaphoreType.DMA((370,)),
            pltpu.SemaphoreType.DMA((60,)),
        ],
        compiler_params=pltpu.CompilerParams(
            collective_id=cid, has_side_effects=True, vmem_limit_bytes=62 * 2**20
        ),
        name="forward",
    )(*args)


def back_kernel(
    od_any, dkv_any, upstream_any, hidden_any, in_t, up_t, pairs, heads_w0, heads_w1, last_w,
    inputs_any, share_in, d_share_in, bias_up, b_up, gain, near_cos,
    near_sin, base_cos, base_sin, input_grad, sum0, sum1, done, vec_out, *refs,
):
    accs, refs = refs[:PARTS], refs[PARTS:]
    far1, near1, far2, near2, refs = *refs[:4], refs[4:]
    weights, pair, factors, share, d_share, od_in, dkv_in, upstream, hidden, inputs, refs = *refs[:10], refs[10:]
    y_far, y_near, vecs, vec_acc, cores, alongx, alongz, alongy, t_cos, t_low, t_high, send, recv, loc = refs
    net = Net(send, recv)
    c = net.c
    tables = (t_cos, t_low, t_high)
    left = lax.broadcasted_iota(jnp.int32, (128, 128), 1) < 64
    mine = span(c * 384, 384)
    sems = iter(range(40))

    def here(src, dst):
        copy = pltpu.make_async_copy(src, dst, loc.at[next(sems)])
        copy.start()
        return copy

    factor_loads = [here(src.at[k], factors.at[j, :, pl.ds(384 * k, 384)]) for j, src in enumerate((in_t, up_t)) for k in (0, 1)]
    pair_loads = {0: here(pairs.at[0], pair.at[0])}
    head_loads = [here(od_any, od_in), here(dkv_any, dkv_in)]
    unit_loads = [here(last_w, weights.at[0]), here(inputs_any, inputs), here(upstream_any, upstream)]
    pair_loads[1] = here(pairs.at[1], pair.at[1])
    share_loads = [here(d_share_in, d_share), here(share_in, share)]
    weight_loads = [here(heads_w1, weights.at[1])]
    row_loads = [here(hidden_any, hidden)]
    net.greet(RING_XZ + RING_Y + FAR)
    parts = [
        Scatter(net, ("g", i), accs[i], far1.at[i], near1.at[i], far2.at[i], near2.at[i], done.at[i])
        for i in range(PARTS)
    ]

    fill_tables(tables, near_cos, near_sin, base_cos, base_sin)

    def rows_of(s, carry):
        own = span(c * 384 + s * 128, 128)
        for h in range(8):
            columns = pl.ds(h * 128, 128)
            value = dkv_in[s, :, columns].astype(F32)
            pair[2, own, columns] = jnp.where(left, turn(value, tables, -1.0), value).astype(BF)
        for h in range(4):
            a = od_in[s, :, 256 * h : 256 * h + 128].astype(F32)
            b = od_in[s, :, 256 * h + 128 : 256 * h + 256].astype(F32)
            asked, got = halves(a, b, left)
            pair[3, own, pl.ds(h * 128, 128)] = turn(asked, tables, -1.0).astype(BF)
            pair[3, own, pl.ds(512 + h * 128, 128)] = got.astype(BF)
        return carry

    def heads():
        for copy in head_loads:
            copy.wait()
        lax.fori_loop(0, 3, rows_of, 0)
        for slot in (2, 3):
            rows = pair.at[slot, mine]
            net.push(("p", slot), rows, rows, "s", 1)

    def gradients(u, slot, first_t, second_t):
        acc = accs[u]

        def some(z, carry):
            rows = span(z * 256, 256)
            for k, j in enumerate((first_t, second_t)):
                columns = pl.ds(k * 512, 512)
                value = dot(factors[j, rows], pair[slot, :, columns], ((1,), (0,)))
                acc[z, :, :, columns] = value.astype(BF).reshape(4, 64, 512)
            return carry

        lax.fori_loop(0, 4, some, 0)
        parts[u].step2()

    def tile(u):
        pair_loads[u].wait()
        gradients(u, u % 2, 0, 1)
        if u + 2 < EARLY:
            pair_loads[u + 2] = here(pairs.at[u + 2], pair.at[u % 2])

    def spread(total, slot, source, columns):
        value = pair[slot, mine, columns]

        def chunk(j, carry):
            rows = span(j * 512, 512)
            total[:, rows] += dot(value, weights[source, rows, columns], ((1,), (1,)))
            return carry

        lax.fori_loop(0, 4, chunk, 0)

    def units():
        for copy in unit_loads + share_loads:
            copy.wait()

        def some(j, carry):
            low, high = span(j * 256, 256), span(512 + j * 256, 256)
            unit = span(EARLY * 512 + j * 256, 256)
            v = dot(inputs[...], weights[0, :, low], ((1,), (0,))) + b_up[:, unit]
            d = dot(upstream[...], weights[0, :, high], ((1,), (0,)))
            d_up, active = gelu_both(v, d)
            pair[4, mine, low] = d_up
            pair[4, mine, high] = active
            return carry

        lax.fori_loop(0, 2, some, 0)
        rows = pair.at[4, mine]
        net.push(("p", 4), rows, rows, "s", 1)
        spread(d_share, 4, 0, LOW)
        spread(share, 4, 0, HIGH)
        weight_loads.append(here(heads_w0, weights.at[0]))

    def normed(rows):
        value = hidden[rows].astype(F32)
        value = value - jnp.mean(value, axis=1, keepdims=True)
        inverse = lax.rsqrt(jnp.mean(value * value, axis=1, keepdims=True) + 1e-05)
        return value * inverse, inverse

    def vectors():
        vec_acc[...] = jnp.zeros_like(vec_acc)
        vecs[...] = jnp.zeros_like(vecs)

        def chunk(t, carry):
            rows = span(t * 16, 16, 16)
            standard, _ = normed(rows)
            value = d_share[rows]
            for k, item in enumerate((value * standard, value, upstream[rows].astype(F32))):
                vec_acc[k] += item[:8] + item[8:]
            return carry

        lax.fori_loop(0, 24, chunk, 0)
        for k in range(3):
            vecs[k : k + 1] = jnp.sum(vec_acc[k], axis=0, keepdims=True)
        vecs[3:4, 0 : EARLY * 512] = bias_up[:, 0 : EARLY * 512]
        vecs[3:4, EARLY * 512 : 2048] = jnp.sum(pair[4, mine, LOW].astype(F32), axis=0, keepdims=True)
        for k in range(4):
            columns = pl.ds(k * 256, 256)
            vecs[4:5, columns] = jnp.sum(pair[2, mine, columns].astype(F32), axis=0, keepdims=True)
        vecs[4:5, 1024:1536] = jnp.sum(pair[3, mine, LOW].astype(F32), axis=0, keepdims=True)

    def finish_in():
        def chunk(t, carry):
            rows = span(t * 16, 16, 16)
            base = t // 6 * 192 + lax.rem(t, 6) * 16
            standard, inverse = normed(rows)
            got = [weights[1, span(base + 96 * k, 16, 16)].astype(F32) for k in (0, 1)]
            scaled = jnp.concatenate(got, axis=1) * gain[...]
            mean = jnp.mean(scaled, axis=1, keepdims=True)
            along = jnp.mean(scaled * standard, axis=1, keepdims=True)
            d_share[rows] = upstream[rows].astype(F32) + inverse * (scaled - mean - standard * along)
            return carry

        lax.fori_loop(0, 24, chunk, 0)

    ys = [
        Sum(net, "yi", weights.at[0, pl.ds(0, 768)], y_far.at[0], y_near.at[0], sum0),
        Sum(net, "yo", weights.at[0, pl.ds(768, 768)], y_far.at[1], y_near.at[1], sum1),
    ]
    for copy in factor_loads:
        copy.wait()
    tile(0)
    heads()
    tile(1)
    parts[0].step3()
    units()
    parts[1].step3()
    weight_loads[0].wait()
    spread(d_share, 3, 1, LOW)
    parts[0].step4()
    weight_loads[1].wait()
    spread(d_share, 2, 0, ALL)
    ys[0].step1(d_share)
    parts[1].step4()
    spread(share, 3, 1, HIGH)
    ys[1].step1(share)
    tile(2)
    parts[0].step5()
    ys[0].step2()
    net.arrived(("p", 4))
    gradients(3, 4, 0, 1)
    parts[2].step3()
    parts[1].step5()
    ys[1].step2()
    row_loads[0].wait()
    vectors()
    vec = vector_sum(net, vecs, cores, alongx, alongz, alongy, vec_out)
    next(vec)
    parts[3].step3()
    parts[0].step6()
    parts[2].step4()
    ys[0].step3(loc.at[next(sems)])
    for slot in (2, 3):
        net.arrived(("p", slot))
    gradients(4, 2, 0, 0)
    next(vec)
    parts[3].step4()
    parts[1].step6()
    parts[2].step5()
    ys[1].step3(loc.at[next(sems)])
    gradients(5, 3, 0, 1)
    next(vec)
    parts[4].step3()
    parts[3].step5()
    ys[0].step4()
    parts[5].step3()
    next(vec)
    parts[4].step4()
    parts[2].step6()
    ys[1].step4()
    parts[5].step4()
    parts[3].step6()
    next(vec)
    parts[4].step5()
    ys[0].step5()
    got0 = here(sum0, weights.at[1, pl.ds(0, 768)].reshape(4, 192, 1024))
    parts[5].step5()
    got0.wait()
    finish_in()
    out0 = here(d_share, input_grad)
    parts[4].step6()
    ys[1].step5()
    parts[5].step6()
    out0.wait()
    net.drain()


def backward(args, cid):
    wide = jax.ShapeDtypeStruct((384, 2048), F32)
    return pl.pallas_call(
        back_kernel,
        out_shape=[wide]
        + [jax.ShapeDtypeStruct((4, 192, 1024), BF)] * 2
        + [jax.ShapeDtypeStruct((PARTS, 64, 1024), F32), jax.ShapeDtypeStruct((8, 2048), F32)],
        in_specs=[ANY] * 13 + [VMEM] * 7,
        out_specs=[ANY] * 3 + [VMEM] * 2,
        scratch_shapes=[pltpu.VMEM((4, 4, 64, 1024), BF)] * PARTS
        + [
            pltpu.VMEM((PARTS, 2, 2, 4, 16, 1024), BF),
            pltpu.VMEM((PARTS, 2, 2, 4, 32, 1024), BF),
            pltpu.VMEM((PARTS, 2, 2, 16, 1024), BF),
            pltpu.VMEM((PARTS, 2, 2, 32, 1024), BF),
            pltpu.VMEM((2, 2048, 1024), BF),
            pltpu.VMEM((5, 768, 1024), BF),
            pltpu.VMEM((2, 1024, 768), BF),
            pltpu.VMEM((384, 2048), F32),
            pltpu.VMEM((384, 2048), F32),
            pltpu.VMEM((3, 128, 1024), BF),
            pltpu.VMEM((3, 128, 1024), BF),
            pltpu.VMEM((384, 2048), BF),
            pltpu.VMEM((384, 2048), BF),
            pltpu.VMEM((384, 2048), BF),
            pltpu.VMEM((2, 2, 96, 1024), BF),
            pltpu.VMEM((2, 2, 192, 1024), BF),
            pltpu.VMEM((8, 2048), F32),
            pltpu.VMEM((3, 8, 2048), F32),
            pltpu.VMEM((2, 8, 2048), F32),
            pltpu.VMEM((4, 8, 2048), F32),
            pltpu.VMEM((4, 8, 2048), F32),
            pltpu.VMEM((4, 8, 2048), F32),
            pltpu.VMEM((128, 128), F32),
            pltpu.VMEM((128, 128), F32),
            pltpu.VMEM((128, 128), F32),
            pltpu.SemaphoreType.DMA((140,)),
            pltpu.SemaphoreType.DMA((140,)),
            pltpu.SemaphoreType.DMA((40,)),
        ],
        compiler_params=pltpu.CompilerParams(
            collective_id=cid, has_side_effects=True, vmem_limit_bytes=63 * 2**20
        ),
        name="backward",
    )(*args)


def finish_kernel(
    hidden, summed, b_dense, b_down, grad, done, vecs, block_out, input_grad, g_qkv, g_dense, g_up, g_down, v_gain,
    v_shift, v_out, v_up, v_qkv, v_out2,
):
    for half in (0, 1):
        columns = pl.ds(half * 1024, 1024)
        bias = b_dense[:, columns] + b_down[:, columns]
        got = summed[0, pl.ds(96 * half, 96)].astype(F32)
        block_out[:, columns] = hidden[:, columns].astype(F32) + got + bias
    input_grad[...] = grad[...]

    @pl.when(pl.program_id(0) == 0)
    def _():
        left = lax.broadcasted_iota(jnp.int32, (64, 128), 1) < 64
        for u in range(TILES):
            g_up[:, pl.ds(u * 512, 512)] = done[u, :, :512]
            g_down[:, pl.ds(u * 512, 512)] = done[u, :, 512:]
        g_qkv[0] = done[5, :, :512]
        g_dense[...] = done[5, :, 512:]
        v_qkv[0:1] = vecs[4:5, 1024:1536]
        for k in range(4):
            a, b = pl.ds(256 * k, 128), pl.ds(256 * k + 128, 128)
            pieces = halves(done[4, :, a], done[4, :, b], left)
            rows = halves(vecs[4:5, a], vecs[4:5, b], left[:1])
            for j in (0, 1):
                g_qkv[1 + j, :, pl.ds(k * 128, 128)] = pieces[j]
                v_qkv[1 + j : 2 + j, pl.ds(k * 128, 128)] = rows[j]
        for k, dst in ((0, v_gain), (1, v_shift), (2, v_out), (2, v_out2), (3, v_up)):
            dst[...] = vecs[k]


def finish(hidden, summed, b_dense, b_down, grad, done, vecs):
    wide, row = jax.ShapeDtypeStruct((384, 2048), F32), jax.ShapeDtypeStruct((2048,), F32)
    rows = pl.BlockSpec((96, 2048), lambda i: (i, 0))
    small = [
        jax.ShapeDtypeStruct((3, 64, 512), F32),
        jax.ShapeDtypeStruct((64, 512), F32),
        jax.ShapeDtypeStruct((64, 2048), F32),
        jax.ShapeDtypeStruct((64, 2048), F32),
        row,
        row,
        row,
        row,
        jax.ShapeDtypeStruct((3, 512), F32),
        row,
    ]

    def whole(shape):
        return pl.BlockSpec(shape, lambda i: (0,) * len(shape))

    return pl.pallas_call(
        finish_kernel,
        grid=(4,),
        out_shape=[wide, wide] + small,
        in_specs=[rows, pl.BlockSpec((1, 192, 1024), lambda i: (i, 0, 0)), whole((1, 2048)), whole((1, 2048)), rows]
        + [whole((PARTS, 64, 1024)), whole((8, 2048))],
        out_specs=[rows, rows] + [whole(s.shape) for s in small],
        compiler_params=pltpu.CompilerParams(vmem_limit_bytes=62 * 2**20),
        name="finish",
    )(hidden, summed, b_dense, b_down, grad, done, vecs)


def local(
    hidden_in, segments, keep_mask, ln_gain, ln_shift, w_qkv, b_qkv, w_dense, b_dense, w_up, b_up, w_down, b_down,
    cotangent,
):
    rows, width = 384, 2048
    lanes_of = np.arange(128) % HD
    frequency = np.float32(10000.0) ** (-(np.arange(ROT // 2, dtype=np.float32) * 2.0) / ROT)
    frequency = np.where(lanes_of < ROT, np.resize(frequency.astype(np.float64), 128), 0.0)
    near, base = np.arange(128)[:, None] * frequency, 128 * np.arange(16)[:, None] * frequency
    tables = [jnp.asarray(t.astype(np.float32)) for t in (np.cos(near), np.sin(near), np.cos(base), np.sin(base))]
    hidden = hidden_in.reshape(rows, width)
    upstream = cotangent.reshape(rows, width)
    outs = forward(
        [hidden, upstream, w_up, w_down.T, ln_gain[None], ln_shift[None], w_qkv.transpose(1, 0, 2), b_qkv, w_dense.T]
        + [b_up[None], segments, keep_mask, *tables],
        0,
    )
    heads_w = [outs[u].reshape(2048, 1024) for u in (0, 1, PARTS - 1)]
    in_t, up_t, pairs, od_in, dkv_in, inputs, share, d_share, bias_up = outs[PARTS:]
    input_grad, _, summed, done, vectors = backward(
        [od_in, dkv_in, upstream, hidden, in_t, up_t, pairs, *heads_w, inputs, share, d_share, bias_up]
        + [b_up[None], ln_gain[None], *tables],
        1,
    )
    block_out, input_grad, grad_qkv, grad_dense, grad_up, grad_down, gain, shift, out, up, grad_bqkv, out2 = finish(
        hidden, summed, b_dense[None], b_down[None], input_grad, done, vectors
    )
    return (
        block_out.reshape(3, 128, width),
        input_grad.reshape(3, 128, width),
        gain,
        shift,
        grad_qkv.transpose(1, 0, 2),
        grad_bqkv,
        grad_dense.T,
        out,
        grad_up,
        up,
        grad_down.T,
        out2,
    )


def solution(mesh):
    return jax.shard_map(
        local,
        mesh=mesh,
        in_specs=(
            P("dp", "seq", None),
            P("dp", "seq"),
            P("dp", "seq"),
            P(),
            P(),
            P(("dp", "seq"), None, "tp"),
            P(None, "tp"),
            P("tp", ("dp", "seq")),
            P(),
            P(("dp", "seq"), "tp"),
            P("tp"),
            P("tp", ("dp", "seq")),
            P(),
            P("dp", "seq", None),
        ),
        out_specs=(
            P("dp", "seq", None),
            P("dp", "seq", None),
            P(),
            P(),
            P(("dp", "seq"), None, "tp"),
            P(None, "tp"),
            P("tp", ("dp", "seq")),
            P(),
            P(("dp", "seq"), "tp"),
            P("tp"),
            P("tp", ("dp", "seq")),
            P(),
        ),
        check_vma=False,
    )
```

```python
import functools

import jax
import jax.numpy as jnp
import numpy as np
from jax import lax
from jax.experimental import pallas as pl
from jax.experimental.pallas import tpu as pltpu
from jax.sharding import PartitionSpec as P

MESH = pl.DeviceIdType.MESH
HD = 64
ROT = 32
WINDOW = 1024
BF = jnp.bfloat16
F32 = jnp.float32
ANY = pl.BlockSpec(memory_space=pl.ANY)
VMEM = pl.BlockSpec(memory_space=pltpu.VMEM)


def wrap(v):
    return lax.rem(v + 4, 4)


def place():
    dp, sq, tp = lax.axis_index("dp"), lax.axis_index("seq"), lax.axis_index("tp")
    return dp * 2 + sq // 8, lax.rem(sq // 2, 4), lax.rem(sq, 2), tp


def device(z, x, c, y):
    z, x, y = wrap(z), wrap(x), wrap(y)
    return {"dp": z // 2, "seq": lax.rem(z, 2) * 8 + x * 2 + c, "tp": y}


class Net:
    def __init__(self, send, recv):
        self.send, self.recv, self.n, self.out, self.keys = send, recv, 0, {}, {}
        self.z, self.x, self.c, self.y = place()
        self.flip = 1 - 2 * lax.rem(self.z, 2)
        self.chip = lax.rem(self.z, 2) * 4 + self.x

    def to(self, axis, way):
        z, x, c, y = self.z, self.x, self.c, self.y
        if axis == "s":
            return device(z, x, 1 - c, y)
        if axis == "x":
            return device(z, x + way, c, y)
        if axis == "z":
            return device(z + way, x, c, y)
        if axis == "y":
            return device(z, x, c, y + way)
        return device(z + axis * self.flip, x + way, c, y)

    def greet(self, targets):
        bar = pltpu.get_barrier_semaphore()
        for axis, way in targets:
            pl.semaphore_signal(bar, inc=1, device_id=self.to(axis, way), device_id_type=MESH)
        pl.semaphore_wait(bar, len(targets))

    def chip_at(self, dz, dx):
        return lax.rem(lax.rem(self.z, 2) + dz, 2) * 4 + wrap(self.x + dx)

    def push(self, key, src, dst, axis, way):
        k = self.n
        self.n += 1
        copy = pltpu.make_async_remote_copy(
            src_ref=src,
            dst_ref=dst,
            send_sem=self.send.at[k],
            recv_sem=self.recv.at[k],
            device_id=self.to(axis, way),
            device_id_type=MESH,
        )
        copy.start()
        self.out[key] = copy
        self.keys[key] = copy

    def arrived(self, key):
        self.keys.pop(key).wait_recv()

    def sent(self, key):
        self.out.pop(key).wait_send()

    def settle(self, keep=0):
        for key in list(self.out)[: len(self.out) - keep]:
            self.sent(key)

    def drain(self):
        for key in list(self.out):
            self.sent(key)
        for key in list(self.keys):
            self.arrived(key)


def lanes(chip):
    return pl.ds(pl.multiple_of(chip * 128, 128), 128)


def dot(a, b, dims):
    return lax.dot_general(a, b, (dims, ((), ())), preferred_element_type=F32)


def span(start, size, unit=128):
    return pl.ds(pl.multiple_of(start, unit), size)


RING_XZ = (("x", 1), ("x", -1), ("z", 1), ("z", -1), ("s", 1))
RING_Y = (("y", 1), ("y", -1))
FAR = (("x", 2), ("z", 2), ("y", 2))
FARTHER = ((1, 1), (1, 2), (1, 3))
OTHERS = tuple((dz, dx) for dz in (1, 0) for dx in (2, 1, 3, 0) if dz or dx)
PARTS = 6
TILES = 4
EARLY = 3
LOW, HIGH, ALL = pl.ds(0, 512), pl.ds(512, 512), pl.ds(0, 1024)


class Gather:
    def __init__(self, net, name, src, dst):
        self.net, self.name, self.src, self.dst = net, name, src, dst
        self.half, self.quarter = src.shape[0] // 2, src.shape[0] // 4

    def axes(self, h):
        return ("x", "z") if h == 0 else ("z", "x")

    def block(self, h, a, r0, rn):
        n, rows = self.net, pl.ds(h * self.half + r0, rn)
        if h == 0:
            return self.dst.at[n.z, wrap(n.x + a), n.c, rows]
        return self.dst.at[wrap(n.z + a), n.x, n.c, rows]

    def line(self, h, b, r0, rn):
        n, rows = self.net, pl.ds(h * self.half + r0, rn)
        if h == 0:
            return self.dst.at[wrap(n.z + b), :, n.c, rows]
        return self.dst.at[:, wrap(n.x + b), n.c, rows]

    def begin(self, sem):
        n = self.net
        for h in (0, 1):
            own = self.src.at[pl.ds(h * self.half, self.half)]
            for w in (1, -1):
                n.push((self.name, h, "A", w), own, self.block(h, 0, 0, self.half), self.axes(h)[0], w)
        self.local = pltpu.make_async_copy(self.src, self.dst.at[n.z, n.x, n.c], sem)
        self.local.start()

    def near(self):
        n = self.net
        for h in (0, 1):
            for w in (1, -1):
                n.arrived((self.name, h, "A", w))
                part = self.block(h, -w, 0 if w == 1 else self.quarter, self.quarter)
                n.push((self.name, h, "AF", w), part, part, self.axes(h)[0], w)

    def far(self):
        n = self.net
        self.local.wait()
        for h in (0, 1):
            for w in (1, -1):
                n.arrived((self.name, h, "AF", w))
            line = self.line(h, 0, 0, self.half)
            for w in (1, -1):
                n.push((self.name, h, "B", w), line, line, self.axes(h)[1], w)
            n.push((self.name, h, "s", 0), line, line, "s", 1)

    def pass_on(self):
        n = self.net
        for h in (0, 1):
            for w in (1, -1):
                n.arrived((self.name, h, "B", w))
                part = self.line(h, -w, 0 if w == 1 else self.quarter, self.quarter)
                n.push((self.name, h, "BF", w), part, part, self.axes(h)[1], w)
                line = self.line(h, -w, 0, self.half)
                n.push((self.name, h, "s", -w), line, line, "s", 1)

    def close(self):
        n = self.net
        for h in (0, 1):
            for w in (1, -1):
                n.arrived((self.name, h, "BF", w))
            line = self.line(h, 2, 0, self.half)
            n.push((self.name, h, "s", 2), line, line, "s", 1)

    def landed(self):
        for h in (0, 1):
            for b in (0, -1, 1, 2):
                self.net.arrived((self.name, h, "s", b))


class FineGather:
    def __init__(self, net, name, src, dst):
        self.net, self.name, self.src, self.dst = net, name, src, dst
        self.half, self.quarter = src.shape[0] // 2, src.shape[0] // 4

    def at(self, h, a, b, r0, rn):
        n = self.net
        z, x = (n.z + b, n.x + a) if h == 0 else (n.z + a, n.x + b)
        return self.dst.at[wrap(z), wrap(x), n.c, pl.ds(h * self.half + r0, rn)]

    def own(self, h):
        return self.src.at[pl.ds(h * self.half, self.half)]

    def axes(self, h):
        return ("x", "z") if h == 0 else ("z", "x")

    def begin(self, sem):
        n = self.net
        for h in (0, 1):
            for w in (1, -1):
                n.push((self.name, h, "A", w), self.own(h), self.at(h, 0, 0, 0, self.half), self.axes(h)[0], w)
        for h in (0, 1):
            for w in (1, -1):
                n.push((self.name, h, "B", 0, w), self.own(h), self.at(h, 0, 0, 0, self.half), self.axes(h)[1], w)
        whole = self.dst.at[n.z, n.x, n.c]
        n.push((self.name, "s"), self.src, whole, "s", 1)
        self.local = pltpu.make_async_copy(self.src, whole, sem)
        self.local.start()

    def spread(self, h, a):
        n = self.net
        block = self.at(h, a, 0, 0, self.half)
        for w in (1, -1):
            n.push((self.name, h, "B", a, w), block, block, self.axes(h)[1], w)
        n.push((self.name, h, "s", a, 0), block, block, "s", 1)

    def near(self):
        n = self.net
        for h in (0, 1):
            for w in (1, -1):
                n.arrived((self.name, h, "A", w))
                part = self.at(h, -w, 0, 0 if w == 1 else self.quarter, self.quarter)
                n.push((self.name, h, "AF", w), part, part, self.axes(h)[0], w)
                self.spread(h, -w)

    def far(self):
        for h in (0, 1):
            for w in (1, -1):
                self.net.arrived((self.name, h, "AF", w))
            self.spread(h, 2)

    def pass_on(self, a):
        n = self.net
        for h in (0, 1):
            for w in (1, -1):
                n.arrived((self.name, h, "B", a, w))
                part = self.at(h, a, -w, 0 if w == 1 else self.quarter, self.quarter)
                n.push((self.name, h, "BF", a, w), part, part, self.axes(h)[1], w)
                block = self.at(h, a, -w, 0, self.half)
                n.push((self.name, h, "s", a, -w), block, block, "s", 1)

    def close(self, a):
        n = self.net
        for h in (0, 1):
            for w in (1, -1):
                n.arrived((self.name, h, "BF", a, w))
            block = self.at(h, a, 2, 0, self.half)
            n.push((self.name, h, "s", a, 2), block, block, "s", 1)

    def landed(self):
        n = self.net
        self.local.wait()
        n.arrived((self.name, "s"))
        for h in (0, 1):
            for a in (-1, 1, 2):
                n.arrived((self.name, h, "s", a, 0))
            for a in (0, -1, 1, 2):
                for b in (-1, 1, 2):
                    n.arrived((self.name, h, "s", a, b))


def gelu_both(v, d):
    k = 0.7978845608028654
    square = v * v
    t = jnp.tanh(k * v * (1.0 + 0.044715 * square))
    half = 0.5 * (1.0 + t)
    slope = half + 0.5 * v * (1.0 - t * t) * (k * (1.0 + 0.134145 * square))
    return (d * slope).astype(BF), (v * half).astype(BF)


def fill_tables(tables, near_cos, near_sin, base_cos, base_sin):
    own = pl.ds(lax.axis_index("seq"), 1)
    cosine, sine = base_cos[own], base_sin[own]
    place_in = lax.rem(lax.broadcasted_iota(jnp.int32, (128, 128), 1), HD)
    tables[0][...] = near_cos[...] * cosine - near_sin[...] * sine
    total = near_sin[...] * cosine + near_cos[...] * sine
    tables[1][...] = jnp.where(place_in < ROT // 2, total, 0.0)
    tables[2][...] = jnp.where(place_in < ROT // 2, 0.0, total)


def turn(tensor, tables, sign):
    cosine, low, high = tables
    moved = pltpu.roll(tensor, 16, 1) * high[...] - pltpu.roll(tensor, 112, 1) * low[...]
    return tensor * cosine[...] + sign * moved


class Scatter:
    def __init__(self, net, name, acc, far1, near1, far2, near2, out):
        self.net, self.name, self.acc = net, name, acc
        self.far1, self.near1, self.far2, self.near2, self.out = far1, near1, far2, near2, out

    def axes(self, h):
        return ("z", "x") if h == 0 else ("x", "z")

    def first(self, h, d, r0, rn):
        n, rows = self.net, pl.ds(h * 32 + r0, rn)
        if h == 0:
            return self.acc.at[wrap(n.z + d), :, rows]
        return self.acc.at[:, wrap(n.x + d), rows]

    def second(self, h, d, r0, rn):
        n, rows = self.net, pl.ds(h * 32 + r0, rn)
        if h == 0:
            return self.acc.at[n.z, wrap(n.x + d), rows]
        return self.acc.at[wrap(n.z + d), n.x, rows]

    def step2(self):
        n = self.net
        for h in (0, 1):
            for k, w in ((0, -1), (1, 1)):
                n.push((self.name, h, "f1", w), self.first(h, 2, 16 * k, 16), self.far1.at[h, k], self.axes(h)[0], w)

    def step3(self):
        n = self.net
        for h in (0, 1):
            for k, w in ((0, -1), (1, 1)):
                n.arrived((self.name, h, "f1", w))
                part = self.first(h, w, 16 * k, 16)

                def add(t, carry):
                    part[t] = part[t] + self.far1[h, k, t]
                    return carry

                lax.fori_loop(0, 4, add, 0)
                n.push((self.name, h, "n1", w), self.first(h, w, 0, 32), self.near1.at[h, k], self.axes(h)[0], w)

    def step4(self):
        n = self.net
        for h in (0, 1):
            n.arrived((self.name, h, "n1", -1))
            n.arrived((self.name, h, "n1", 1))
            part = self.first(h, 0, 0, 32)

            def add(t, carry):
                for r in (0, 16):
                    rows = pl.ds(r, 16)
                    value = part[t, rows].astype(F32) + self.near1[h, 0, t, rows].astype(F32)
                    part[t, rows] = (value + self.near1[h, 1, t, rows].astype(F32)).astype(BF)
                return carry

            lax.fori_loop(0, 4, add, 0)
            for k, w in ((0, -1), (1, 1)):
                n.push((self.name, h, "f2", w), self.second(h, 2, 16 * k, 16), self.far2.at[h, k], self.axes(h)[1], w)

    def step5(self):
        n = self.net
        for h in (0, 1):
            for k, w in ((0, -1), (1, 1)):
                n.arrived((self.name, h, "f2", w))
                part = self.second(h, w, 16 * k, 16)
                part[...] = part[...] + self.far2[h, k]
                n.push((self.name, h, "n2", w), self.second(h, w, 0, 32), self.near2.at[h, k], self.axes(h)[1], w)

    def step6(self):
        n = self.net
        for h in (0, 1):
            n.arrived((self.name, h, "n2", -1))
            n.arrived((self.name, h, "n2", 1))
            part = self.second(h, 0, 0, 32)
            for r in (0, 16):
                rows = pl.ds(r, 16)
                value = part[rows].astype(F32) + self.near2[h, 0, rows].astype(F32)
                self.out[pl.ds(h * 32 + r, 16)] = value + self.near2[h, 1, rows].astype(F32)


class Sum:
    def __init__(self, net, name, acc, far, near, out):
        self.net, self.name, self.acc = net, name, acc
        self.far, self.near, self.out = far, near, out

    def block(self, d, r0, rn):
        start = pl.multiple_of(wrap(self.net.y + d) * 192 + r0, 16)
        return self.acc.at[pl.ds(start, rn)]

    def step1(self, value):
        n = self.net

        def fill(d, carry):
            for half in (0, 1):
                rows = pl.ds(pl.multiple_of(d * 192 + half * 96, 16), 96)
                held = value[pl.ds(pl.multiple_of(d * 96, 16), 96), pl.ds(half * 1024, 1024)]
                self.acc[rows] = held.astype(BF)
            return carry

        lax.fori_loop(0, 4, fill, 0)
        for k, w in ((0, -1), (1, 1)):
            n.push((self.name, "f", w), self.block(2, 96 * k, 96), self.far.at[k], "y", w)

    def step2(self):
        n = self.net
        for k, w in ((0, -1), (1, 1)):
            n.arrived((self.name, "f", w))
            part = self.block(w, 96 * k, 96)
            part[...] = part[...] + self.far[k]
            n.push((self.name, "n", w), self.block(w, 0, 192), self.near.at[k], "y", w)

    def step3(self, sem):
        n = self.net
        n.arrived((self.name, "n", -1))
        n.arrived((self.name, "n", 1))
        part = self.block(0, 0, 192)

        def add(t, carry):
            rows = pl.ds(pl.multiple_of(t * 16, 16), 16)
            value = part[rows].astype(F32) + self.near[0, rows].astype(F32)
            part[rows] = (value + self.near[1, rows].astype(F32)).astype(BF)
            return carry

        lax.fori_loop(0, 12, add, 0)
        for w in (-1, 1):
            n.push((self.name, "g", w), part, self.out.at[n.y], "y", w)
        self.last = pltpu.make_async_copy(part, self.out.at[n.y], sem)
        self.last.start()

    def step4(self):
        n = self.net
        for k, w in ((0, -1), (1, 1)):
            n.arrived((self.name, "g", w))
            part = self.out.at[wrap(n.y - w), pl.ds(96 * k, 96)]
            n.push((self.name, "gf", w), part, part, "y", w)

    def step5(self):
        self.last.wait()
        for w in (-1, 1):
            self.net.arrived((self.name, "gf", w))


def vector_sum(net, src, pairs, alongx, alongz, alongy, out):
    z, x, c, y = net.z, net.x, net.c, net.y
    pairs[c] = src[...]
    net.push("vs", pairs.at[c], pairs.at[c], "s", 1)
    yield
    net.arrived("vs")
    alongx[x] = pairs[0] + pairs[1]
    for w in (1, -1, 2):
        net.push(("vx", w), alongx.at[x], alongx.at[x], "x", w)
    yield
    for w in (1, -1, 2):
        net.arrived(("vx", w))
    alongz[z] = (alongx[0] + alongx[1]) + (alongx[2] + alongx[3])
    for w in (1, -1, 2):
        net.push(("vz", w), alongz.at[z], alongz.at[z], "z", w)
    yield
    for w in (1, -1, 2):
        net.arrived(("vz", w))
    alongy[y] = (alongz[0] + alongz[1]) + (alongz[2] + alongz[3])
    out[...] = alongy[y]
    for w in (1, -1, 2):
        net.push(("vy", w), alongy.at[y], alongy.at[y], "y", w)
    yield
    for w in (1, -1, 2):
        net.arrived(("vy", w))
    out[0:2] = (alongy[0, 0:2] + alongy[1, 0:2]) + (alongy[2, 0:2] + alongy[3, 0:2])
    yield


def halves(a, b, left):
    return jnp.where(left, a, pltpu.roll(b, 64, 1)), jnp.where(left, pltpu.roll(a, 64, 1), b)


def front_kernel(
    hidden_in, upstream_in, w_up_in, w_down_in, gain, shift, w_qkv, b_qkv, w_dense, b_up, segments, keep,
    near_cos, near_sin, base_cos, base_sin, *refs,
):
    gathered, refs = refs[:PARTS], refs[PARTS:]
    in_t, up_t, pairs, od_in, dkv_in, inputs_out, share_out, d_share_out, bias_up, refs = *refs[:9], refs[9:]
    shards, inputs, staged, kept, weights, qd, kv, qd_all, kv_all, info_all, seen, total, refs = *refs[:12], refs[12:]
    od, dkv, theirs, ours, pair, share, d_share, hidden, upstream, w_up, w_down, info, refs = *refs[:12], refs[12:]
    t_cos, t_low, t_high, send, recv, loc = refs
    net = Net(send, recv)
    me, c = net.chip, net.c
    tables = (t_cos, t_low, t_high)
    lane = lax.broadcasted_iota(jnp.int32, (128, 128), 1)
    row = lax.broadcasted_iota(jnp.int32, (128, 128), 0)
    left = lane < 64
    mine = span(c * 384, 384)
    sems = iter(range(60))

    def here(src, dst):
        copy = pltpu.make_async_copy(src, dst, loc.at[next(sems)])
        copy.start()
        return copy

    reads = [here(a, b) for a, b in ((hidden_in, hidden), (upstream_in, upstream), (w_up_in, w_up), (w_down_in, w_down))]

    for k in range(4):
        columns = pl.ds(k * 128, 128)
        pieces = halves(w_qkv[1, :, columns], w_qkv[2, :, columns], left[:64])
        for j in (0, 1):
            shards[0, :, pl.ds(256 * k + 128 * j, 128)] = pieces[j].astype(BF)
    net.greet(RING_XZ + FARTHER + (("x", 2),))
    parts = [(FineGather if u < 2 else Gather)(net, u, shards.at[u], gathered[u]) for u in range(PARTS)]
    parts[0].begin(loc.at[next(sems)])
    shards[1, :, LOW] = w_qkv[0].astype(BF)
    shards[1, :, HIGH] = w_dense[...].astype(BF)
    parts[1].begin(loc.at[next(sems)])
    fill_tables(tables, near_cos, near_sin, base_cos, base_sin)
    info[0:3] = jnp.where(keep[...] > 0, segments[...], -1)
    info[3:6] = segments[...]
    info[6:8] = jnp.zeros((2, 128), jnp.int32)

    def norm(t, carry):
        rows = span(t * 16, 16, 16)
        value = hidden[rows].astype(F32)
        value = value - jnp.mean(value, axis=1, keepdims=True)
        value = value * lax.rsqrt(jnp.mean(value * value, axis=1, keepdims=True) + 1e-05)
        inputs[rows] = (value * gain[...] + shift[...]).astype(BF)
        return carry

    reads[0].wait()
    lax.fori_loop(0, 24, norm, 0)

    def transpose(t, carry):
        columns, rows = span(t * 128, 128), span(t * 64, 64, 64)
        for k, src in enumerate((inputs, upstream)):
            tile = src[:, columns].T
            first, second = tile[:64], tile[64:]
            kept[k, rows] = jnp.where(c == 0, first, second)
            staged[k, rows] = jnp.where(c == 0, second, first)
        return carry

    stays = [here(inputs, inputs_out)]

    def factors():
        lax.fori_loop(0, 16, transpose, 0)
        for k, dst in enumerate((in_t, up_t)):
            stays.append(here(kept.at[k], dst.at[c]))
            net.push(("t", k), staged.at[k], dst.at[c], "s", 1)

    def load(u):
        parts[u].landed()
        return here(gathered[u], weights.at[u % 4].reshape(4, 4, 2, 64, 1024))

    first, second = parts[:2]
    first.near()
    first.pass_on(0)
    second.near()
    first.far()
    second.pass_on(0)
    reads[2].wait()
    reads[3].wait()
    for u in range(TILES):
        shards[2 + u, :, LOW] = w_up[:, pl.ds(u * 512, 512)].astype(BF)
        shards[2 + u, :, HIGH] = w_down[:, pl.ds(u * 512, 512)].astype(BF)
    first.pass_on(-1)
    first.pass_on(1)
    second.far()
    parts[2].begin(loc.at[next(sems)])
    first.pass_on(2)
    first.close(0)
    second.pass_on(-1)
    second.pass_on(1)
    parts[3].begin(loc.at[next(sems)])
    for a in (-1, 1, 2):
        first.close(a)
    second.pass_on(2)
    parts[2].near()
    parts[3].near()
    loads = {0: load(0)}
    second.close(0)
    second.close(-1)
    parts[4].begin(loc.at[next(sems)])
    parts[5].begin(loc.at[next(sems)])
    parts[2].far()

    loads[0].wait()

    def keys_values(h, carry):
        columns = span(h * 256, 256)
        value = dot(inputs[...], weights[0, :, columns], ((1,), (0,)))
        bk, bv = b_qkv[1:2, span(h * 128, 128)], b_qkv[2:3, span(h * 128, 128)]
        bias = halves(bk, bv, left[:1])
        for j in (0, 1):
            tile = value[:, 128 * j : 128 * j + 128] + bias[j]
            for s in range(3):
                piece = tile[128 * s : 128 * s + 128]
                kv[s, :, span(h * 256 + 128 * j, 128)] = jnp.where(left, turn(piece, tables, 1.0), piece).astype(BF)
        return carry

    lax.fori_loop(0, 4, keys_values, 0)
    pairs_of = kv_all.reshape(3, 8, 2, 128, 128)
    for dz, dx in OTHERS:
        net.push(("i", dz, dx), info, info_all.at[2 * me + c], dz, dx)
    for s in range(3):
        for dz, dx in OTHERS:
            net.push(("k", s, dz, dx), kv.at[s, :, lanes(net.chip_at(dz, dx))], kv_all.at[s, 2 * me + c], dz, dx)
        stays.append(here(kv.at[s, :, lanes(me)], kv_all.at[s, 2 * me + c]))
    stays.append(here(info, info_all.at[2 * me + c]))
    second.close(1)
    second.close(2)
    loads[1] = load(1)
    reads[1].wait()
    loads[1].wait()

    def queries(h, carry):
        columns = span(h * 128, 128)
        q = dot(inputs[...], weights[1, :, columns], ((1,), (0,))) + b_qkv[0:1, columns]
        d = dot(upstream[...], weights[1, :, span(512 + h * 128, 128)], ((1,), (0,)))
        for s in range(3):
            pieces = halves(turn(q[128 * s : 128 * s + 128], tables, 1.0), d[128 * s : 128 * s + 128], left)
            for j in (0, 1):
                qd[s, :, span(h * 256 + 128 * j, 128)] = pieces[j].astype(BF)
        return carry

    lax.fori_loop(0, 4, queries, 0)
    for s in range(3):
        for dz, dx in OTHERS:
            net.push(("q", s, dz, dx), qd.at[s, :, lanes(net.chip_at(dz, dx))], qd_all.at[me, s], dz, dx)
        stays.append(here(qd.at[s, :, lanes(me)], qd_all.at[me, s]))

    def units(u):
        slot = (2 + u) % 4
        loads[2 + u].wait()

        def some(j, carry):
            low, high = span(j * 256, 256), span(512 + j * 256, 256)
            unit = span(u * 512 + j * 256, 256)
            v = dot(inputs[...], weights[slot, :, low], ((1,), (0,))) + b_up[:, unit]
            d = dot(upstream[...], weights[slot, :, high], ((1,), (0,)))
            d_up, active = gelu_both(v, d)
            pair[u, :, low] = d_up
            pair[u, :, high] = active
            bias_up[:, unit] = jnp.sum(d_up.astype(F32), axis=0, keepdims=True)
            return carry

        lax.fori_loop(0, 2, some, 0)
        net.push(("p", u), pair.at[u], pairs.at[u, mine], "s", 1)
        stays.append(here(pair.at[u], pairs.at[u, mine]))
        for total_ref, columns in ((d_share, LOW), (share, HIGH)):
            value = pair[u, :, columns]

            def spread(j, carry):
                rows = span(j * 512, 512)
                added = dot(value, weights[slot, rows, columns], ((1,), (1,)))
                if u == 0:
                    total_ref[:, rows] = added
                else:
                    total_ref[:, rows] += added
                return carry

            lax.fori_loop(0, 4, spread, 0)
            if u == EARLY - 1:
                stays.append(here(total_ref, share_out if total_ref is share else d_share_out))

    def attend(s, i, blocks, own, first):
        width = blocks * 128
        begin = first * 128 if isinstance(first, int) else pl.multiple_of(first * 128, 128)
        tile = qd_all[i, s].astype(F32)
        both_halves = [jnp.where(left, tile * (HD**-0.5), 0.0), jnp.where(left, 0.0, tile)]
        asking = jnp.concatenate(both_halves, axis=0).astype(BF)
        keys = kv_all[s, pl.ds(first, blocks)].reshape(width, 128)
        both = dot(asking, keys, ((1,), (1,)))
        asked = jnp.broadcast_to(info_all[own, pl.ds(3 + s, 1), :].astype(F32), (128, 128)).T
        held = seen[pl.ds(s, 1), pl.ds(begin, width)].astype(F32)
        pieces = []
        for b in range(blocks):
            fits = asked == held[:, b * 128 : (b + 1) * 128]
            if isinstance(first, int):
                if b >= blocks - 2:
                    ahead = lane + (b * 128 - own * 128) - row
                    fits = (fits | (ahead == 0)) & (ahead <= 0)
            elif b == blocks - 1:
                fits = (fits | (lane == row)) & (lane <= row)
            elif b == 0:
                fits = fits & (lane > row)
            pieces.append(jnp.where(fits, both[:128, b * 128 : (b + 1) * 128], -1e30))
        scores = jnp.concatenate(pieces, axis=1)
        expo = jnp.exp(scores - jnp.max(scores, axis=1, keepdims=True))
        probs = expo * (1.0 / jnp.sum(expo, axis=1, keepdims=True))
        d_probs = both[128:]
        delta = jnp.sum(probs * d_probs, axis=1, keepdims=True)
        mixed = jnp.concatenate([(probs * (d_probs - delta)).astype(BF), probs.astype(BF)], axis=0)
        back = dot(mixed, keys, ((1,), (0,)))
        od[i, s] = jnp.where(left, back[:128] * (HD**-0.5), back[128:]).astype(BF)
        total[pl.ds(begin, width)] += dot(mixed, asking, ((0,), (0,)))

    def early(s):
        total[...] = jnp.zeros_like(total)
        for i in range(4):
            attend(s, i, 2 * i + 2, 2 * i + c, 0)

    def late(s):
        def some(i, carry):
            attend(s, i, 9, 2 * i + c, 2 * i + c - 8)
            return carry

        lax.fori_loop(4, 8, some, 0)
        dkv[s] = total[...].astype(BF).reshape(8, 2, 128, 128)

    def relay(s):
        for dz, dx in OTHERS:
            net.arrived(("k", s, dz, dx))
        held = pairs_of.at[s, :, c]
        net.push(("ks", s), held, held, "s", 1)

    def ready(s):
        net.arrived(("ks", s))
        for dz, dx in OTHERS:
            net.arrived(("q", s, dz, dx))

    def give(s):
        net.push(("b", s), dkv.at[s, :, 1 - c], theirs.at[s], "s", 1)
        stays.append(here(od.at[me, s], od_in.at[s, :, lanes(me)]))
        for dz, dx in OTHERS:
            net.push(("o", s, dz, dx), od.at[net.chip_at(dz, dx), s], od_in.at[s, :, lanes(me)], dz, dx)

    def give_more(s):
        net.arrived(("b", s))
        ours[s] = dkv[s, :, c] + theirs[s]
        for dz, dx in OTHERS:
            net.push(("d", s, dz, dx), ours.at[s, net.chip_at(dz, dx)], dkv_in.at[s, :, lanes(me)], dz, dx)
        stays.append(here(ours.at[s, me], dkv_in.at[s, :, lanes(me)]))

    parts[4].near()
    parts[5].near()
    factors()
    parts[2].pass_on()
    for copy in stays:
        copy.wait()
    stays.clear()
    for dz, dx in OTHERS:
        net.arrived(("i", dz, dx))
    held_info = info_all.reshape(8, 2, 8, 128).at[:, c]
    net.push("is", held_info, held_info, "s", 1)
    relay(0)
    relay(1)
    relay(2)
    net.arrived("is")
    for b in range(16):
        seen[:, b * 128 : (b + 1) * 128] = info_all[b]
    parts[3].far()
    parts[2].close()
    net.settle(60)
    ready(0)
    early(0)
    parts[3].pass_on()
    late(0)
    give(0)
    parts[4].far()
    loads[2] = load(2)
    units(0)
    net.settle(50)
    ready(1)
    parts[3].close()
    early(1)
    parts[4].pass_on()
    give_more(0)
    parts[5].far()
    late(1)
    give(1)
    loads[3] = load(3)
    units(1)
    net.settle(50)
    ready(2)
    parts[4].close()
    early(2)
    parts[5].pass_on()
    give_more(1)
    late(2)
    give(2)
    loads[4] = load(4)
    net.settle(40)
    parts[5].close()
    give_more(2)
    units(2)
    parts[5].landed()
    for copy in stays:
        copy.wait()
    net.drain()


def forward(args, cid):
    big = jax.ShapeDtypeStruct((4, 4, 2, 64, 1024), BF)
    factor = jax.ShapeDtypeStruct((2, 1024, 384), BF)
    heads = jax.ShapeDtypeStruct((3, 128, 1024), BF)
    wide = jax.ShapeDtypeStruct((384, 2048), F32)
    return pl.pallas_call(
        front_kernel,
        out_shape=[big] * PARTS
        + [factor, factor, jax.ShapeDtypeStruct((EARLY, 768, 1024), BF), heads, heads]
        + [jax.ShapeDtypeStruct((384, 2048), BF)]
        + [wide, wide, jax.ShapeDtypeStruct((1, 2048), F32)],
        in_specs=[ANY] * 4 + [VMEM] * (len(args) - 4),
        out_specs=[ANY] * (PARTS + 8) + [VMEM],
        scratch_shapes=[
            pltpu.VMEM((PARTS, 64, 1024), BF),
            pltpu.VMEM((384, 2048), BF),
            pltpu.VMEM((2, 1024, 384), BF),
            pltpu.VMEM((2, 1024, 384), BF),
            pltpu.VMEM((4, 2048, 1024), BF),
            pltpu.VMEM((3, 128, 1024), BF),
            pltpu.VMEM((3, 128, 1024), BF),
            pltpu.VMEM((8, 3, 128, 128), BF),
            pltpu.VMEM((3, 16, 128, 128), BF),
            pltpu.VMEM((16, 8, 128), jnp.int32),
            pltpu.VMEM((8, 2048), jnp.int32),
            pltpu.VMEM((2048, 128), F32),
            pltpu.VMEM((8, 3, 128, 128), BF),
            pltpu.VMEM((3, 8, 2, 128, 128), BF),
            pltpu.VMEM((3, 8, 128, 128), BF),
            pltpu.VMEM((3, 8, 128, 128), BF),
            pltpu.VMEM((EARLY, 384, 1024), BF),
            pltpu.VMEM((384, 2048), F32),
            pltpu.VMEM((384, 2048), F32),
            pltpu.VMEM((384, 2048), BF),
            pltpu.VMEM((384, 2048), BF),
            pltpu.VMEM((64, 2048), F32),
            pltpu.VMEM((64, 2048), F32),
            pltpu.VMEM((8, 128), jnp.int32),
            pltpu.VMEM((128, 128), F32),
            pltpu.VMEM((128, 128), F32),
            pltpu.VMEM((128, 128), F32),
            pltpu.SemaphoreType.DMA((370,)),
            pltpu.SemaphoreType.DMA((370,)),
            pltpu.SemaphoreType.DMA((60,)),
        ],
        compiler_params=pltpu.CompilerParams(
            collective_id=cid, has_side_effects=True, vmem_limit_bytes=62 * 2**20
        ),
        name="forward",
    )(*args)


def back_kernel(
    od_any, dkv_any, upstream_any, hidden_any, in_t, up_t, pairs, heads_w0, heads_w1, last_w,
    inputs_any, share_in, d_share_in, bias_up, b_up, gain, near_cos,
    near_sin, base_cos, base_sin, input_grad, sum0, sum1, done, vec_out, *refs,
):
    accs, refs = refs[:PARTS], refs[PARTS:]
    far1, near1, far2, near2, refs = *refs[:4], refs[4:]
    weights, pair, factors, share, d_share, od_in, dkv_in, upstream, hidden, inputs, refs = *refs[:10], refs[10:]
    y_far, y_near, vecs, vec_acc, cores, alongx, alongz, alongy, t_cos, t_low, t_high, send, recv, loc = refs
    net = Net(send, recv)
    c = net.c
    tables = (t_cos, t_low, t_high)
    left = lax.broadcasted_iota(jnp.int32, (128, 128), 1) < 64
    mine = span(c * 384, 384)
    sems = iter(range(40))

    def here(src, dst):
        copy = pltpu.make_async_copy(src, dst, loc.at[next(sems)])
        copy.start()
        return copy

    factor_loads = [here(src.at[k], factors.at[j, :, pl.ds(384 * k, 384)]) for j, src in enumerate((in_t, up_t)) for k in (0, 1)]
    pair_loads = {0: here(pairs.at[0], pair.at[0])}
    head_loads = [here(od_any, od_in), here(dkv_any, dkv_in)]
    unit_loads = [here(last_w, weights.at[0]), here(inputs_any, inputs), here(upstream_any, upstream)]
    pair_loads[1] = here(pairs.at[1], pair.at[1])
    share_loads = [here(d_share_in, d_share), here(share_in, share)]
    weight_loads = [here(heads_w1, weights.at[1])]
    row_loads = [here(hidden_any, hidden)]
    net.greet(RING_XZ + RING_Y + FAR)
    parts = [
        Scatter(net, ("g", i), accs[i], far1.at[i], near1.at[i], far2.at[i], near2.at[i], done.at[i])
        for i in range(PARTS)
    ]

    fill_tables(tables, near_cos, near_sin, base_cos, base_sin)

    def rows_of(s, carry):
        own = span(c * 384 + s * 128, 128)
        for h in range(8):
            columns = pl.ds(h * 128, 128)
            value = dkv_in[s, :, columns].astype(F32)
            pair[2, own, columns] = jnp.where(left, turn(value, tables, -1.0), value).astype(BF)
        for h in range(4):
            a = od_in[s, :, 256 * h : 256 * h + 128].astype(F32)
            b = od_in[s, :, 256 * h + 128 : 256 * h + 256].astype(F32)
            asked, got = halves(a, b, left)
            pair[3, own, pl.ds(h * 128, 128)] = turn(asked, tables, -1.0).astype(BF)
            pair[3, own, pl.ds(512 + h * 128, 128)] = got.astype(BF)
        return carry

    def heads():
        for copy in head_loads:
            copy.wait()
        lax.fori_loop(0, 3, rows_of, 0)
        for slot in (2, 3):
            rows = pair.at[slot, mine]
            net.push(("p", slot), rows, rows, "s", 1)

    def gradients(u, slot, first_t, second_t):
        acc = accs[u]

        def some(z, carry):
            rows = span(z * 256, 256)
            for k, j in enumerate((first_t, second_t)):
                columns = pl.ds(k * 512, 512)
                value = dot(factors[j, rows], pair[slot, :, columns], ((1,), (0,)))
                acc[z, :, :, columns] = value.astype(BF).reshape(4, 64, 512)
            return carry

        lax.fori_loop(0, 4, some, 0)
        parts[u].step2()

    def tile(u):
        pair_loads[u].wait()
        gradients(u, u % 2, 0, 1)
        if u + 2 < EARLY:
            pair_loads[u + 2] = here(pairs.at[u + 2], pair.at[u % 2])

    def spread(total, slot, source, columns):
        value = pair[slot, mine, columns]

        def chunk(j, carry):
            rows = span(j * 512, 512)
            total[:, rows] += dot(value, weights[source, rows, columns], ((1,), (1,)))
            return carry

        lax.fori_loop(0, 4, chunk, 0)

    def units():
        for copy in unit_loads + share_loads:
            copy.wait()

        def some(j, carry):
            low, high = span(j * 256, 256), span(512 + j * 256, 256)
            unit = span(EARLY * 512 + j * 256, 256)
            v = dot(inputs[...], weights[0, :, low], ((1,), (0,))) + b_up[:, unit]
            d = dot(upstream[...], weights[0, :, high], ((1,), (0,)))
            d_up, active = gelu_both(v, d)
            pair[4, mine, low] = d_up
            pair[4, mine, high] = active
            return carry

        lax.fori_loop(0, 2, some, 0)
        rows = pair.at[4, mine]
        net.push(("p", 4), rows, rows, "s", 1)
        spread(d_share, 4, 0, LOW)
        spread(share, 4, 0, HIGH)
        weight_loads.append(here(heads_w0, weights.at[0]))

    def normed(rows):
        value = hidden[rows].astype(F32)
        value = value - jnp.mean(value, axis=1, keepdims=True)
        inverse = lax.rsqrt(jnp.mean(value * value, axis=1, keepdims=True) + 1e-05)
        return value * inverse, inverse

    def vectors():
        vec_acc[...] = jnp.zeros_like(vec_acc)
        vecs[...] = jnp.zeros_like(vecs)

        def chunk(t, carry):
            rows = span(t * 16, 16, 16)
            standard, _ = normed(rows)
            value = d_share[rows]
            for k, item in enumerate((value * standard, value, upstream[rows].astype(F32))):
                vec_acc[k] += item[:8] + item[8:]
            return carry

        lax.fori_loop(0, 24, chunk, 0)
        for k in range(3):
            vecs[k : k + 1] = jnp.sum(vec_acc[k], axis=0, keepdims=True)
        vecs[3:4, 0 : EARLY * 512] = bias_up[:, 0 : EARLY * 512]
        vecs[3:4, EARLY * 512 : 2048] = jnp.sum(pair[4, mine, LOW].astype(F32), axis=0, keepdims=True)
        for k in range(4):
            columns = pl.ds(k * 256, 256)
            vecs[4:5, columns] = jnp.sum(pair[2, mine, columns].astype(F32), axis=0, keepdims=True)
        vecs[4:5, 1024:1536] = jnp.sum(pair[3, mine, LOW].astype(F32), axis=0, keepdims=True)

    def finish_in():
        def chunk(t, carry):
            rows = span(t * 16, 16, 16)
            base = t // 6 * 192 + lax.rem(t, 6) * 16
            standard, inverse = normed(rows)
            got = [weights[1, span(base + 96 * k, 16, 16)].astype(F32) for k in (0, 1)]
            scaled = jnp.concatenate(got, axis=1) * gain[...]
            mean = jnp.mean(scaled, axis=1, keepdims=True)
            along = jnp.mean(scaled * standard, axis=1, keepdims=True)
            d_share[rows] = upstream[rows].astype(F32) + inverse * (scaled - mean - standard * along)
            return carry

        lax.fori_loop(0, 24, chunk, 0)

    ys = [
        Sum(net, "yi", weights.at[0, pl.ds(0, 768)], y_far.at[0], y_near.at[0], sum0),
        Sum(net, "yo", weights.at[0, pl.ds(768, 768)], y_far.at[1], y_near.at[1], sum1),
    ]
    for copy in factor_loads:
        copy.wait()
    tile(0)
    heads()
    tile(1)
    parts[0].step3()
    units()
    parts[1].step3()
    weight_loads[0].wait()
    spread(d_share, 3, 1, LOW)
    parts[0].step4()
    weight_loads[1].wait()
    spread(d_share, 2, 0, ALL)
    ys[0].step1(d_share)
    parts[1].step4()
    spread(share, 3, 1, HIGH)
    ys[1].step1(share)
    tile(2)
    parts[0].step5()
    ys[0].step2()
    net.arrived(("p", 4))
    gradients(3, 4, 0, 1)
    parts[2].step3()
    parts[1].step5()
    ys[1].step2()
    row_loads[0].wait()
    vectors()
    vec = vector_sum(net, vecs, cores, alongx, alongz, alongy, vec_out)
    next(vec)
    parts[3].step3()
    parts[0].step6()
    parts[2].step4()
    ys[0].step3(loc.at[next(sems)])
    for slot in (2, 3):
        net.arrived(("p", slot))
    gradients(4, 2, 0, 0)
    next(vec)
    parts[3].step4()
    parts[1].step6()
    parts[2].step5()
    ys[1].step3(loc.at[next(sems)])
    gradients(5, 3, 0, 1)
    next(vec)
    parts[4].step3()
    parts[3].step5()
    ys[0].step4()
    parts[5].step3()
    next(vec)
    parts[4].step4()
    parts[2].step6()
    ys[1].step4()
    parts[5].step4()
    parts[3].step6()
    next(vec)
    parts[4].step5()
    ys[0].step5()
    got0 = here(sum0, weights.at[1, pl.ds(0, 768)].reshape(4, 192, 1024))
    parts[5].step5()
    got0.wait()
    finish_in()
    out0 = here(d_share, input_grad)
    parts[4].step6()
    ys[1].step5()
    parts[5].step6()
    out0.wait()
    net.drain()


def backward(args, cid):
    wide = jax.ShapeDtypeStruct((384, 2048), F32)
    return pl.pallas_call(
        back_kernel,
        out_shape=[wide]
        + [jax.ShapeDtypeStruct((4, 192, 1024), BF)] * 2
        + [jax.ShapeDtypeStruct((PARTS, 64, 1024), F32), jax.ShapeDtypeStruct((8, 2048), F32)],
        in_specs=[ANY] * 13 + [VMEM] * 7,
        out_specs=[ANY] * 3 + [VMEM] * 2,
        scratch_shapes=[pltpu.VMEM((4, 4, 64, 1024), BF)] * PARTS
        + [
            pltpu.VMEM((PARTS, 2, 2, 4, 16, 1024), BF),
            pltpu.VMEM((PARTS, 2, 2, 4, 32, 1024), BF),
            pltpu.VMEM((PARTS, 2, 2, 16, 1024), BF),
            pltpu.VMEM((PARTS, 2, 2, 32, 1024), BF),
            pltpu.VMEM((2, 2048, 1024), BF),
            pltpu.VMEM((5, 768, 1024), BF),
            pltpu.VMEM((2, 1024, 768), BF),
            pltpu.VMEM((384, 2048), F32),
            pltpu.VMEM((384, 2048), F32),
            pltpu.VMEM((3, 128, 1024), BF),
            pltpu.VMEM((3, 128, 1024), BF),
            pltpu.VMEM((384, 2048), BF),
            pltpu.VMEM((384, 2048), BF),
            pltpu.VMEM((384, 2048), BF),
            pltpu.VMEM((2, 2, 96, 1024), BF),
            pltpu.VMEM((2, 2, 192, 1024), BF),
            pltpu.VMEM((8, 2048), F32),
            pltpu.VMEM((3, 8, 2048), F32),
            pltpu.VMEM((2, 8, 2048), F32),
            pltpu.VMEM((4, 8, 2048), F32),
            pltpu.VMEM((4, 8, 2048), F32),
            pltpu.VMEM((4, 8, 2048), F32),
            pltpu.VMEM((128, 128), F32),
            pltpu.VMEM((128, 128), F32),
            pltpu.VMEM((128, 128), F32),
            pltpu.SemaphoreType.DMA((140,)),
            pltpu.SemaphoreType.DMA((140,)),
            pltpu.SemaphoreType.DMA((40,)),
        ],
        compiler_params=pltpu.CompilerParams(
            collective_id=cid, has_side_effects=True, vmem_limit_bytes=63 * 2**20
        ),
        name="backward",
    )(*args)


def finish_kernel(
    hidden, summed, b_dense, b_down, grad, done, vecs, block_out, input_grad, g_qkv, g_dense, g_up, g_down, v_gain,
    v_shift, v_out, v_up, v_qkv, v_out2,
):
    for half in (0, 1):
        columns = pl.ds(half * 1024, 1024)
        bias = b_dense[:, columns] + b_down[:, columns]
        for d in (0, 1):
            rows = pl.ds(96 * d, 96)
            got = summed[d, pl.ds(96 * half, 96)].astype(F32)
            block_out[rows, columns] = hidden[rows, columns].astype(F32) + got + bias
    input_grad[...] = grad[...]

    @pl.when(pl.program_id(0) == 0)
    def _():
        left = lax.broadcasted_iota(jnp.int32, (64, 128), 1) < 64
        for u in range(TILES):
            g_up[:, pl.ds(u * 512, 512)] = done[u, :, :512]
            g_down[:, pl.ds(u * 512, 512)] = done[u, :, 512:]
        g_qkv[0] = done[5, :, :512]
        g_dense[...] = done[5, :, 512:]
        v_qkv[0:1] = vecs[4:5, 1024:1536]
        for k in range(4):
            a, b = pl.ds(256 * k, 128), pl.ds(256 * k + 128, 128)
            pieces = halves(done[4, :, a], done[4, :, b], left)
            rows = halves(vecs[4:5, a], vecs[4:5, b], left[:1])
            for j in (0, 1):
                g_qkv[1 + j, :, pl.ds(k * 128, 128)] = pieces[j]
                v_qkv[1 + j : 2 + j, pl.ds(k * 128, 128)] = rows[j]
        for k, dst in ((0, v_gain), (1, v_shift), (2, v_out), (2, v_out2), (3, v_up)):
            dst[...] = vecs[k]


def finish(hidden, summed, b_dense, b_down, grad, done, vecs):
    wide, row = jax.ShapeDtypeStruct((384, 2048), F32), jax.ShapeDtypeStruct((2048,), F32)
    rows = pl.BlockSpec((192, 2048), lambda i: (i, 0))
    small = [
        jax.ShapeDtypeStruct((3, 64, 512), F32),
        jax.ShapeDtypeStruct((64, 512), F32),
        jax.ShapeDtypeStruct((64, 2048), F32),
        jax.ShapeDtypeStruct((64, 2048), F32),
        row,
        row,
        row,
        row,
        jax.ShapeDtypeStruct((3, 512), F32),
        row,
    ]

    def whole(shape):
        return pl.BlockSpec(shape, lambda i: (0,) * len(shape))

    return pl.pallas_call(
        finish_kernel,
        grid=(2,),
        out_shape=[wide, wide] + small,
        in_specs=[rows, pl.BlockSpec((2, 192, 1024), lambda i: (i, 0, 0)), whole((1, 2048)), whole((1, 2048)), rows]
        + [whole((PARTS, 64, 1024)), whole((8, 2048))],
        out_specs=[rows, rows] + [whole(s.shape) for s in small],
        compiler_params=pltpu.CompilerParams(vmem_limit_bytes=62 * 2**20),
        name="finish",
    )(hidden, summed, b_dense, b_down, grad, done, vecs)


def local(
    hidden_in, segments, keep_mask, ln_gain, ln_shift, w_qkv, b_qkv, w_dense, b_dense, w_up, b_up, w_down, b_down,
    cotangent,
):
    rows, width = 384, 2048
    lanes_of = np.arange(128) % HD
    frequency = np.float32(10000.0) ** (-(np.arange(ROT // 2, dtype=np.float32) * 2.0) / ROT)
    frequency = np.where(lanes_of < ROT, np.resize(frequency.astype(np.float64), 128), 0.0)
    near, base = np.arange(128)[:, None] * frequency, 128 * np.arange(16)[:, None] * frequency
    tables = [jnp.asarray(t.astype(np.float32)) for t in (np.cos(near), np.sin(near), np.cos(base), np.sin(base))]
    hidden = hidden_in.reshape(rows, width)
    upstream = cotangent.reshape(rows, width)
    outs = forward(
        [hidden, upstream, w_up, w_down.T, ln_gain[None], ln_shift[None], w_qkv.transpose(1, 0, 2), b_qkv, w_dense.T]
        + [b_up[None], segments, keep_mask, *tables],
        0,
    )
    heads_w = [outs[u].reshape(2048, 1024) for u in (0, 1, PARTS - 1)]
    in_t, up_t, pairs, od_in, dkv_in, inputs, share, d_share, bias_up = outs[PARTS:]
    input_grad, _, summed, done, vectors = backward(
        [od_in, dkv_in, upstream, hidden, in_t, up_t, pairs, *heads_w, inputs, share, d_share, bias_up]
        + [b_up[None], ln_gain[None], *tables],
        1,
    )
    block_out, input_grad, grad_qkv, grad_dense, grad_up, grad_down, gain, shift, out, up, grad_bqkv, out2 = finish(
        hidden, summed, b_dense[None], b_down[None], input_grad, done, vectors
    )
    return (
        block_out.reshape(3, 128, width),
        input_grad.reshape(3, 128, width),
        gain,
        shift,
        grad_qkv.transpose(1, 0, 2),
        grad_bqkv,
        grad_dense.T,
        out,
        grad_up,
        up,
        grad_down.T,
        out2,
    )


def solution(mesh):
    return jax.shard_map(
        local,
        mesh=mesh,
        in_specs=(
            P("dp", "seq", None),
            P("dp", "seq"),
            P("dp", "seq"),
            P(),
            P(),
            P(("dp", "seq"), None, "tp"),
            P(None, "tp"),
            P("tp", ("dp", "seq")),
            P(),
            P(("dp", "seq"), "tp"),
            P("tp"),
            P("tp", ("dp", "seq")),
            P(),
            P("dp", "seq", None),
        ),
        out_specs=(
            P("dp", "seq", None),
            P("dp", "seq", None),
            P(),
            P(),
            P(("dp", "seq"), None, "tp"),
            P(None, "tp"),
            P("tp", ("dp", "seq")),
            P(),
            P(("dp", "seq"), "tp"),
            P("tp"),
            P("tp", ("dp", "seq")),
            P(),
        ),
        check_vma=False,
    )
```
